32 devices in a mesh: dp: 8 (over z, x), tensor: 4 (over y, core).
Axes of the slice: x: 2, y: 2, z: 4, core: 2. Of those that a mesh axis runs over, the one named last changes fastest.
Arguments:
- tokens: bfloat16 [16384, 768], P(('dp', 'tensor')), may hold values from -6 to 6
- cotangent: bfloat16 [16384, 768], P(('dp', 'tensor')), may hold values from -6 to 6
- first_gain: float32 [768], P('dp'), may hold values from 0.25 to 1.75
- first_shift: float32 [768], P('dp'), may hold values from -1.5 to 1.5
- w_qkv: bfloat16 [3, 768, 768], P(None, 'dp', 'tensor'), may hold values from -0.21875 to 0.21875
- qkv_bias: float32 [3, 768], P(None, 'dp'), may hold values from -2.5 to 2.5
- w_out: bfloat16 [768, 768], P('tensor', 'dp'), may hold values from -1.75 to 1.75
- out_bias: float32 [768], P('dp'), may hold values from -5 to 5
- second_gain: float32 [768], P('dp'), may hold values from 0.25 to 1.75
- second_shift: float32 [768], P('dp'), may hold values from -1.5 to 1.5
- w_up: bfloat16 [768, 3072], P('dp', 'tensor'), may hold values from -0.21875 to 0.21875
- up_bias: float32 [3072], P('dp'), may hold values from -2.5 to 2.5
- w_down: bfloat16 [3072, 768], P('tensor', 'dp'), may hold values from -0.4375 to 0.4375
- down_bias: float32 [768], P('dp'), may hold values from -5 to 5
Outputs:
- block_out: bfloat16 [16384, 768], P(('dp', 'tensor'))
- tokens_grad: bfloat16 [16384, 768], P(('dp', 'tensor'))
- first_gain_grad: float32 [768], P('dp')
- first_shift_grad: float32 [768], P('dp')
- w_qkv_grad: float32 [3, 768, 768], P(None, 'dp', 'tensor')
- qkv_bias_grad: float32 [3, 768], P(None, 'dp')
- w_out_grad: float32 [768, 768], P('tensor', 'dp')
- out_bias_grad: float32 [768], P('dp')
- second_gain_grad: float32 [768], P('dp')
- second_shift_grad: float32 [768], P('dp')
- w_up_grad: float32 [768, 3072], P('dp', 'tensor')
- up_bias_grad: float32 [3072], P('dp')
- w_down_grad: float32 [3072, 768], P('tensor', 'dp')
- down_bias_grad: float32 [768], P('dp')
The draws below stay inside these ranges and needn't reach their ends.
All inputs are finite; a program needn't handle non-finite values.
Results may differ from the reference program's by a relative error of at most 0.039.
Values may be sent and summed in bfloat16 or wider, within the bound.
No kernel may reach another device: no remote copies, remote signals or barrier semaphores. Data moves between devices by JAX's collectives and lax.ppermute only.
A program may use at most 128 MiB of HBM per device.

```python
import jax
import jax.numpy as jnp
from jax import lax

D = 768
HEADS = 12
HEAD_DIM = 64
FF = 3072
LENGTH = 1024
TOKENS = 16384


def level_of(key, shape, shards, smallest, largest):
    level, own = 1.0, jax.random.fold_in(key, 6)
    for position, shards_of in shards:
        draws = jnp.exp(jax.random.uniform(jax.random.fold_in(own, position), (shards_of,), jnp.float32, smallest / len(shards), largest / len(shards)))
        level = level * jnp.repeat(draws, shape[position] // shards_of).reshape([-1 if axis == position else 1 for axis in range(len(shape))])
    return level


def noise(key, dims, deviation, limit, shards=(), kind=jnp.bfloat16):
    level = level_of(key, dims, shards, -0.22, 0.18) if shards else 1.0
    array = jax.random.normal(key, dims, jnp.float32) * deviation * level
    return jnp.minimum(jnp.maximum(array, -limit), limit).astype(kind)


def setup_inputs(seed: int = 0) -> dict:
    keys = jax.random.split(jax.random.key(seed), 15)
    return {
        "tokens": noise(keys[0], (TOKENS, D), 1.0, 6.0, ((0, 32),)),
        "cotangent": noise(keys[1], (TOKENS, D), 1.0, 6.0, ((0, 32),)),
        "first_gain": jnp.clip(1.0 + 0.15 * jax.random.normal(keys[2], (D,), jnp.float32), 0.25, 1.75),
        "first_shift": noise(keys[3], (D,), 0.3, 1.5, ((0, 8),), jnp.float32),
        "w_qkv": noise(keys[4], (3, D, D), D ** -0.5, 0.21875, ((1, 8), (2, 4))),
        "qkv_bias": noise(keys[5], (3, D), 0.5, 2.5, ((1, 8),), jnp.float32),
        "w_out": noise(keys[6], (D, D), (D // 64) ** -0.5, 1.75, ((0, 4), (1, 8))),
        "out_bias": noise(keys[7], (D,), 1.0, 5.0, ((0, 8),), jnp.float32),
        "second_gain": jnp.clip(1.0 + 0.15 * jax.random.normal(keys[8], (D,), jnp.float32), 0.25, 1.75),
        "second_shift": noise(keys[9], (D,), 0.3, 1.5, ((0, 8),), jnp.float32),
        "w_up": noise(keys[10], (D, FF), D ** -0.5, 0.21875, ((0, 8), (1, 4))),
        "up_bias": noise(keys[11], (FF,), 0.5, 2.5, ((0, 8),), jnp.float32),
        "w_down": noise(keys[12], (FF, D), (FF // 16) ** -0.5, 0.4375, ((0, 4), (1, 8))),
        "down_bias": noise(keys[13], (D,), 1.0, 5.0, ((0, 8),), jnp.float32),
    }


EPS = 1e-05

@jax.custom_vjp
def low(v):
    return lax.optimization_barrier(v.astype(jnp.bfloat16)).astype(jnp.float32)

@jax.custom_vjp
def low_back(v):
    return v

def low_keep(v):
    return (low(v), None)

def low_pass(kept, grad):
    return (grad,)

def back_keep(v):
    return (v, None)

def back_low(kept, grad):
    return (low(grad),)
low.defvjp(low_keep, low_pass)
low_back.defvjp(back_keep, back_low)

def layer_norm(values, gain, shift):
    center = values - lax.optimization_barrier(jnp.mean(values, -1, keepdims=True))
    spread = lax.optimization_barrier(jnp.mean(center * center, -1, keepdims=True))
    return center * lax.rsqrt(spread + EPS) * gain + shift

def block_forward(params, sequence):
    first_gain, first_shift, w_qkv, qkv_bias, w_out, out_bias, second_gain, second_shift, w_up, up_bias, w_down, down_bias = params
    highest = lax.Precision.HIGHEST
    normed_one = low(layer_norm(sequence, first_gain, first_shift))
    projected = jnp.einsum('rd,cde->cre', normed_one, w_qkv, precision=highest) + qkv_bias[:, None, :]
    projected = low(low_back(projected))
    shaped = projected.reshape(3, LENGTH, HEADS, HEAD_DIM)
    scores = jnp.einsum('qhd,khd->hqk', shaped[0], shaped[1], precision=highest) * HEAD_DIM ** (-0.5)
    scores = low_back(scores)
    causal = jnp.arange(LENGTH)[:, None] >= jnp.arange(LENGTH)[None, :]
    probs = low(jax.nn.softmax(jnp.where(causal, scores, -jnp.inf), axis=-1))
    context = jnp.einsum('hqk,khd->qhd', probs, shaped[2], precision=highest).reshape(LENGTH, HEADS * HEAD_DIM)
    context = low(low_back(context))
    attended = low_back(jnp.dot(context, w_out, precision=highest) + out_bias)
    hidden = sequence + attended
    normed_two = low(layer_norm(hidden, second_gain, second_shift))
    upward = low_back(jnp.dot(normed_two, w_up, precision=highest) + up_bias)
    active = low(jax.nn.gelu(upward, approximate=True))
    mlp_out = low_back(jnp.dot(active, w_down, precision=highest) + down_bias)
    return hidden + mlp_out

def reference(tokens, cotangent, first_gain, first_shift, w_qkv, qkv_bias, w_out, out_bias, second_gain, second_shift, w_up, up_bias, w_down, down_bias):
    params = tuple((item.astype(jnp.float32) for item in (first_gain, first_shift, w_qkv, qkv_bias, w_out, out_bias, second_gain, second_shift, w_up, up_bias, w_down, down_bias)))
    sequences = tokens.astype(jnp.float32).reshape(-1, LENGTH, D)
    seq_cots = cotangent.astype(jnp.float32).reshape(-1, LENGTH, D)

    def one_step(totals, item):
        sequence, seq_cot = item
        output, backward = jax.vjp(block_forward, params, sequence)
        param_grads, input_grad = backward(seq_cot)
        totals = jax.tree.map(lambda left, right: left + right, totals, param_grads)
        return (totals, (output.astype(jnp.bfloat16), input_grad.astype(jnp.bfloat16)))
    start = jax.tree.map(jnp.zeros_like, params)
    totals, (outputs, input_grads) = lax.scan(one_step, start, (sequences, seq_cots))
    return (outputs.reshape(-1, D), input_grads.reshape(-1, D), totals[0], totals[1], totals[2], totals[3], totals[4], totals[5], totals[6], totals[7], totals[8], totals[9], totals[10], totals[11])
```

```python
import functools

import jax
import jax.numpy as jnp
from jax import lax
from jax.experimental import pallas as pl
from jax.experimental.pallas import tpu as pltpu
from jax.sharding import Mesh
from jax.sharding import PartitionSpec as P

HEAD_DIM = 64
LENGTH = 1024
EPS = 1e-05
BLOCK = 256
BF = jnp.bfloat16
F32 = jnp.float32
VMEM_LIMIT = 48 * 1024 * 1024


def swap(value, axis, bit):
    size = lax.axis_size(axis)
    return lax.ppermute(value, axis, [(i, i ^ bit) for i in range(size)])


def nt_dot(left, right):
    return lax.dot_general(left, right, (((1,), (1,)), ((), ())), preferred_element_type=F32)


def tn_dot(left, right):
    return lax.dot_general(left, right, (((0,), (0,)), ((), ())), preferred_element_type=F32)


def nn_dot(left, right):
    return jnp.dot(left, right, preferred_element_type=F32)


def attend_kernel(p_ref, c_ref):
    width = c_ref.shape[1]
    pair = pl.multiple_of(pl.program_id(0) * 128, 128)
    q = p_ref[:, pl.ds(pair, 128)] * BF(HEAD_DIM**-0.5)
    k = p_ref[:, pl.ds(width + pair, 128)]
    v = p_ref[:, pl.ds(2 * width + pair, 128)]
    lane = lax.broadcasted_iota(jnp.int32, (LENGTH, 128), 1)
    low_lane = lax.broadcasted_iota(jnp.int32, (BLOCK, 128), 1) < HEAD_DIM
    causal = lax.broadcasted_iota(jnp.int32, (BLOCK, BLOCK), 0) >= lax.broadcasted_iota(
        jnp.int32, (BLOCK, BLOCK), 1
    )
    for start in range(0, LENGTH, BLOCK):
        stop = start + BLOCK
        halves = []
        for head in range(2):
            mine = (lane < HEAD_DIM) if head == 0 else (lane >= HEAD_DIM)
            q_part = jnp.where(mine[start:stop], q[start:stop], BF(0))
            v_part = jnp.where(mine[:stop], v[:stop], BF(1))
            scores = nt_dot(q_part, k[:stop])
            last = jnp.where(causal, scores[:, start:], -1e30)
            scores = jnp.concatenate([scores[:, :start], last], 1) if start else last
            top = jnp.max(scores, 1, keepdims=True)
            weights = jnp.exp(scores - top).astype(BF)
            result = nn_dot(weights, v_part)
            halves.append(result / pltpu.roll(result, HEAD_DIM, 1))
        c_ref[start:stop, pl.ds(pair, 128)] = jnp.where(low_lane, halves[0], halves[1]).astype(BF)


def attend(projected):
    width = projected.shape[1] // 3
    pairs = width // 128
    return pl.pallas_call(
        attend_kernel,
        out_shape=jax.ShapeDtypeStruct((LENGTH, width), BF),
        grid=(pairs,),
        in_specs=[pl.BlockSpec((LENGTH, 3 * width), lambda i: (0, 0))],
        out_specs=pl.BlockSpec((LENGTH, width), lambda i: (0, 0)),
        compiler_params=pltpu.CompilerParams(vmem_limit_bytes=VMEM_LIMIT),
        cost_estimate=pl.CostEstimate(
            flops=pairs * 4 * LENGTH * LENGTH * 128,
            bytes_accessed=LENGTH * width * 8,
            transcendentals=pairs * LENGTH * LENGTH,
        ),
        name="attend",
    )(projected)


def attend_back_kernel(p_ref, g_ref, d_ref, bias_ref, dk_ref, dv_ref, dq_ref):
    width = g_ref.shape[1]
    pair = pl.multiple_of(pl.program_id(0) * 128, 128)
    q = p_ref[:, pl.ds(pair, 128)] * BF(HEAD_DIM**-0.5)
    k = p_ref[:, pl.ds(width + pair, 128)]
    v = p_ref[:, pl.ds(2 * width + pair, 128)]
    g = g_ref[:, pl.ds(pair, 128)]
    lane = lax.broadcasted_iota(jnp.int32, (LENGTH, 128), 1)
    low_lane = lax.broadcasted_iota(jnp.int32, (BLOCK, 128), 1) < HEAD_DIM
    causal = lax.broadcasted_iota(jnp.int32, (BLOCK, BLOCK), 0) <= lax.broadcasted_iota(
        jnp.int32, (BLOCK, BLOCK), 1
    )
    dk_ref[...] = jnp.zeros_like(dk_ref)
    dv_ref[...] = jnp.zeros_like(dv_ref)
    for start in range(0, LENGTH, BLOCK):
        stop = start + BLOCK
        query_grads = []
        for head in range(2):
            mine = (lane < HEAD_DIM) if head == 0 else (lane >= HEAD_DIM)
            q_part = jnp.where(mine[start:stop], q[start:stop], BF(0))
            g_part = jnp.where(mine[start:stop], g[start:stop], BF(0))
            scores = nt_dot(k[:stop], q_part)
            last = jnp.where(causal, scores[start:], -1e30)
            scores = jnp.concatenate([scores[:start], last], 0) if start else last
            top = jnp.max(scores, 0, keepdims=True)
            weights = jnp.exp(scores - top)
            probs = weights * (1.0 / jnp.sum(weights, 0, keepdims=True))
            prob_grad = nt_dot(v[:stop], g_part)
            delta = jnp.sum(probs * prob_grad, 0, keepdims=True)
            score_grad = (probs * (prob_grad - delta)).astype(BF)
            dv_ref[:stop] += nn_dot(probs.astype(BF), g_part)
            dk_ref[:stop] += nn_dot(score_grad, q_part)
            query_grads.append(tn_dot(score_grad, k[:stop]))
        dq_ref[start:stop] = jnp.where(low_lane, query_grads[0], query_grads[1]) * HEAD_DIM**-0.5
    for position, ref in enumerate((dq_ref, dk_ref, dv_ref)):
        result = ref[...].astype(BF)
        columns = pl.ds(position * width + pair, 128)
        d_ref[:, columns] = result
        bias_ref[:, columns] = jnp.sum(
            result.astype(F32).reshape(LENGTH // 8, 8, 128), 0
        )


def attend_back(projected, ctx_grad):
    width = projected.shape[1] // 3
    pairs = width // 128
    return pl.pallas_call(
        attend_back_kernel,
        out_shape=(
            jax.ShapeDtypeStruct((LENGTH, 3 * width), BF),
            jax.ShapeDtypeStruct((8, 3 * width), F32),
        ),
        grid=(pairs,),
        in_specs=[
            pl.BlockSpec((LENGTH, 3 * width), lambda i: (0, 0)),
            pl.BlockSpec((LENGTH, width), lambda i: (0, 0)),
        ],
        out_specs=(
            pl.BlockSpec((LENGTH, 3 * width), lambda i: (0, 0)),
            pl.BlockSpec((8, 3 * width), lambda i: (0, 0)),
        ),
        scratch_shapes=[pltpu.VMEM((LENGTH, 128), F32)] * 3,
        compiler_params=pltpu.CompilerParams(vmem_limit_bytes=VMEM_LIMIT),
        cost_estimate=pl.CostEstimate(
            flops=pairs * 10 * LENGTH * LENGTH * 128,
            bytes_accessed=LENGTH * width * 14,
            transcendentals=pairs * LENGTH * LENGTH,
        ),
        name="attend_back",
    )(projected, ctx_grad)


def place_kernel(dp_ref, h1_ref, h2_ref, h1y_ref, h2x_ref, w_ref, sems):
    dp = dp_ref[0]
    copies = []

    def put(source, row, block):
        copies.append(
            pltpu.make_async_copy(source, w_ref.at[row, dp ^ block], sems.at[len(copies)])
        )

    for low in range(2):
        for x in range(2):
            put(h1_ref.at[x * 2 + low], 0, low * 2 + x)
            put(h1y_ref.at[x * 2 + low], 1, low * 2 + x)
        for y in range(2):
            put(h2_ref.at[y * 2 + low], y, 4 + low * 2)
            put(h2x_ref.at[y * 2 + low], y, 4 + low * 2 + 1)
    for copy in copies:
        copy.start()
    for copy in copies:
        copy.wait()


def gather_weight(shard, dp):
    rows, columns = shard.shape
    count = lax.axis_size("dp")
    if count != 8 or rows % 16:
        own = lax.all_gather(shard, "dp", axis=0, tiled=True)
        return jnp.stack([own, swap(own, "y", 1)])
    r1, r2, r3 = swap(shard, "dp", 2), swap(shard, "dp", 4), swap(shard, "dp", 6)
    h1 = jnp.stack([shard, r1])
    h2 = jnp.stack([r2, r3])
    h1 = jnp.concatenate([h1, swap(h1, "dp", 1)])
    h2 = jnp.concatenate([h2, swap(h2, "y", 1)])
    h1y = swap(h1, "y", 1)
    h2x = swap(h2, "dp", 1)
    placed = pl.pallas_call(
        place_kernel,
        out_shape=jax.ShapeDtypeStruct((2, 8, rows, columns), BF),
        in_specs=[pl.BlockSpec(memory_space=pltpu.SMEM)] + [pl.BlockSpec(memory_space=pl.ANY)] * 4,
        out_specs=pl.BlockSpec(memory_space=pl.ANY),
        scratch_shapes=[pltpu.SemaphoreType.DMA((16,))],
        cost_estimate=pl.CostEstimate(
            flops=0, bytes_accessed=64 * rows * columns, transcendentals=0
        ),
        name="place",
    )(dp, h1, h2, h1y, h2x)
    return placed.reshape(2, 8 * rows, columns)


def spread_kernel(dp_ref, g_ref, k1_ref, s1_ref, k2_ref, s2_ref, sems):
    dp = dp_ref[0]
    copies = []

    def put(row, block, target):
        copies.append(
            pltpu.make_async_copy(g_ref.at[row, dp ^ block], target, sems.at[len(copies)])
        )

    for low in range(2):
        for x in range(2):
            put(0, low * 2 + x, k1_ref.at[x * 2 + low])
            put(1, low * 2 + x, s1_ref.at[x * 2 + low])
        for y in range(2):
            put(y, 4 + low * 2, k2_ref.at[y * 2 + low])
            put(y, 4 + low * 2 + 1, s2_ref.at[y * 2 + low])
    for copy in copies:
        copy.start()
    for copy in copies:
        copy.wait()


def add_low(left, right):
    return (left.astype(F32) + right.astype(F32)).astype(BF)


def scatter_grad(grad, dp):
    count = lax.axis_size("dp")
    columns = grad.shape[2]
    rows = grad.shape[1] // count
    if count != 8 or rows % 16:
        both = grad[0].astype(F32) + swap(grad[1], "y", 1).astype(F32)
        return lax.psum_scatter(both, "dp", scatter_dimension=0, tiled=True)
    part = jax.ShapeDtypeStruct((4, rows, columns), BF)
    k1, s1, k2, s2 = pl.pallas_call(
        spread_kernel,
        out_shape=(part,) * 4,
        in_specs=[pl.BlockSpec(memory_space=pltpu.SMEM), pl.BlockSpec(memory_space=pl.ANY)],
        out_specs=(pl.BlockSpec(memory_space=pl.ANY),) * 4,
        scratch_shapes=[pltpu.SemaphoreType.DMA((16,))],
        cost_estimate=pl.CostEstimate(
            flops=0, bytes_accessed=64 * rows * columns, transcendentals=0
        ),
        name="spread",
    )(dp, grad.reshape(2, 8, rows, columns))
    t1 = swap(s1, "y", 1)
    t2 = swap(s2, "dp", 1)
    u1 = swap(add_low(k1[2:], t1[2:]), "dp", 1)
    u2 = swap(add_low(k2[2:], t2[2:]), "y", 1)
    v1 = k1[:2].astype(F32) + t1[:2].astype(F32) + u1.astype(F32)
    v2 = k2[:2].astype(F32) + t2[:2].astype(F32) + u2.astype(F32)
    r1 = swap(v1[1].astype(BF), "dp", 2)
    r2 = swap(v2[0].astype(BF), "dp", 4)
    r3 = swap(v2[1].astype(BF), "dp", 6)
    return v1[0] + r1.astype(F32) + r2.astype(F32) + r3.astype(F32)


def norm_parts(values):
    center = values - jnp.mean(values, -1, keepdims=True)
    spread = jnp.mean(center * center, -1, keepdims=True)
    scale = lax.rsqrt(spread + EPS)
    return center * scale, scale


def norm_back(xhat, scale, gain, grad):
    scaled = grad * gain
    first = jnp.mean(scaled, -1, keepdims=True)
    second = jnp.mean(scaled * xhat, -1, keepdims=True)
    return scale * (scaled - first - xhat * second)


def body(
    tokens,
    cotangent,
    first_gain,
    first_shift,
    w_qkv,
    qkv_bias,
    w_out,
    out_bias,
    second_gain,
    second_shift,
    w_up,
    up_bias,
    w_down,
    down_bias,
):
    dp_count = lax.axis_size("dp")
    dp = lax.axis_index("dp")
    y = lax.axis_index("y")
    core = lax.axis_index("core")
    dp_ref = dp.reshape(1).astype(jnp.int32)
    own_rows, width = tokens.shape
    piece = first_gain.shape[0]
    heads_own = w_qkv.shape[2]
    ff_own = w_up.shape[1]
    ff_piece = up_bias.shape[0]

    vectors = jnp.concatenate(
        [
            first_gain,
            first_shift,
            qkv_bias.reshape(-1),
            out_bias,
            second_gain,
            second_shift,
            up_bias,
            down_bias,
        ]
    )
    vectors = lax.all_to_all(
        jnp.broadcast_to(vectors[None], (dp_count, vectors.shape[0])), "dp", 0, 0, tiled=True
    )

    def full(position, count=1):
        return vectors[:, position * piece : (position + count) * piece]

    gain_one = full(0).reshape(-1)
    shift_one = full(1).reshape(-1)
    qkv_full = full(2, 3).reshape(dp_count, 3, piece).transpose(1, 0, 2).reshape(3, width)
    out_full = full(5).reshape(-1)
    gain_two = full(6).reshape(-1)
    shift_two = full(7).reshape(-1)
    up_full = vectors[:, 8 * piece : 8 * piece + ff_piece].reshape(-1)
    down_full = vectors[:, 8 * piece + ff_piece :].reshape(-1)

    def own_blocks(values):
        lead = values.shape[:-1]
        block = values.shape[-1] // 4
        cut = values.reshape(lead + (2, 2, block))
        cut = jnp.where(core == 0, cut[..., 0, :], cut[..., 1, :])
        cut = jnp.where(y == 0, cut, cut[..., ::-1, :])
        return cut.reshape(lead + (2 * block,))

    qkv_own = own_blocks(qkv_full).reshape(-1)
    up_own = own_blocks(up_full)

    shard_one = jnp.concatenate([w_qkv[0], w_qkv[1], w_qkv[2], w_out.T], 1)
    weight_one = gather_weight(shard_one, dp_ref)
    weight_up = gather_weight(w_up, dp_ref)
    weight_down = gather_weight(w_down.T, dp_ref)

    def in_order(own, other):
        return jnp.where(
            core == 0, jnp.concatenate([own, other], 0), jnp.concatenate([other, own], 0)
        )

    def own_half(rows):
        return lax.dynamic_slice_in_dim(rows, core * own_rows, own_rows, 0)

    def other_half(rows):
        return lax.dynamic_slice_in_dim(rows, (1 - core) * own_rows, own_rows, 0)

    inputs = in_order(tokens, swap(tokens, "core", 1)).astype(F32)
    cot = in_order(cotangent, swap(cotangent, "core", 1))

    xhat_one, scale_one = norm_parts(inputs)
    normed_one = (xhat_one * gain_one + shift_one).astype(BF)

    w_proj = (
        weight_one[:, :, : 3 * heads_own]
        .reshape(2, width, 3, heads_own)
        .transpose(1, 2, 0, 3)
        .reshape(width, 6 * heads_own)
    )
    w_ctx = weight_one[:, :, 3 * heads_own :].transpose(1, 0, 2).reshape(width, 2 * heads_own)
    projected = (nn_dot(normed_one, w_proj) + qkv_own).astype(BF)
    context = attend(projected)
    out_part = nt_dot(context, w_ctx).astype(BF)
    out_other = swap(out_part, "core", 1)
    hidden = inputs + (out_part.astype(F32) + out_other.astype(F32)) + out_full

    xhat_two, scale_two = norm_parts(hidden)
    normed_two = (xhat_two * gain_two + shift_two).astype(BF)
    up_blocks = up_own.reshape(2, 1, ff_own)
    upward = jnp.einsum("rd,yde->yre", normed_two, weight_up, preferred_element_type=F32)
    upward = upward + up_blocks
    active, gelu_back = jax.vjp(functools.partial(jax.nn.gelu, approximate=True), upward)
    active = active.astype(BF)
    down_wgrad = jnp.einsum("rd,yre->yde", cot, active, preferred_element_type=F32).astype(BF)
    active_grad = jnp.einsum("rd,yde->yre", cot, weight_down, preferred_element_type=F32)
    upward_grad = gelu_back(active_grad)[0].astype(BF)
    normed_two_part = jnp.einsum(
        "yre,yde->rd", upward_grad, weight_up, preferred_element_type=F32
    ).astype(BF)
    normed_two_other = swap(normed_two_part, "core", 1)
    up_wgrad = jnp.einsum(
        "rd,yre->yde", normed_two, upward_grad, preferred_element_type=F32
    ).astype(BF)
    mlp_part = jnp.einsum("yre,yde->rd", active, weight_down, preferred_element_type=F32)
    mlp_other = swap(other_half(mlp_part).astype(BF), "core", 1).astype(F32)
    block_out = (own_half(hidden) + own_half(mlp_part) + mlp_other + down_full).astype(BF)

    down_wgrad = scatter_grad(down_wgrad, dp_ref)
    up_wgrad = scatter_grad(up_wgrad, dp_ref)

    normed_two_grad = normed_two_part.astype(F32) + normed_two_other.astype(F32)
    hidden_grad = cot.astype(F32) + norm_back(xhat_two, scale_two, gain_two, normed_two_grad)
    branch_grad = hidden_grad.astype(BF)
    ctx_grad = nn_dot(branch_grad, w_ctx).astype(BF)
    proj_grad, qkv_bias_own = attend_back(projected, ctx_grad)
    out_wgrad = tn_dot(branch_grad, context).astype(BF)
    qkv_wgrad = tn_dot(normed_one, proj_grad).astype(BF)
    one_wgrad = jnp.concatenate(
        [
            qkv_wgrad.reshape(width, 3, 2, heads_own)
            .transpose(2, 0, 1, 3)
            .reshape(2, width, 3 * heads_own),
            out_wgrad.reshape(width, 2, heads_own).transpose(1, 0, 2),
        ],
        2,
    )
    one_wgrad = scatter_grad(one_wgrad, dp_ref)
    normed_one_part = nt_dot(proj_grad, w_proj)
    normed_one_other = swap(other_half(normed_one_part).astype(BF), "core", 1)
    normed_one_grad = own_half(normed_one_part) + normed_one_other.astype(F32)
    xhat_own = own_half(xhat_one)
    input_part = norm_back(xhat_own, own_half(scale_one), gain_one, normed_one_grad)
    tokens_grad = (own_half(hidden_grad) + input_part).astype(BF)

    def spread_blocks(values):
        lead = values.shape[:-1]
        block = values.shape[-1] // 2
        cut = values.reshape(lead + (2, 1, block))
        cut = jnp.where(y == 0, cut, cut[..., ::-1, :, :])
        cut = jnp.where(jnp.arange(2)[:, None] == core, cut, 0.0)
        return cut.reshape(lead + (4 * block,))

    qkv_bias_grad = spread_blocks(jnp.sum(qkv_bias_own, 0).reshape(3, 2 * heads_own))
    up_bias_grad = spread_blocks(jnp.sum(upward_grad.astype(F32), 1).reshape(-1))
    sums = [
        jnp.sum(normed_one_grad * xhat_own, 0),
        jnp.sum(normed_one_grad, 0),
        qkv_bias_grad,
        0.5 * jnp.sum(branch_grad.astype(F32), 0),
        0.5 * jnp.sum(normed_two_grad * xhat_two, 0),
        0.5 * jnp.sum(normed_two_grad, 0),
        up_bias_grad,
        jnp.sum(cotangent.astype(F32), 0),
    ]
    sums = [
        item.reshape(-1, dp_count, item.shape[-1] // dp_count).transpose(1, 0, 2).reshape(dp_count, -1)
        for item in sums
    ]
    sums = jnp.concatenate(sums, 1)
    sums = jnp.broadcast_to(sums[:, None, :], (dp_count, 4, sums.shape[1]))
    sums = lax.all_to_all(
        sums.reshape(dp_count * 4, -1), ("dp", "y", "core"), 0, 0, tiled=True
    )
    sums = jnp.sum(sums, 0)

    def piece_of(position, count=1):
        return sums[position * piece : (position + count) * piece]

    return (
        block_out,
        tokens_grad,
        piece_of(0),
        piece_of(1),
        one_wgrad[:, : 3 * heads_own].reshape(piece, 3, heads_own).transpose(1, 0, 2),
        piece_of(2, 3).reshape(3, piece),
        one_wgrad[:, 3 * heads_own :].T,
        piece_of(5),
        piece_of(6),
        piece_of(7),
        up_wgrad,
        sums[8 * piece : 8 * piece + ff_piece],
        down_wgrad.T,
        sums[8 * piece + ff_piece :],
    )


def solution(mesh):
    devices = mesh.devices
    split = Mesh(devices.reshape(devices.shape[0], 2, 2), ("dp", "y", "core"))
    tensor = ("y", "core")
    rows = P(("dp", "y", "core"), None)
    specs = (
        P("dp"),
        P("dp"),
        P(None, "dp", tensor),
        P(None, "dp"),
        P(tensor, "dp"),
        P("dp"),
        P("dp"),
        P("dp"),
        P("dp", tensor),
        P("dp"),
        P(tensor, "dp"),
        P("dp"),
    )
    return jax.shard_map(
        body,
        mesh=split,
        in_specs=(rows, rows) + specs,
        out_specs=(rows, rows) + specs,
        check_vma=False,
    )
```

```python
import jax
import jax.numpy as jnp
from jax import lax
from jax.experimental import pallas as pl
from jax.experimental.pallas import tpu as pltpu
from jax.sharding import Mesh
from jax.sharding import PartitionSpec as P

HEAD_DIM = 64
LENGTH = 1024
EPS = 1e-05
BLOCK = 256
BF = jnp.bfloat16
F32 = jnp.float32
VMEM_LIMIT = 48 * 1024 * 1024


def swap(value, axis, bit):
    size = lax.axis_size(axis)
    return lax.ppermute(value, axis, [(i, i ^ bit) for i in range(size)])


def nt_dot(left, right):
    return lax.dot_general(left, right, (((1,), (1,)), ((), ())), preferred_element_type=F32)


def tn_dot(left, right):
    return lax.dot_general(left, right, (((0,), (0,)), ((), ())), preferred_element_type=F32)


def nn_dot(left, right):
    return jnp.dot(left, right, preferred_element_type=F32)


def attend_kernel(p_ref, c_ref):
    width = c_ref.shape[1]
    pair = pl.multiple_of(pl.program_id(0) * 128, 128)
    q = p_ref[:, pl.ds(pair, 128)] * BF(HEAD_DIM**-0.5)
    k = p_ref[:, pl.ds(width + pair, 128)]
    v = p_ref[:, pl.ds(2 * width + pair, 128)]
    lane = lax.broadcasted_iota(jnp.int32, (LENGTH, 128), 1)
    low_lane = lax.broadcasted_iota(jnp.int32, (BLOCK, 128), 1) < HEAD_DIM
    causal = lax.broadcasted_iota(jnp.int32, (BLOCK, BLOCK), 0) >= lax.broadcasted_iota(
        jnp.int32, (BLOCK, BLOCK), 1
    )
    for start in range(0, LENGTH, BLOCK):
        stop = start + BLOCK
        halves = []
        for head in range(2):
            mine = (lane < HEAD_DIM) if head == 0 else (lane >= HEAD_DIM)
            q_part = jnp.where(mine[start:stop], q[start:stop], BF(0))
            v_part = jnp.where(mine[:stop], v[:stop], BF(1))
            scores = nt_dot(q_part, k[:stop])
            last = jnp.where(causal, scores[:, start:], -1e30)
            scores = jnp.concatenate([scores[:, :start], last], 1) if start else last
            top = jnp.max(scores, 1, keepdims=True)
            weights = jnp.exp(scores - top).astype(BF)
            result = nn_dot(weights, v_part)
            halves.append(result / pltpu.roll(result, HEAD_DIM, 1))
        c_ref[start:stop, pl.ds(pair, 128)] = jnp.where(low_lane, halves[0], halves[1]).astype(BF)


def attend(projected):
    width = projected.shape[1] // 3
    pairs = width // 128
    return pl.pallas_call(
        attend_kernel,
        out_shape=jax.ShapeDtypeStruct((LENGTH, width), BF),
        grid=(pairs,),
        in_specs=[pl.BlockSpec((LENGTH, 3 * width), lambda i: (0, 0))],
        out_specs=pl.BlockSpec((LENGTH, width), lambda i: (0, 0)),
        compiler_params=pltpu.CompilerParams(vmem_limit_bytes=VMEM_LIMIT),
        cost_estimate=pl.CostEstimate(
            flops=pairs * 4 * LENGTH * LENGTH * 128,
            bytes_accessed=LENGTH * width * 8,
            transcendentals=pairs * LENGTH * LENGTH,
        ),
        name="attend",
    )(projected)


def attend_back_kernel(p_ref, g_ref, d_ref, bias_ref, dk_ref, dv_ref, dq_ref):
    width = g_ref.shape[1]
    pair = pl.multiple_of(pl.program_id(0) * 128, 128)
    q = p_ref[:, pl.ds(pair, 128)] * BF(HEAD_DIM**-0.5)
    k = p_ref[:, pl.ds(width + pair, 128)]
    v = p_ref[:, pl.ds(2 * width + pair, 128)]
    g = g_ref[:, pl.ds(pair, 128)]
    lane = lax.broadcasted_iota(jnp.int32, (LENGTH, 128), 1)
    low_lane = lax.broadcasted_iota(jnp.int32, (BLOCK, 128), 1) < HEAD_DIM
    causal = lax.broadcasted_iota(jnp.int32, (BLOCK, BLOCK), 0) <= lax.broadcasted_iota(
        jnp.int32, (BLOCK, BLOCK), 1
    )
    dk_ref[...] = jnp.zeros_like(dk_ref)
    dv_ref[...] = jnp.zeros_like(dv_ref)
    for start in range(0, LENGTH, BLOCK):
        stop = start + BLOCK
        query_grads = []
        for head in range(2):
            mine = (lane < HEAD_DIM) if head == 0 else (lane >= HEAD_DIM)
            q_part = jnp.where(mine[start:stop], q[start:stop], BF(0))
            g_part = jnp.where(mine[start:stop], g[start:stop], BF(0))
            scores = nt_dot(k[:stop], q_part)
            last = jnp.where(causal, scores[start:], -1e30)
            scores = jnp.concatenate([scores[:start], last], 0) if start else last
            top = jnp.max(scores, 0, keepdims=True)
            weights = jnp.exp(scores - top)
            probs = weights * (1.0 / jnp.sum(weights, 0, keepdims=True))
            prob_grad = nt_dot(v[:stop], g_part)
            delta = jnp.sum(probs * prob_grad, 0, keepdims=True)
            score_grad = (probs * (prob_grad - delta)).astype(BF)
            dv_ref[:stop] += nn_dot(probs.astype(BF), g_part)
            dk_ref[:stop] += nn_dot(score_grad, q_part)
            query_grads.append(tn_dot(score_grad, k[:stop]))
        dq_ref[start:stop] = jnp.where(low_lane, query_grads[0], query_grads[1]) * HEAD_DIM**-0.5
    for position, ref in enumerate((dq_ref, dk_ref, dv_ref)):
        result = ref[...].astype(BF)
        columns = pl.ds(position * width + pair, 128)
        d_ref[:, columns] = result
        bias_ref[:, columns] = jnp.sum(
            result.astype(F32).reshape(LENGTH // 8, 8, 128), 0
        )


def attend_back(projected, ctx_grad):
    width = projected.shape[1] // 3
    pairs = width // 128
    return pl.pallas_call(
        attend_back_kernel,
        out_shape=(
            jax.ShapeDtypeStruct((LENGTH, 3 * width), BF),
            jax.ShapeDtypeStruct((8, 3 * width), F32),
        ),
        grid=(pairs,),
        in_specs=[
            pl.BlockSpec((LENGTH, 3 * width), lambda i: (0, 0)),
            pl.BlockSpec((LENGTH, width), lambda i: (0, 0)),
        ],
        out_specs=(
            pl.BlockSpec((LENGTH, 3 * width), lambda i: (0, 0)),
            pl.BlockSpec((8, 3 * width), lambda i: (0, 0)),
        ),
        scratch_shapes=[pltpu.VMEM((LENGTH, 128), F32)] * 3,
        compiler_params=pltpu.CompilerParams(vmem_limit_bytes=VMEM_LIMIT),
        cost_estimate=pl.CostEstimate(
            flops=pairs * 10 * LENGTH * LENGTH * 128,
            bytes_accessed=LENGTH * width * 14,
            transcendentals=pairs * LENGTH * LENGTH,
        ),
        name="attend_back",
    )(projected, ctx_grad)


def row_sums(values):
    return jnp.sum(values.reshape(values.shape[0] // 8, 8, values.shape[1]), 0)


def vmem_specs(count):
    return [pl.BlockSpec(memory_space=pltpu.VMEM)] * count


def smem_spec():
    return pl.BlockSpec(memory_space=pltpu.SMEM)


def params():
    return pltpu.CompilerParams(vmem_limit_bytes=VMEM_LIMIT)


def cost(flops, bytes_accessed, transcendentals=0):
    return pl.CostEstimate(
        flops=flops, bytes_accessed=bytes_accessed, transcendentals=transcendentals
    )


def place_kernel(dp_ref, h1_ref, h2_ref, h1y_ref, h2x_ref, w_ref):
    dp = dp_ref[0]
    for low in range(2):
        for x in range(2):
            w_ref[0, dp ^ (low * 2 + x)] = h1_ref[x * 2 + low]
            w_ref[1, dp ^ (low * 2 + x)] = h1y_ref[x * 2 + low]
        for row in range(2):
            w_ref[row, dp ^ (4 + low * 2)] = h2_ref[row * 2 + low]
            w_ref[row, dp ^ (4 + low * 2 + 1)] = h2x_ref[row * 2 + low]


def place_blocks(pieces, dp):
    if len(pieces) == 2:
        return jnp.stack(pieces)
    rows, columns = pieces[0].shape[1:]
    placed = pl.pallas_call(
        place_kernel,
        out_shape=jax.ShapeDtypeStruct((2, 8, rows, columns), BF),
        in_specs=[smem_spec()] + vmem_specs(4),
        out_specs=pl.BlockSpec(memory_space=pltpu.VMEM),
        compiler_params=params(),
        cost_estimate=cost(0, 64 * rows * columns),
        name="place",
    )(dp, *pieces)
    return placed.reshape(2, 8 * rows, columns)


def place_one_kernel(dp_ref, h1_ref, h2_ref, h1y_ref, h2x_ref, proj_ref, ctx_ref):
    dp = dp_ref[0]
    block = h1_ref.shape[2] // 4

    def put(index, own, other):
        for kind in range(4):
            columns = slice(kind * block, (kind + 1) * block)
            both = jnp.concatenate([own[:, columns], other[:, columns]], 1)
            if kind < 3:
                proj_ref[dp ^ index, :, kind * 2 * block : (kind + 1) * 2 * block] = both
            else:
                ctx_ref[dp ^ index] = both

    for low in range(2):
        for x in range(2):
            put(low * 2 + x, h1_ref[x * 2 + low], h1y_ref[x * 2 + low])
        put(4 + low * 2, h2_ref[low], h2_ref[2 + low])
        put(4 + low * 2 + 1, h2x_ref[low], h2x_ref[2 + low])


def place_one(pieces, dp):
    if len(pieces) == 2:
        width = pieces[0].shape[0]
        cut = jnp.stack([piece.reshape(width, 4, -1) for piece in pieces], 2)
        return cut[:, :3].reshape(width, -1), cut[:, 3].reshape(width, -1)
    rows, columns = pieces[0].shape[1:]
    proj, ctx = pl.pallas_call(
        place_one_kernel,
        out_shape=(
            jax.ShapeDtypeStruct((8, rows, columns * 3 // 2), BF),
            jax.ShapeDtypeStruct((8, rows, columns // 2), BF),
        ),
        in_specs=[smem_spec()] + vmem_specs(4),
        out_specs=tuple(vmem_specs(2)),
        compiler_params=params(),
        cost_estimate=cost(0, 64 * rows * columns),
        name="place_one",
    )(dp, *pieces)
    return proj.reshape(8 * rows, -1), ctx.reshape(8 * rows, -1)


def direct(shard):
    return lax.axis_size("dp") == 8 and shard.shape[0] % 16 == 0


def gather_z(shard):
    r1, r2, r3 = swap(shard, "dp", 2), swap(shard, "dp", 4), swap(shard, "dp", 6)
    return jnp.stack([shard, r1]), jnp.stack([r2, r3])


def gather_xy1(h1, h2):
    return swap(h1, "dp", 1), swap(h2, "y", 1)


def gather_xy2(h1, h2, h1x, h2y):
    h1 = jnp.concatenate([h1, h1x])
    h2 = jnp.concatenate([h2, h2y])
    return h1, h2, swap(h1, "y", 1), swap(h2, "dp", 1)


def gather_plain(shard):
    own = lax.all_gather(shard, "dp", axis=0, tiled=True)
    return own, swap(own, "y", 1)


def spread_put(dp, outs, result, row, columns=slice(None)):
    k1, s1, k2, s2, stage = outs
    rows = k1.shape[1]
    for index in range(8):
        stage[index] = result[index * rows : (index + 1) * rows].astype(BF)
    first = s1 if row else k1
    for low in range(2):
        for x in range(2):
            first[x * 2 + low, :, columns] = stage[dp ^ (low * 2 + x)]
        k2[row * 2 + low, :, columns] = stage[dp ^ (4 + low * 2)]
        s2[row * 2 + low, :, columns] = stage[dp ^ (4 + low * 2 + 1)]


def wgrad_kernel(dp_ref, left_ref, right_ref, k1, s1, k2, s2, stage):
    for row in range(2):
        result = tn_dot(left_ref[...], right_ref[row])
        spread_put(dp_ref[0], (k1, s1, k2, s2, stage), result, row)


def wgrad(left, right, dp):
    width = left.shape[1]
    columns = right.shape[2]
    count = lax.axis_size("dp")
    if count != 8 or (width // count) % 16:
        return jnp.einsum("rd,yre->yde", left, right, preferred_element_type=F32).astype(BF)
    part = jax.ShapeDtypeStruct((4, width // 8, columns), BF)
    return pl.pallas_call(
        wgrad_kernel,
        out_shape=(part,) * 4,
        in_specs=[smem_spec()] + vmem_specs(2),
        out_specs=tuple(vmem_specs(4)),
        scratch_shapes=[pltpu.VMEM((8, width // 8, columns), BF)],
        compiler_params=params(),
        cost_estimate=cost(4 * LENGTH * width * columns, 4 * (LENGTH + width) * columns * 2),
        name="wgrad",
    )(dp, left, right)


def wgrad_one_kernel(dp_ref, n_ref, d_ref, g_ref, c_ref, k1, s1, k2, s2, stage):
    block = c_ref.shape[1] // 2
    for kind in range(4):
        if kind < 3:
            left, right = n_ref, d_ref[:, kind * 2 * block : (kind + 1) * 2 * block]
        else:
            left, right = g_ref, c_ref[...]
        result = tn_dot(left[...], right)
        for row in range(2):
            spread_put(
                dp_ref[0],
                (k1, s1, k2, s2, stage),
                result[:, row * block : (row + 1) * block],
                row,
                slice(kind * block, (kind + 1) * block),
            )


def wgrad_one(normed, proj_grad, branch_grad, context, dp):
    width = normed.shape[1]
    block = context.shape[1] // 2
    count = lax.axis_size("dp")
    if count != 8 or (width // count) % 16:
        proj = tn_dot(normed, proj_grad).reshape(width, 3, 2, block)
        out = tn_dot(branch_grad, context).reshape(width, 1, 2, block)
        both = jnp.concatenate([proj, out], 1).transpose(2, 0, 1, 3)
        return both.reshape(2, width, 4 * block).astype(BF)
    part = jax.ShapeDtypeStruct((4, width // 8, 4 * block), BF)
    return pl.pallas_call(
        wgrad_one_kernel,
        out_shape=(part,) * 4,
        in_specs=[smem_spec()] + vmem_specs(4),
        out_specs=tuple(vmem_specs(4)),
        scratch_shapes=[pltpu.VMEM((8, width // 8, block), BF)],
        compiler_params=params(),
        cost_estimate=cost(16 * LENGTH * width * block, LENGTH * width * 10),
        name="wgrad_one",
    )(dp, normed, proj_grad, branch_grad, context)


def add_low(left, right):
    return (left.astype(F32) + right.astype(F32)).astype(BF)


def scatter_xy1(parts):
    k1, s1, k2, s2 = parts
    return k1, k2, swap(s1, "y", 1), swap(s2, "dp", 1)


def scatter_xy2(k1, k2, t1, t2):
    u1 = swap(add_low(k1[2:], t1[2:]), "dp", 1)
    u2 = swap(add_low(k2[2:], t2[2:]), "y", 1)
    return k1, k2, t1, t2, u1, u2


def scatter_z(k1, k2, t1, t2, u1, u2):
    v1 = k1[:2].astype(F32) + t1[:2].astype(F32) + u1.astype(F32)
    v2 = k2[:2].astype(F32) + t2[:2].astype(F32) + u2.astype(F32)
    r1 = swap(v1[1].astype(BF), "dp", 2)
    r2 = swap(v2[0].astype(BF), "dp", 4)
    r3 = swap(v2[1].astype(BF), "dp", 6)
    return v1[0], r1, r2, r3


def scatter_end(v, r1, r2, r3):
    return v + r1.astype(F32) + r2.astype(F32) + r3.astype(F32)


def scatter_plain(grad):
    both = grad[0].astype(F32) + swap(grad[1], "y", 1).astype(F32)
    return lax.psum_scatter(both, "dp", scatter_dimension=0, tiled=True)


def norm_parts(values):
    center = values - jnp.mean(values, -1, keepdims=True)
    spread = jnp.mean(center * center, -1, keepdims=True)
    scale = lax.rsqrt(spread + EPS)
    return center * scale, scale


def norm_back(xhat, scale, gain, grad):
    scaled = grad * gain
    first = jnp.mean(scaled, -1, keepdims=True)
    second = jnp.mean(scaled * xhat, -1, keepdims=True)
    return scale * (scaled - first - xhat * second)


def rows_spec(columns, lead=None):
    if lead is None:
        return pl.BlockSpec((BLOCK, columns), lambda i, c: (i, 0))
    return pl.BlockSpec((lead, BLOCK, columns), lambda i, c: (0, i, 0))


def whole_spec(shape):
    return pl.BlockSpec(shape, lambda i, c: (0,) * len(shape))


def half_spec(columns, mine):
    per_core = LENGTH // 2 // BLOCK

    def index(i, c):
        inside = i // per_core == (c[0] if mine else 1 - c[0])
        return (jnp.where(inside, i % per_core, 0), 0)

    return pl.BlockSpec((BLOCK, columns), index)


def pick_rows(core_ref, own_ref, other_ref):
    per_core = LENGTH // 2 // BLOCK
    mine = (pl.program_id(0) // per_core == core_ref[0]).astype(F32)
    return own_ref[...].astype(F32) * mine + other_ref[...].astype(F32) * (1.0 - mine)


def block_call(kernel, name, outs, specs, grid, scratch=(), estimate=None):
    return pl.pallas_call(
        kernel,
        out_shape=tuple(shape for shape, _ in outs),
        grid_spec=pltpu.PrefetchScalarGridSpec(
            num_scalar_prefetch=1,
            grid=(grid,),
            in_specs=specs,
            out_specs=tuple(spec for _, spec in outs),
            scratch_shapes=list(scratch),
        ),
        compiler_params=params(),
        cost_estimate=estimate,
        name=name,
    )


def project_kernel(core_ref, own_ref, other_ref, gain_ref, shift_ref, w_ref, b_ref, n_ref, p_ref):
    xhat, _ = norm_parts(pick_rows(core_ref, own_ref, other_ref))
    normed = (xhat * gain_ref[...] + shift_ref[...]).astype(BF)
    n_ref[...] = normed
    p_ref[...] = (nn_dot(normed, w_ref[...]) + b_ref[...]).astype(BF)


def project(core, own, other, gain, shift, weight, bias):
    width, columns = weight.shape
    return block_call(
        project_kernel,
        "project",
        [
            (jax.ShapeDtypeStruct((LENGTH, width), BF), rows_spec(width)),
            (jax.ShapeDtypeStruct((LENGTH, columns), BF), rows_spec(columns)),
        ],
        [
            half_spec(width, True),
            half_spec(width, False),
            whole_spec((1, width)),
            whole_spec((1, width)),
            whole_spec((width, columns)),
            whole_spec((1, columns)),
        ],
        LENGTH // BLOCK,
        estimate=cost(2 * LENGTH * width * columns, LENGTH * (width * 4 + columns * 2)),
    )(core, own, other, gain[None], shift[None], weight, bias[None])


def up_kernel(
    core_ref, own_ref, other_ref, part_ref, part_other_ref, ob_ref, gain_ref, shift_ref, w_ref, b_ref,
    h_ref, n_ref, a_ref, d_ref,
):
    attended = part_ref[...].astype(F32) + part_other_ref[...].astype(F32)
    hidden = pick_rows(core_ref, own_ref, other_ref) + attended + ob_ref[...]
    h_ref[...] = hidden
    xhat, _ = norm_parts(hidden)
    normed = (xhat * gain_ref[...] + shift_ref[...]).astype(BF)
    n_ref[...] = normed
    slope = 0.7978845608028654
    for row in range(2):
        up = nn_dot(normed, w_ref[row]) + b_ref[row]
        square = up * up
        bend = jnp.tanh(up * (slope + slope * 0.044715 * square))
        half = 0.5 * up
        a_ref[row] = (half + half * bend).astype(BF)
        inner = slope + slope * 3 * 0.044715 * square
        d_ref[row] = (0.5 + 0.5 * bend + half * (1.0 - bend * bend) * inner).astype(BF)


def up_project(core, own, other, part, part_other, out_bias, gain, shift, weight, bias):
    width, columns = weight.shape[1:]
    low = jax.ShapeDtypeStruct((LENGTH, width), BF)
    both = jax.ShapeDtypeStruct((2, LENGTH, columns), BF)
    return block_call(
        up_kernel,
        "up_project",
        [
            (jax.ShapeDtypeStruct((LENGTH, width), F32), rows_spec(width)),
            (low, rows_spec(width)),
            (both, rows_spec(columns, 2)),
            (both, rows_spec(columns, 2)),
        ],
        [
            half_spec(width, True),
            half_spec(width, False),
            rows_spec(width),
            rows_spec(width),
            whole_spec((1, width)),
            whole_spec((1, width)),
            whole_spec((1, width)),
            whole_spec((2, width, columns)),
            whole_spec((2, 1, columns)),
        ],
        LENGTH // BLOCK,
        estimate=cost(
            4 * LENGTH * width * columns, LENGTH * (width * 12 + columns * 8), LENGTH * columns * 2
        ),
    )(
        core, own, other, part, part_other, out_bias[None], gain[None], shift[None], weight,
        bias[:, None],
    )


def up_back_kernel(core_ref, cot_ref, d_ref, down_ref, up_ref, u_ref, b_ref, n_ref):
    total = None
    for row in range(2):
        grad = nn_dot(cot_ref[...], down_ref[row]) * d_ref[row].astype(F32)
        low = grad.astype(BF)
        u_ref[row] = low
        sums = row_sums(low.astype(F32))

        @pl.when(pl.program_id(0) == 0)
        def _():
            b_ref[row] = sums

        @pl.when(pl.program_id(0) > 0)
        def _():
            b_ref[row] += sums

        part = nt_dot(low, up_ref[row])
        total = part if total is None else total + part
    n_ref[...] = total.astype(BF)


def up_back(core, cot, slope, down, up):
    width, columns = down.shape[1:]
    return block_call(
        up_back_kernel,
        "up_back",
        [
            (jax.ShapeDtypeStruct((2, LENGTH, columns), BF), rows_spec(columns, 2)),
            (jax.ShapeDtypeStruct((2, 8, columns), F32), whole_spec((2, 8, columns))),
            (jax.ShapeDtypeStruct((LENGTH, width), BF), rows_spec(width)),
        ],
        [
            rows_spec(width),
            rows_spec(columns, 2),
            whole_spec((2, width, columns)),
            whole_spec((2, width, columns)),
        ],
        LENGTH // BLOCK,
        estimate=cost(8 * LENGTH * width * columns, LENGTH * (width * 4 + columns * 8)),
    )(core, cot, slope, down, up)


def second_back_kernel(
    core_ref, h_ref, part_ref, other_ref, cot_ref, gain_ref, w_ref, dh_ref, do_ref, dc_ref, sum_ref
):
    xhat, scale = norm_parts(h_ref[...])
    grad = part_ref[...].astype(F32) + other_ref[...].astype(F32)
    hidden_grad = cot_ref[...].astype(F32) + norm_back(xhat, scale, gain_ref[...], grad)
    low = hidden_grad.astype(BF)
    dh_ref[...] = hidden_grad
    do_ref[...] = low
    dc_ref[...] = nn_dot(low, w_ref[...]).astype(BF)
    sums = (row_sums(low.astype(F32)), row_sums(grad * xhat), row_sums(grad))
    for position, value in enumerate(sums):

        @pl.when(pl.program_id(0) == 0)
        def _():
            sum_ref[position] = value

        @pl.when(pl.program_id(0) > 0)
        def _():
            sum_ref[position] += value


def second_back(core, hidden, part, other, cot, gain, weight):
    width, columns = weight.shape
    return block_call(
        second_back_kernel,
        "second_back",
        [
            (jax.ShapeDtypeStruct((LENGTH, width), F32), rows_spec(width)),
            (jax.ShapeDtypeStruct((LENGTH, width), BF), rows_spec(width)),
            (jax.ShapeDtypeStruct((LENGTH, columns), BF), rows_spec(columns)),
            (jax.ShapeDtypeStruct((3, 8, width), F32), whole_spec((3, 8, width))),
        ],
        [rows_spec(width)] * 4 + [whole_spec((1, width)), whole_spec((width, columns))],
        LENGTH // BLOCK,
        estimate=cost(2 * LENGTH * width * columns, LENGTH * (width * 16 + columns * 2)),
    )(core, hidden, part, other, cot, gain[None], weight)


def first_back_kernel(core_ref, x_ref, part_ref, other_ref, dh_ref, gain_ref, t_ref, sum_ref):
    xhat, scale = norm_parts(x_ref[...].astype(F32))
    grad = part_ref[...] + other_ref[...].astype(F32)
    t_ref[...] = (dh_ref[...] + norm_back(xhat, scale, gain_ref[...], grad)).astype(BF)
    for position, value in enumerate((row_sums(grad * xhat), row_sums(grad))):

        @pl.when(pl.program_id(0) == 0)
        def _():
            sum_ref[position] = value

        @pl.when(pl.program_id(0) > 0)
        def _():
            sum_ref[position] += value


def first_back(core, own, part, other, hidden_grad, gain):
    width = own.shape[1]
    per_core = LENGTH // 2 // BLOCK
    mine = pl.BlockSpec((BLOCK, width), lambda i, c: (c[0] * per_core + i, 0))
    return block_call(
        first_back_kernel,
        "first_back",
        [
            (jax.ShapeDtypeStruct((LENGTH // 2, width), BF), rows_spec(width)),
            (jax.ShapeDtypeStruct((2, 8, width), F32), whole_spec((2, 8, width))),
        ],
        [rows_spec(width), mine, rows_spec(width), mine, whole_spec((1, width))],
        per_core,
        estimate=cost(0, LENGTH * width * 8),
    )(core, own, part, other, hidden_grad, gain[None])


def body(
    tokens,
    cotangent,
    first_gain,
    first_shift,
    w_qkv,
    qkv_bias,
    w_out,
    out_bias,
    second_gain,
    second_shift,
    w_up,
    up_bias,
    w_down,
    down_bias,
):
    dp_count = lax.axis_size("dp")
    dp = lax.axis_index("dp")
    y = lax.axis_index("y")
    core = lax.axis_index("core")
    dp_ref = dp.reshape(1).astype(jnp.int32)
    own_rows, width = tokens.shape
    piece = first_gain.shape[0]
    heads_own = w_qkv.shape[2]
    ff_own = w_up.shape[1]
    ff_piece = up_bias.shape[0]

    vectors = jnp.concatenate(
        [
            first_gain,
            first_shift,
            qkv_bias.reshape(-1),
            out_bias,
            second_gain,
            second_shift,
            up_bias,
            down_bias,
        ]
    )
    vectors = lax.all_to_all(
        jnp.broadcast_to(vectors[None], (dp_count, vectors.shape[0])), "dp", 0, 0, tiled=True
    )

    def full(position, count=1):
        return vectors[:, position * piece : (position + count) * piece]

    gain_one = full(0).reshape(-1)
    shift_one = full(1).reshape(-1)
    qkv_full = full(2, 3).reshape(dp_count, 3, piece).transpose(1, 0, 2).reshape(3, width)
    out_full = full(5).reshape(-1)
    gain_two = full(6).reshape(-1)
    shift_two = full(7).reshape(-1)
    up_full = vectors[:, 8 * piece : 8 * piece + ff_piece].reshape(-1)
    down_full = vectors[:, 8 * piece + ff_piece :].reshape(-1)

    def own_blocks(values):
        lead = values.shape[:-1]
        block = values.shape[-1] // 4
        cut = values.reshape(lead + (2, 2, block))
        cut = jnp.where(core == 0, cut[..., 0, :], cut[..., 1, :])
        first = jnp.where(y == 0, cut[..., 0, :], cut[..., 1, :])
        second = jnp.where(y == 0, cut[..., 1, :], cut[..., 0, :])
        return jnp.concatenate([first, second], -1)

    qkv_own = own_blocks(qkv_full).reshape(-1)
    up_own = own_blocks(up_full)

    core_ref = core.reshape(1).astype(jnp.int32)

    shard_one = jnp.concatenate([w_qkv[0], w_qkv[1], w_qkv[2], w_out.T], 1)
    shard_up, shard_down = w_up, w_down.T
    fast = direct(shard_one)
    tie = lax.optimization_barrier
    if fast:
        one = gather_z(shard_one)
        one_xy1 = gather_xy1(*one)
        one, shard_up = tie((one, shard_up))
        up = gather_z(shard_up)
        up_xy1 = gather_xy1(*up)
        one = gather_xy2(*one, *one_xy1)
        up, shard_down = tie((up, shard_down))
        down = gather_z(shard_down)
        up = up + up_xy1
        one, up = tie((one, up))
        up = gather_xy2(*up)
    else:
        one, up, down = gather_plain(shard_one), gather_plain(shard_up), gather_plain(shard_down)

    def own_half(rows):
        return lax.dynamic_slice_in_dim(rows, core * own_rows, own_rows, 0)

    def other_half(rows):
        return lax.dynamic_slice_in_dim(rows, (1 - core) * own_rows, own_rows, 0)

    tokens_other = swap(tokens, "core", 1)
    cot_other = swap(cotangent, "core", 1)
    cot = jnp.where(
        core == 0,
        jnp.concatenate([cotangent, cot_other], 0),
        jnp.concatenate([cot_other, cotangent], 0),
    )

    w_proj, w_ctx = place_one(one, dp_ref)
    normed_one, projected = project(
        core_ref, tokens, tokens_other, gain_one, shift_one, w_proj, qkv_own
    )
    if fast:
        projected, down = tie((projected, down))
        down = down + gather_xy1(*down)
    context = attend(projected)
    if fast:
        context, up, down = tie((context, up, down))
        down = gather_xy2(*down)
    out_part = nt_dot(context, w_ctx).astype(BF)
    out_other = swap(out_part, "core", 1)
    weight_up = place_blocks(up, dp_ref)
    hidden, normed_two, active, slope = up_project(
        core_ref,
        tokens,
        tokens_other,
        out_part,
        out_other,
        out_full,
        gain_two,
        shift_two,
        weight_up,
        up_own.reshape(2, ff_own),
    )
    down_wgrad = wgrad(cot, active, dp_ref)
    if fast:
        down, down_wgrad = tie((down, down_wgrad))
        down_wgrad = scatter_xy1(down_wgrad)
    weight_down = place_blocks(down, dp_ref)
    upward_grad, up_bias_sums, normed_two_part = up_back(
        core_ref, cot, slope, weight_down, weight_up
    )
    normed_two_other = swap(normed_two_part, "core", 1)
    up_wgrad = wgrad(normed_two, upward_grad, dp_ref)
    if fast:
        up_wgrad, down_wgrad, normed_two_other = tie((up_wgrad, down_wgrad, normed_two_other))
        up_wgrad = scatter_xy1(up_wgrad)
        down_wgrad = scatter_xy2(*down_wgrad)
    hidden_grad, branch_grad, ctx_grad, second_sums = second_back(
        core_ref, hidden, normed_two_part, normed_two_other, cot, gain_two, w_ctx
    )
    proj_grad, qkv_bias_own = attend_back(projected, ctx_grad)
    if fast:
        proj_grad, up_wgrad, down_wgrad = tie((proj_grad, up_wgrad, down_wgrad))
        up_wgrad = scatter_xy2(*up_wgrad)
        down_wgrad = scatter_z(*down_wgrad)
    one_wgrad = wgrad_one(normed_one, proj_grad, branch_grad, context, dp_ref)
    if fast:
        one_wgrad, up_wgrad, down_wgrad = tie((one_wgrad, up_wgrad, down_wgrad))
        one_wgrad = scatter_xy1(one_wgrad)
        up_wgrad = scatter_z(*up_wgrad)
        down_wgrad = scatter_end(*down_wgrad)
    normed_one_part = nt_dot(proj_grad, w_proj)
    normed_one_other = swap(other_half(normed_one_part).astype(BF), "core", 1)
    mlp_part = jnp.einsum("yre,yde->rd", active, weight_down, preferred_element_type=F32)
    mlp_other = swap(other_half(mlp_part).astype(BF), "core", 1).astype(F32)
    block_out = (own_half(hidden) + own_half(mlp_part) + mlp_other + down_full).astype(BF)
    tokens_grad, first_sums = first_back(
        core_ref, tokens, normed_one_part, normed_one_other, hidden_grad, gain_one
    )
    if fast:
        one_wgrad = scatter_xy2(*one_wgrad)
        one_wgrad = scatter_z(*one_wgrad)
        one_wgrad = scatter_end(*one_wgrad)
        up_wgrad = scatter_end(*up_wgrad)
    else:
        one_wgrad = scatter_plain(one_wgrad)
        up_wgrad = scatter_plain(up_wgrad)
        down_wgrad = scatter_plain(down_wgrad)

    def spread_blocks(values):
        lead = values.shape[:-1]
        block = values.shape[-1] // 2
        own, other = values[..., :block], values[..., block:]
        cut = [jnp.where(y == 0, own, other), jnp.where(y == 0, other, own)]
        return jnp.concatenate(
            [jnp.where(core == index, half, 0.0) for half in cut for index in range(2)], -1
        )

    qkv_bias_grad = spread_blocks(jnp.sum(qkv_bias_own, 0).reshape(3, 2 * heads_own))
    up_bias_grad = spread_blocks(jnp.sum(up_bias_sums, 1).reshape(-1))
    first_sums = jnp.sum(first_sums, 1)
    second_sums = 0.5 * jnp.sum(second_sums, 1)
    sums = [
        first_sums[0],
        first_sums[1],
        qkv_bias_grad,
        second_sums[0],
        second_sums[1],
        second_sums[2],
        up_bias_grad,
        jnp.sum(cotangent.astype(F32), 0),
    ]
    sums = [
        item.reshape(-1, dp_count, item.shape[-1] // dp_count).transpose(1, 0, 2).reshape(dp_count, -1)
        for item in sums
    ]
    sums = jnp.concatenate(sums, 1)
    sums = jnp.broadcast_to(sums[:, None, :], (dp_count, 4, sums.shape[1]))
    sums = lax.all_to_all(
        sums.reshape(dp_count * 4, -1), ("dp", "y", "core"), 0, 0, tiled=True
    )
    sums = jnp.sum(sums, 0)

    def piece_of(position, count=1):
        return sums[position * piece : (position + count) * piece]

    return (
        block_out,
        tokens_grad,
        piece_of(0),
        piece_of(1),
        one_wgrad[:, : 3 * heads_own].reshape(piece, 3, heads_own).transpose(1, 0, 2),
        piece_of(2, 3).reshape(3, piece),
        one_wgrad[:, 3 * heads_own :].T,
        piece_of(5),
        piece_of(6),
        piece_of(7),
        up_wgrad,
        sums[8 * piece : 8 * piece + ff_piece],
        down_wgrad.T,
        sums[8 * piece + ff_piece :],
    )


def solution(mesh):
    devices = mesh.devices
    split = Mesh(devices.reshape(devices.shape[0], 2, 2), ("dp", "y", "core"))
    tensor = ("y", "core")
    rows = P(("dp", "y", "core"), None)
    specs = (
        P("dp"),
        P("dp"),
        P(None, "dp", tensor),
        P(None, "dp"),
        P(tensor, "dp"),
        P("dp"),
        P("dp"),
        P("dp"),
        P("dp", tensor),
        P("dp"),
        P(tensor, "dp"),
        P("dp"),
    )
    return jax.shard_map(
        body,
        mesh=split,
        in_specs=(rows, rows) + specs,
        out_specs=(rows, rows) + specs,
        check_vma=False,
    )
```

```python
import functools

import jax
import jax.numpy as jnp
from jax import lax
from jax.experimental import pallas as pl
from jax.experimental.pallas import tpu as pltpu
from jax.sharding import Mesh
from jax.sharding import PartitionSpec as P

HEAD_DIM = 64
LENGTH = 1024
EPS = 1e-05
BLOCK = 256
ROWS = 512
BF = jnp.bfloat16
F32 = jnp.float32
VMEM_LIMIT = 48 * 1024 * 1024


def swap(value, axis, bit):
    size = lax.axis_size(axis)
    return lax.ppermute(value, axis, [(i, i ^ bit) for i in range(size)])


def nt_dot(left, right):
    return lax.dot_general(left, right, (((1,), (1,)), ((), ())), preferred_element_type=F32)


def tn_dot(left, right):
    return lax.dot_general(left, right, (((0,), (0,)), ((), ())), preferred_element_type=F32)


def nn_dot(left, right):
    return jnp.dot(left, right, preferred_element_type=F32)


def attend_pair(p_ref, pair, width):
    q = p_ref[:, pl.ds(pair, 128)] * BF(HEAD_DIM**-0.5)
    k = p_ref[:, pl.ds(width + pair, 128)]
    v = p_ref[:, pl.ds(2 * width + pair, 128)]
    lane = lax.broadcasted_iota(jnp.int32, (LENGTH, 128), 1)
    low_lane = lax.broadcasted_iota(jnp.int32, (BLOCK, 128), 1) < HEAD_DIM
    causal = lax.broadcasted_iota(jnp.int32, (BLOCK, BLOCK), 0) >= lax.broadcasted_iota(
        jnp.int32, (BLOCK, BLOCK), 1
    )
    for start in range(0, LENGTH, BLOCK):
        stop = start + BLOCK
        halves = []
        for head in range(2):
            mine = (lane < HEAD_DIM) if head == 0 else (lane >= HEAD_DIM)
            q_part = jnp.where(mine[start:stop], q[start:stop], BF(0))
            v_part = jnp.where(mine[:stop], v[:stop], BF(1))
            scores = nt_dot(q_part, k[:stop])
            last = jnp.where(causal, scores[:, start:], -1e30)
            scores = jnp.concatenate([scores[:, :start], last], 1) if start else last
            top = jnp.max(scores, 1, keepdims=True)
            weights = jnp.exp(scores - top).astype(BF)
            result = nn_dot(weights, v_part)
            halves.append(result / pltpu.roll(result, HEAD_DIM, 1))
        yield start, jnp.where(low_lane, halves[0], halves[1]).astype(BF)


def attend_first_kernel(p_ref, c_ref):
    for start, context in attend_pair(p_ref, 0, p_ref.shape[1] // 3):
        c_ref[start : start + BLOCK] = context


def attend_rest_kernel(p_ref, first_ref, c_ref):
    width = c_ref.shape[1]
    pair = pl.multiple_of((pl.program_id(0) + 1) * 128, 128)
    for start, context in attend_pair(p_ref, pair, width):
        c_ref[start : start + BLOCK, pl.ds(pair, 128)] = context

    @pl.when(pl.program_id(0) == 0)
    def _():
        c_ref[:, :128] = first_ref[...]


def attend_cost(pairs, factor):
    return pl.CostEstimate(flops=0, bytes_accessed=0, transcendentals=0)


def attend_first(projected):
    return pl.pallas_call(
        attend_first_kernel,
        out_shape=jax.ShapeDtypeStruct((LENGTH, 128), BF),
        in_specs=[pl.BlockSpec(memory_space=pltpu.VMEM)],
        out_specs=pl.BlockSpec(memory_space=pltpu.VMEM),
        compiler_params=pltpu.CompilerParams(vmem_limit_bytes=VMEM_LIMIT),
        cost_estimate=attend_cost(1, 4),
        name="attend_first",
    )(projected)


def attend_rest(projected, first):
    width = projected.shape[1] // 3
    pairs = width // 128 - 1
    return pl.pallas_call(
        attend_rest_kernel,
        out_shape=jax.ShapeDtypeStruct((LENGTH, width), BF),
        grid=(pairs,),
        in_specs=[
            pl.BlockSpec((LENGTH, 3 * width), lambda i: (0, 0)),
            pl.BlockSpec((LENGTH, 128), lambda i: (0, 0)),
        ],
        out_specs=pl.BlockSpec((LENGTH, width), lambda i: (0, 0)),
        compiler_params=pltpu.CompilerParams(vmem_limit_bytes=VMEM_LIMIT),
        cost_estimate=attend_cost(pairs, 4),
        name="attend_rest",
    )(projected, first)


def attend_back_pair(p_ref, g_ref, pair, width, dk_ref, dv_ref, dq_ref):
    q = p_ref[:, pl.ds(pair, 128)] * BF(HEAD_DIM**-0.5)
    k = p_ref[:, pl.ds(width + pair, 128)]
    v = p_ref[:, pl.ds(2 * width + pair, 128)]
    g = g_ref[:, pl.ds(pair, 128)]
    lane = lax.broadcasted_iota(jnp.int32, (LENGTH, 128), 1)
    low_lane = lax.broadcasted_iota(jnp.int32, (BLOCK, 128), 1) < HEAD_DIM
    causal = lax.broadcasted_iota(jnp.int32, (BLOCK, BLOCK), 0) <= lax.broadcasted_iota(
        jnp.int32, (BLOCK, BLOCK), 1
    )
    dk_ref[...] = jnp.zeros_like(dk_ref)
    dv_ref[...] = jnp.zeros_like(dv_ref)
    for start in range(0, LENGTH, BLOCK):
        stop = start + BLOCK
        query_grads = []
        for head in range(2):
            mine = (lane < HEAD_DIM) if head == 0 else (lane >= HEAD_DIM)
            q_part = jnp.where(mine[start:stop], q[start:stop], BF(0))
            g_part = jnp.where(mine[start:stop], g[start:stop], BF(0))
            scores = nt_dot(k[:stop], q_part)
            last = jnp.where(causal, scores[start:], -1e30)
            scores = jnp.concatenate([scores[:start], last], 0) if start else last
            top = jnp.max(scores, 0, keepdims=True)
            weights = jnp.exp(scores - top)
            probs = weights * (1.0 / jnp.sum(weights, 0, keepdims=True))
            prob_grad = nt_dot(v[:stop], g_part)
            delta = jnp.sum(probs * prob_grad, 0, keepdims=True)
            score_grad = (probs * (prob_grad - delta)).astype(BF)
            dv_ref[:stop] += nn_dot(probs.astype(BF), g_part)
            dk_ref[:stop] += nn_dot(score_grad, q_part)
            query_grads.append(tn_dot(score_grad, k[:stop]))
        dq_ref[start:stop] = jnp.where(low_lane, query_grads[0], query_grads[1]) * HEAD_DIM**-0.5
    return [ref[...].astype(BF) for ref in (dq_ref, dk_ref, dv_ref)]


def column_sums(values):
    return jnp.sum(values.astype(F32).reshape(LENGTH // 8, 8, 128), 0)


def attend_back_part_kernel(pair, p_ref, g_ref, d_ref, dk_ref, dv_ref, dq_ref):
    width = g_ref.shape[1]
    results = attend_back_pair(p_ref, g_ref, pair * 128, width, dk_ref, dv_ref, dq_ref)
    for position, result in enumerate(results):
        d_ref[:, position * 128 : (position + 1) * 128] = result


def attend_back_last_kernel(p_ref, g_ref, *refs):
    parts, (d_ref, bias_ref, dk_ref, dv_ref, dq_ref) = refs[:-5], refs[-5:]
    width = g_ref.shape[1]
    results = attend_back_pair(p_ref, g_ref, len(parts) * 128, width, dk_ref, dv_ref, dq_ref)
    pieces = [[ref[:, i * 128 : (i + 1) * 128] for i in range(3)] for ref in parts]
    for pair, piece in enumerate(pieces + [results]):
        for position, result in enumerate(piece):
            columns = slice(position * width + pair * 128, position * width + pair * 128 + 128)
            d_ref[:, columns] = result
            bias_ref[:, columns] = column_sums(result)


def attend_back_part(projected, ctx_grad, pair):
    return pl.pallas_call(
        functools.partial(attend_back_part_kernel, pair),
        out_shape=jax.ShapeDtypeStruct((LENGTH, 384), BF),
        in_specs=[pl.BlockSpec(memory_space=pltpu.VMEM)] * 2,
        out_specs=pl.BlockSpec(memory_space=pltpu.VMEM),
        scratch_shapes=[pltpu.VMEM((LENGTH, 128), F32)] * 3,
        compiler_params=pltpu.CompilerParams(vmem_limit_bytes=VMEM_LIMIT),
        cost_estimate=attend_cost(1, 10),
        name="attend_back_part",
    )(projected, ctx_grad)


def attend_back_last(projected, ctx_grad, parts):
    width = projected.shape[1]
    return pl.pallas_call(
        attend_back_last_kernel,
        out_shape=(
            jax.ShapeDtypeStruct((LENGTH, width), BF),
            jax.ShapeDtypeStruct((8, width), F32),
        ),
        in_specs=[pl.BlockSpec(memory_space=pltpu.VMEM)] * (2 + len(parts)),
        out_specs=(pl.BlockSpec(memory_space=pltpu.VMEM),) * 2,
        scratch_shapes=[pltpu.VMEM((LENGTH, 128), F32)] * 3,
        compiler_params=pltpu.CompilerParams(vmem_limit_bytes=VMEM_LIMIT),
        cost_estimate=attend_cost(1, 10),
        name="attend_back_last",
    )(projected, ctx_grad, *parts)


def row_sums(values):
    return jnp.sum(values.reshape(values.shape[0] // 8, 8, values.shape[1]), 0)


def vmem_specs(count):
    return [pl.BlockSpec(memory_space=pltpu.VMEM)] * count


def smem_spec():
    return pl.BlockSpec(memory_space=pltpu.SMEM)


def params():
    return pltpu.CompilerParams(vmem_limit_bytes=VMEM_LIMIT)


def cost(flops, bytes_accessed, transcendentals=0):
    return pl.CostEstimate(flops=0, bytes_accessed=0, transcendentals=0)


def place_kernel(dp_ref, h1_ref, h2_ref, h1y_ref, h2x_ref, w_ref):
    dp = dp_ref[0]
    for low in range(2):
        for x in range(2):
            w_ref[0, dp ^ (low * 2 + x)] = h1_ref[x * 2 + low]
            w_ref[1, dp ^ (low * 2 + x)] = h1y_ref[x * 2 + low]
        for row in range(2):
            w_ref[row, dp ^ (4 + low * 2)] = h2_ref[row * 2 + low]
            w_ref[row, dp ^ (4 + low * 2 + 1)] = h2x_ref[row * 2 + low]


def place_blocks(pieces, dp):
    if len(pieces) == 2:
        return jnp.stack(pieces)
    rows, columns = pieces[0].shape[1:]
    placed = pl.pallas_call(
        place_kernel,
        out_shape=jax.ShapeDtypeStruct((2, 8, rows, columns), BF),
        in_specs=[smem_spec()] + vmem_specs(4),
        out_specs=pl.BlockSpec(memory_space=pltpu.VMEM),
        compiler_params=params(),
        cost_estimate=cost(0, 64 * rows * columns),
        name="place",
    )(dp, *pieces)
    return placed.reshape(2, 8 * rows, columns)


def place_one_kernel(dp_ref, h1_ref, h2_ref, h1y_ref, h2x_ref, proj_ref, ctx_ref):
    dp = dp_ref[0]
    block = h1_ref.shape[2] // 4

    def put(index, own, other):
        for kind in range(4):
            columns = slice(kind * block, (kind + 1) * block)
            both = jnp.concatenate([own[:, columns], other[:, columns]], 1)
            if kind < 3:
                proj_ref[dp ^ index, :, kind * 2 * block : (kind + 1) * 2 * block] = both
            else:
                ctx_ref[dp ^ index] = both

    for low in range(2):
        for x in range(2):
            put(low * 2 + x, h1_ref[x * 2 + low], h1y_ref[x * 2 + low])
        put(4 + low * 2, h2_ref[low], h2_ref[2 + low])
        put(4 + low * 2 + 1, h2x_ref[low], h2x_ref[2 + low])


def place_one(pieces, dp):
    if len(pieces) == 2:
        width = pieces[0].shape[0]
        cut = jnp.stack([piece.reshape(width, 4, -1) for piece in pieces], 2)
        return cut[:, :3].reshape(width, -1), cut[:, 3].reshape(width, -1)
    rows, columns = pieces[0].shape[1:]
    proj, ctx = pl.pallas_call(
        place_one_kernel,
        out_shape=(
            jax.ShapeDtypeStruct((8, rows, columns * 3 // 2), BF),
            jax.ShapeDtypeStruct((8, rows, columns // 2), BF),
        ),
        in_specs=[smem_spec()] + vmem_specs(4),
        out_specs=tuple(vmem_specs(2)),
        compiler_params=params(),
        cost_estimate=cost(0, 64 * rows * columns),
        name="place_one",
    )(dp, *pieces)
    return proj.reshape(8 * rows, -1), ctx.reshape(8 * rows, -1)


def direct(shard):
    return lax.axis_size("dp") == 8 and shard.shape[0] % 16 == 0


def gather_z(shard):
    return swap(shard, "dp", 2), swap(shard, "dp", 4), swap(shard, "dp", 6)


def pair_up(shard, r1, r2, r3):
    return jnp.stack([shard, r1]), jnp.stack([r2, r3])


def gather_xy1(h1, h2):
    return swap(h1, "dp", 1), swap(h2, "y", 1)


def gather_xy2(h1, h2, h1x, h2y):
    h1 = jnp.concatenate([h1, h1x])
    h2 = jnp.concatenate([h2, h2y])
    return h1, h2, swap(h1, "y", 1), swap(h2, "dp", 1)


def gather_plain(shard):
    own = lax.all_gather(shard, "dp", axis=0, tiled=True)
    return own, swap(own, "y", 1)


def spread_put(dp, outs, result, row, columns=slice(None)):
    k1, s1, k2, s2, stage = outs
    rows = k1.shape[1]
    for index in range(8):
        stage[index] = result[index * rows : (index + 1) * rows].astype(BF)
    first = s1 if row else k1
    for low in range(2):
        for x in range(2):
            first[x * 2 + low, :, columns] = stage[dp ^ (low * 2 + x)]
        k2[row * 2 + low, :, columns] = stage[dp ^ (4 + low * 2)]
        s2[row * 2 + low, :, columns] = stage[dp ^ (4 + low * 2 + 1)]


def wgrad_kernel(dp_ref, left_ref, right_ref, k1, s1, k2, s2, stage):
    for row in range(2):

        @pl.when(pl.program_id(0) == row)
        def _():
            result = tn_dot(left_ref[...], right_ref[0])
            spread_put(dp_ref[0], (k1, s1, k2, s2, stage), result, row)


def wgrad(left, right, dp):
    width = left.shape[1]
    columns = right.shape[2]
    count = lax.axis_size("dp")
    if count != 8 or (width // count) % 16:
        return jnp.einsum("rd,yre->yde", left, right, preferred_element_type=F32).astype(BF)
    part = jax.ShapeDtypeStruct((4, width // 8, columns), BF)
    return pl.pallas_call(
        wgrad_kernel,
        out_shape=(part,) * 4,
        grid=(2,),
        in_specs=[
            smem_spec(),
            pl.BlockSpec((LENGTH, width), lambda i: (0, 0)),
            pl.BlockSpec((1, LENGTH, columns), lambda i: (i, 0, 0)),
        ],
        out_specs=(pl.BlockSpec(part.shape, lambda i: (0, 0, 0)),) * 4,
        scratch_shapes=[pltpu.VMEM((8, width // 8, columns), BF)],
        compiler_params=params(),
        cost_estimate=cost(0, 0),
        name="wgrad",
    )(dp, left, right)


def wgrad_one_kernel(dp_ref, n_ref, d_ref, g_ref, c_ref, k1, s1, k2, s2, stage):
    block = c_ref.shape[1] // 2
    for kind in range(4):

        @pl.when(pl.program_id(0) == kind)
        def _():
            left, right = (n_ref, d_ref) if kind < 3 else (g_ref, c_ref)
            result = tn_dot(left[...], right[...])
            for row in range(2):
                spread_put(
                    dp_ref[0],
                    (k1, s1, k2, s2, stage),
                    result[:, row * block : (row + 1) * block],
                    row,
                    slice(kind * block, (kind + 1) * block),
                )


def wgrad_one(normed, proj_grad, branch_grad, context, dp):
    width = normed.shape[1]
    block = context.shape[1] // 2
    count = lax.axis_size("dp")
    if count != 8 or (width // count) % 16:
        proj = tn_dot(normed, proj_grad).reshape(width, 3, 2, block)
        out = tn_dot(branch_grad, context).reshape(width, 1, 2, block)
        both = jnp.concatenate([proj, out], 1).transpose(2, 0, 1, 3)
        return both.reshape(2, width, 4 * block).astype(BF)
    part = jax.ShapeDtypeStruct((4, width // 8, 4 * block), BF)
    return pl.pallas_call(
        wgrad_one_kernel,
        out_shape=(part,) * 4,
        grid=(4,),
        in_specs=[
            smem_spec(),
            pl.BlockSpec((LENGTH, width), lambda i: (0, 0)),
            pl.BlockSpec((LENGTH, 2 * block), lambda i: (0, jnp.minimum(i, 2))),
            pl.BlockSpec((LENGTH, width), lambda i: (0, 0)),
            pl.BlockSpec((LENGTH, 2 * block), lambda i: (0, 0)),
        ],
        out_specs=(pl.BlockSpec(part.shape, lambda i: (0, 0, 0)),) * 4,
        scratch_shapes=[pltpu.VMEM((8, width // 8, block), BF)],
        compiler_params=params(),
        cost_estimate=cost(16 * LENGTH * width * block, LENGTH * width * 10),
        name="wgrad_one",
    )(dp, normed, proj_grad, branch_grad, context)


def add_kernel(*refs):
    ins, (first, second) = refs[:-2], refs[-2:]
    columns = ins[0].shape[2]
    for i in range(len(ins) // 4):
        k1, t1, k2, t2 = ins[4 * i : 4 * i + 4]
        cut = slice(i * columns, (i + 1) * columns)
        first[:, :, cut] = (k1[...].astype(F32) + t1[...].astype(F32)).astype(BF)
        second[:, :, cut] = (k2[...].astype(F32) + t2[...].astype(F32)).astype(BF)


def sum_kernel(*refs):
    u1, u2, *ins, v, z1, z2, z3 = refs
    columns = ins[0].shape[2]
    for i in range(len(ins) // 4):
        k1, t1, k2, t2 = ins[4 * i : 4 * i + 4]
        cut = slice(i * columns, (i + 1) * columns)

        def total(k, t, u, index):
            return k[index].astype(F32) + t[index].astype(F32) + u[index, :, cut].astype(F32)

        v[:, cut] = total(k1, t1, u1, 0)
        z1[:, cut] = total(k1, t1, u1, 1).astype(BF)
        z2[:, cut] = total(k2, t2, u2, 0).astype(BF)
        z3[:, cut] = total(k2, t2, u2, 1).astype(BF)


def pair_spec(shape, index):
    return pl.BlockSpec((2,) + shape[1:], lambda i: (index, 0, 0))


def scatter_xy1(parts):
    k1, s1, k2, s2 = parts
    return k1, swap(s1, "y", 1), k2, swap(s2, "dp", 1)


def scatter_xy2(*items):
    _, rows, columns = items[0][0].shape
    half = jax.ShapeDtypeStruct((2, rows, columns * len(items)), BF)
    flat = [part for item in items for part in item]
    first, second = pl.pallas_call(
        add_kernel,
        out_shape=(half, half),
        grid=(1,),
        in_specs=[pair_spec(part.shape, 1) for part in flat],
        out_specs=(pair_spec(half.shape, 0),) * 2,
        compiler_params=params(),
        cost_estimate=cost(0, 0),
        name="add_pairs",
    )(*flat)
    return swap(first, "dp", 1), swap(second, "y", 1)


def scatter_z(sent, *items):
    _, rows, columns = sent[0].shape
    low = jax.ShapeDtypeStruct((rows, columns), BF)
    whole = pl.BlockSpec((rows, columns), lambda i: (0, 0))
    flat = [part for item in items for part in item]
    v, z1, z2, z3 = pl.pallas_call(
        sum_kernel,
        out_shape=(jax.ShapeDtypeStruct((rows, columns), F32), low, low, low),
        grid=(1,),
        in_specs=[pair_spec(part.shape, 0) for part in list(sent) + flat],
        out_specs=(whole,) * 4,
        compiler_params=params(),
        cost_estimate=cost(0, 0),
        name="sum_pairs",
    )(*sent, *flat)
    return v, swap(z1, "dp", 2), swap(z2, "dp", 4), swap(z3, "dp", 6)


def scatter_end(v, r1, r2, r3):
    return v + r1.astype(F32) + r2.astype(F32) + r3.astype(F32)


def scatter_plain(grad):
    both = grad[0].astype(F32) + swap(grad[1], "y", 1).astype(F32)
    return lax.psum_scatter(both, "dp", scatter_dimension=0, tiled=True)


def norm_parts(values):
    center = values - jnp.mean(values, -1, keepdims=True)
    spread = jnp.mean(center * center, -1, keepdims=True)
    scale = lax.rsqrt(spread + EPS)
    return center * scale, scale


def norm_back(xhat, scale, gain, grad):
    scaled = grad * gain
    first = jnp.mean(scaled, -1, keepdims=True)
    second = jnp.mean(scaled * xhat, -1, keepdims=True)
    return scale * (scaled - first - xhat * second)


def rows_spec(columns, lead=None):
    if lead is None:
        return pl.BlockSpec((ROWS, columns), lambda i, c: (i, 0))
    return pl.BlockSpec((lead, ROWS, columns), lambda i, c: (0, i, 0))


def whole_spec(shape):
    return pl.BlockSpec(shape, lambda i, c: (0,) * len(shape))


def half_spec(columns, mine):
    per_core = LENGTH // 2 // ROWS

    def index(i, c):
        inside = i // per_core == (c[0] if mine else 1 - c[0])
        return (jnp.where(inside, i % per_core, 0), 0)

    return pl.BlockSpec((ROWS, columns), index)


def pick_rows(core_ref, own_ref, other_ref):
    per_core = LENGTH // 2 // ROWS
    mine = (pl.program_id(0) // per_core == core_ref[0]).astype(F32)
    return own_ref[...].astype(F32) * mine + other_ref[...].astype(F32) * (1.0 - mine)


def block_call(kernel, name, outs, specs, grid, scratch=(), estimate=None):
    return pl.pallas_call(
        kernel,
        out_shape=tuple(shape for shape, _ in outs),
        grid_spec=pltpu.PrefetchScalarGridSpec(
            num_scalar_prefetch=1,
            grid=(grid,),
            in_specs=specs,
            out_specs=tuple(spec for _, spec in outs),
            scratch_shapes=list(scratch),
        ),
        compiler_params=params(),
        cost_estimate=estimate,
        name=name,
    )


def prepare_kernel(
    core_ref, own_ref, other_ref, cot_ref, cot_other_ref, gain_ref, shift_ref, n_ref, c_ref, s_ref
):
    cot = pick_rows(core_ref, cot_ref, cot_other_ref)
    c_ref[...] = cot.astype(BF)
    sums = row_sums(cot)

    @pl.when(pl.program_id(0) == 0)
    def _():
        s_ref[...] = sums

    @pl.when(pl.program_id(0) > 0)
    def _():
        s_ref[...] += sums

    xhat, _ = norm_parts(pick_rows(core_ref, own_ref, other_ref))
    n_ref[...] = (xhat * gain_ref[...] + shift_ref[...]).astype(BF)


def prepare(core, own, other, cot, cot_other, gain, shift):
    width = own.shape[1]
    rows = (jax.ShapeDtypeStruct((LENGTH, width), BF), rows_spec(width))
    return block_call(
        prepare_kernel,
        "prepare",
        [rows, rows, (jax.ShapeDtypeStruct((8, width), F32), whole_spec((8, width)))],
        [
            half_spec(width, True),
            half_spec(width, False),
            half_spec(width, True),
            half_spec(width, False),
            whole_spec((1, width)),
            whole_spec((1, width)),
        ],
        LENGTH // ROWS,
        estimate=cost(0, 0),
    )(core, own, other, cot, cot_other, gain, shift)


def project_kernel(core_ref, n_ref, w_ref, b_ref, p_ref):
    p_ref[...] = (nn_dot(n_ref[...], w_ref[...]) + b_ref[...]).astype(BF)


def project(core, normed, weight, bias):
    width, columns = weight.shape
    return block_call(
        project_kernel,
        "project",
        [(jax.ShapeDtypeStruct((LENGTH, columns), BF), rows_spec(columns))],
        [rows_spec(width), whole_spec((width, columns)), whole_spec((1, columns))],
        LENGTH // ROWS,
        estimate=cost(0, 0),
    )(core, normed, weight, bias)[0]


def up_kernel(
    core_ref, own_ref, other_ref, part_ref, part_other_ref, ob_ref, gain_ref, shift_ref, w_ref, b_ref,
    h_ref, n_ref, a_ref, d_ref,
):
    attended = part_ref[...].astype(F32) + part_other_ref[...].astype(F32)
    hidden = pick_rows(core_ref, own_ref, other_ref) + attended + ob_ref[...]
    h_ref[...] = hidden
    xhat, _ = norm_parts(hidden)
    normed = (xhat * gain_ref[...] + shift_ref[...]).astype(BF)
    n_ref[...] = normed
    slope = 0.7978845608028654
    for row in range(2):
        up = nn_dot(normed, w_ref[row]) + b_ref[row]
        square = up * up
        gate = 1.0 / (1.0 + jnp.exp(up * (-2.0 * slope - 2.0 * slope * 0.044715 * square)))
        gated = up * gate
        a_ref[row] = gated.astype(BF)
        inner = 2.0 * slope + 6.0 * slope * 0.044715 * square
        d_ref[row] = (gate + (gated - gated * gate) * inner).astype(BF)


def up_project(core, own, other, part, part_other, out_bias, gain, shift, weight, bias):
    width, columns = weight.shape[1:]
    low = jax.ShapeDtypeStruct((LENGTH, width), BF)
    both = jax.ShapeDtypeStruct((2, LENGTH, columns), BF)
    return block_call(
        up_kernel,
        "up_project",
        [
            (jax.ShapeDtypeStruct((LENGTH, width), F32), rows_spec(width)),
            (low, rows_spec(width)),
            (both, rows_spec(columns, 2)),
            (both, rows_spec(columns, 2)),
        ],
        [
            half_spec(width, True),
            half_spec(width, False),
            rows_spec(width),
            rows_spec(width),
            whole_spec((1, width)),
            whole_spec((1, width)),
            whole_spec((1, width)),
            whole_spec((2, width, columns)),
            whole_spec((2, 1, columns)),
        ],
        LENGTH // ROWS,
        estimate=cost(
            4 * LENGTH * width * columns, LENGTH * (width * 12 + columns * 8), LENGTH * columns * 2
        ),
    )(
        core, own, other, part, part_other, out_bias, gain, shift, weight,
        bias[:, None],
    )


def up_back_kernel(core_ref, cot_ref, d_ref, down_ref, up_ref, u_ref, b_ref, n_ref):
    total = None
    for row in range(2):
        grad = nn_dot(cot_ref[...], down_ref[row]) * d_ref[row].astype(F32)
        low = grad.astype(BF)
        u_ref[row] = low
        sums = row_sums(low.astype(F32))

        @pl.when(pl.program_id(0) == 0)
        def _():
            b_ref[row] = sums

        @pl.when(pl.program_id(0) > 0)
        def _():
            b_ref[row] += sums

        part = nt_dot(low, up_ref[row])
        total = part if total is None else total + part
    n_ref[...] = total.astype(BF)


def up_back(core, cot, slope, down, up):
    width, columns = down.shape[1:]
    return block_call(
        up_back_kernel,
        "up_back",
        [
            (jax.ShapeDtypeStruct((2, LENGTH, columns), BF), rows_spec(columns, 2)),
            (jax.ShapeDtypeStruct((2, 8, columns), F32), whole_spec((2, 8, columns))),
            (jax.ShapeDtypeStruct((LENGTH, width), BF), rows_spec(width)),
        ],
        [
            rows_spec(width),
            rows_spec(columns, 2),
            whole_spec((2, width, columns)),
            whole_spec((2, width, columns)),
        ],
        LENGTH // ROWS,
        estimate=cost(8 * LENGTH * width * columns, LENGTH * (width * 4 + columns * 8)),
    )(core, cot, slope, down, up)


def second_back_kernel(
    core_ref, h_ref, part_ref, other_ref, cot_ref, gain_ref, w_ref, dh_ref, do_ref, dc_ref, sum_ref
):
    xhat, scale = norm_parts(h_ref[...])
    grad = part_ref[...].astype(F32) + other_ref[...].astype(F32)
    hidden_grad = cot_ref[...].astype(F32) + norm_back(xhat, scale, gain_ref[...], grad)
    low = hidden_grad.astype(BF)
    dh_ref[...] = hidden_grad
    do_ref[...] = low
    dc_ref[...] = nn_dot(low, w_ref[...]).astype(BF)
    sums = (row_sums(low.astype(F32)), row_sums(grad * xhat), row_sums(grad))
    for position, value in enumerate(sums):

        @pl.when(pl.program_id(0) == 0)
        def _():
            sum_ref[position] = value

        @pl.when(pl.program_id(0) > 0)
        def _():
            sum_ref[position] += value


def second_back(core, hidden, part, other, cot, gain, weight):
    width, columns = weight.shape
    return block_call(
        second_back_kernel,
        "second_back",
        [
            (jax.ShapeDtypeStruct((LENGTH, width), F32), rows_spec(width)),
            (jax.ShapeDtypeStruct((LENGTH, width), BF), rows_spec(width)),
            (jax.ShapeDtypeStruct((LENGTH, columns), BF), rows_spec(columns)),
            (jax.ShapeDtypeStruct((3, 8, width), F32), whole_spec((3, 8, width))),
        ],
        [rows_spec(width)] * 4 + [whole_spec((1, width)), whole_spec((width, columns))],
        LENGTH // ROWS,
        estimate=cost(2 * LENGTH * width * columns, LENGTH * (width * 16 + columns * 2)),
    )(core, hidden, part, other, cot, gain, weight)


def share(core, left, weight):
    count, _, depth = left.shape
    width = weight.shape[1]
    half = LENGTH // 2

    def kernel(core_ref, left_ref, weight_ref, own_ref, other_ref):
        total = nt_dot(left_ref[0], weight_ref[0])
        for index in range(1, count):
            total = total + nt_dot(left_ref[index], weight_ref[index])

        @pl.when(pl.program_id(0) == 0)
        def _():
            other_ref[...] = total.astype(BF)

        @pl.when(pl.program_id(0) == 1)
        def _():
            own_ref[...] = total

    def rows(i, c):
        return (0, jnp.where(i == 0, 1 - c[0], c[0]), 0)

    return block_call(
        kernel,
        "share",
        [
            (jax.ShapeDtypeStruct((half, width), F32), whole_spec((half, width))),
            (jax.ShapeDtypeStruct((half, width), BF), whole_spec((half, width))),
        ],
        [pl.BlockSpec((count, half, depth), rows), whole_spec(weight.shape)],
        2,
        estimate=cost(0, 0),
    )(core, left, weight)


def first_back_kernel(core_ref, x_ref, part_ref, other_ref, dh_ref, gain_ref, t_ref, sum_ref):
    xhat, scale = norm_parts(x_ref[...].astype(F32))
    grad = part_ref[...] + other_ref[...].astype(F32)
    t_ref[...] = (dh_ref[...] + norm_back(xhat, scale, gain_ref[...], grad)).astype(BF)
    for position, value in enumerate((row_sums(grad * xhat), row_sums(grad))):

        @pl.when(pl.program_id(0) == 0)
        def _():
            sum_ref[position] = value

        @pl.when(pl.program_id(0) > 0)
        def _():
            sum_ref[position] += value


def first_back(core, own, part, other, hidden_grad, gain):
    width = own.shape[1]
    per_core = LENGTH // 2 // ROWS
    mine = pl.BlockSpec((ROWS, width), lambda i, c: (c[0] * per_core + i, 0))
    return block_call(
        first_back_kernel,
        "first_back",
        [
            (jax.ShapeDtypeStruct((LENGTH // 2, width), BF), rows_spec(width)),
            (jax.ShapeDtypeStruct((2, 8, width), F32), whole_spec((2, 8, width))),
        ],
        [rows_spec(width), rows_spec(width), rows_spec(width), mine, whole_spec((1, width))],
        per_core,
        estimate=cost(0, LENGTH * width * 8),
    )(core, own, part, other, hidden_grad, gain)


def unpack_kernel(place_ref, v_ref, g1, s1, qkv, ob, g2, s2, up, down, full):
    y, core = place_ref[0], place_ref[1]
    piece = g1.shape[1] // 8
    for d in range(8):
        rows = v_ref[d : d + 1]
        here = slice(d * piece, (d + 1) * piece)
        for ref, position in ((g1, 0), (s1, 1), (ob, 5), (g2, 6), (s2, 7), (down, 12)):
            ref[:, here] = rows[:, position * piece : (position + 1) * piece]
        for kind in range(3):
            full[kind : kind + 1, here] = rows[:, (2 + kind) * piece : (3 + kind) * piece]
        cut = slice(d % 2 * 4 * piece, (d % 2 + 1) * 4 * piece)
        full[3 + d // 2 : 4 + d // 2, cut] = rows[:, 8 * piece : 12 * piece]
    block = 2 * piece
    for kind in range(3):
        for y_index in range(2):
            cuts = []
            for core_index in range(2):
                at = (2 * y_index + core_index) * block
                cuts.append(full[kind : kind + 1, at : at + block])
            value = jnp.where(core == 0, cuts[0], cuts[1])
            for own in range(2):

                @pl.when((y ^ y_index) == own)
                def _():
                    at = (2 * kind + own) * block
                    qkv[:, at : at + block] = value

    for y_index in range(2):
        rows = [full[3 + 2 * y_index + i : 4 + 2 * y_index + i] for i in range(2)]
        value = jnp.where(core == 0, rows[0], rows[1])
        for own in range(2):

            @pl.when((y ^ y_index) == own)
            def _():
                up[own : own + 1] = value


def unpack(place, vectors, width):
    row = jax.ShapeDtypeStruct((1, width), F32)
    wide = jax.ShapeDtypeStruct((1, 3 * width // 2), F32)
    return pl.pallas_call(
        unpack_kernel,
        out_shape=(row, row, wide, row, row, row, jax.ShapeDtypeStruct((2, width), F32), row),
        in_specs=[smem_spec()] + vmem_specs(1),
        out_specs=tuple(vmem_specs(8)),
        scratch_shapes=[pltpu.VMEM((8, width), F32)],
        compiler_params=params(),
        cost_estimate=cost(0, 0),
        name="unpack",
    )(place, vectors)


def pack_kernel(place_ref, first_ref, qkv_ref, second_ref, up_ref, cot_ref, out_ref, full):
    y, core = place_ref[0], place_ref[1]
    width = full.shape[1]
    piece, block = width // 8, width // 4

    def column_sum(values):
        return jnp.sum(values, 0, keepdims=True)

    full[0:1] = column_sum(first_ref[0])
    full[1:2] = column_sum(first_ref[1])
    for position, index in ((5, 0), (6, 1), (7, 2)):
        full[position : position + 1] = 0.5 * column_sum(second_ref[index])
    full[12:13] = 0.5 * column_sum(cot_ref[...])
    qkv = column_sum(qkv_ref[...])
    ups = [column_sum(up_ref[index]) for index in range(2)]
    for t in range(4):
        keep = (core == t % 2).astype(F32)
        mine = (y == t // 2).astype(F32)
        for kind in range(3):
            at = kind * 2 * block
            value = qkv[:, at : at + block] * mine + qkv[:, at + block : at + 2 * block] * (1.0 - mine)
            full[2 + kind : 3 + kind, t * block : (t + 1) * block] = value * keep
        full[8 + t : 9 + t] = (ups[0] * mine + ups[1] * (1.0 - mine)) * keep
    for d in range(8):
        here = slice(d * piece, (d + 1) * piece)
        for copy in range(4):
            out_ref[4 * d + copy, 0:8] = full[0:8, here]
            out_ref[4 * d + copy, 12:13] = full[12:13, here]
            for j in range(4):
                at = d % 2 * 4 * piece + j * piece
                out_ref[4 * d + copy, 8 + j : 9 + j] = full[8 + d // 2 : 9 + d // 2, at : at + piece]


def pack(place, first, qkv, second, up, cot):
    width = cot.shape[1]
    return pl.pallas_call(
        pack_kernel,
        out_shape=jax.ShapeDtypeStruct((32, 13, width // 8), F32),
        in_specs=[smem_spec()] + vmem_specs(5),
        out_specs=pl.BlockSpec(memory_space=pltpu.VMEM),
        scratch_shapes=[pltpu.VMEM((16, width), F32)],
        compiler_params=params(),
        cost_estimate=cost(0, 0),
        name="pack",
    )(place, first, qkv, second, up, cot)


def body(
    tokens,
    cotangent,
    first_gain,
    first_shift,
    w_qkv,
    qkv_bias,
    w_out,
    out_bias,
    second_gain,
    second_shift,
    w_up,
    up_bias,
    w_down,
    down_bias,
):
    dp_count = lax.axis_size("dp")
    dp = lax.axis_index("dp")
    y = lax.axis_index("y")
    core = lax.axis_index("core")
    dp_ref = dp.reshape(1).astype(jnp.int32)
    own_rows, width = tokens.shape
    piece = first_gain.shape[0]
    heads_own = w_qkv.shape[2]
    ff_own = w_up.shape[1]
    ff_piece = up_bias.shape[0]

    core_ref = core.reshape(1).astype(jnp.int32)
    place_ref = jnp.stack([y, core]).astype(jnp.int32)
    shard_one = jnp.concatenate([w_qkv[0], w_qkv[1], w_qkv[2], w_out.T], 1)
    fast = direct(shard_one)
    tie = lax.optimization_barrier
    tokens_other = swap(tokens, "core", 1)
    vectors = jnp.concatenate(
        [
            first_gain,
            first_shift,
            qkv_bias.reshape(-1),
            out_bias,
            second_gain,
            second_shift,
            up_bias,
            down_bias,
        ]
    )
    vectors = lax.all_to_all(
        jnp.broadcast_to(vectors[None], (dp_count, vectors.shape[0])), "dp", 0, 0, tiled=True
    )

    def own_half(rows):
        return lax.dynamic_slice_in_dim(rows, core * own_rows, own_rows, 0)

    def exchange(rows):
        cuts = [rows[i * BLOCK : (i + 1) * BLOCK] for i in range(rows.shape[0] // BLOCK)]
        return jnp.concatenate([swap(cut, "core", 1) for cut in cuts])

    if fast:
        one = gather_z(shard_one)
        shard_one, one, vectors, tokens_other, cotangent, w_up, w_down = tie(
            (shard_one, one, vectors, tokens_other, cotangent, w_up, w_down)
        )
        one = pair_up(shard_one, *one)
        one_xy1 = gather_xy1(*one)
        one, one_xy1, vectors, cotangent, w_up, w_down = tie(
            (one, one_xy1, vectors, cotangent, w_up, w_down)
        )
        one = gather_xy2(*one, *one_xy1)
        up = gather_z(w_up)
        cot_other = swap(cotangent, "core", 1)
        cot_other, vectors, w_down = tie((cot_other, vectors, w_down))
        shard_down = w_down.T
        gain_one, shift_one, qkv_own, out_full, gain_two, shift_two, up_own, down_full = unpack(
            place_ref, vectors, width
        )
    else:
        one, up, down = map(gather_plain, (shard_one, w_up, w_down.T))
        cot_other = swap(cotangent, "core", 1)

        def full(position, count=1):
            return vectors[:, position * piece : (position + count) * piece]

        def own_blocks(values):
            cut = values.reshape(values.shape[0], 2, 2, -1)
            cut = jnp.where(core == 0, cut[:, :, 0], cut[:, :, 1])
            both = [cut[:, 0], cut[:, 1]]
            first = jnp.where(y == 0, both[0], both[1])
            second = jnp.where(y == 0, both[1], both[0])
            return jnp.stack([first, second], 1)

        gain_one, shift_one, out_full, gain_two, shift_two = (
            full(position).reshape(1, -1) for position in (0, 1, 5, 6, 7)
        )
        qkv_full = full(2, 3).reshape(dp_count, 3, piece).transpose(1, 0, 2).reshape(3, width)
        qkv_own = own_blocks(qkv_full).reshape(1, -1)
        up_own = own_blocks(vectors[:, 8 * piece : 8 * piece + ff_piece].reshape(1, -1))[0]
        down_full = vectors[:, 8 * piece + ff_piece :].reshape(1, -1)
    normed_one, cot, cot_sums = prepare(
        core_ref, tokens, tokens_other, cotangent, cot_other, gain_one, shift_one
    )

    if fast:
        one, up, normed_one, cot, qkv_own, shard_down = tie(
            (one, up, normed_one, cot, qkv_own, shard_down)
        )
        up = pair_up(w_up, *up)
        up_xy1 = gather_xy1(*up)
        down = gather_z(shard_down)
    w_proj, w_ctx = place_one(one, dp_ref)
    projected = project(core_ref, normed_one, w_proj, qkv_own)
    context_first = attend_first(projected)
    if fast:
        context_first, up, up_xy1, down = tie((context_first, up, up_xy1, down))
        up = gather_xy2(*up, *up_xy1)
    context = attend_rest(projected, context_first)
    if fast:
        context, up, down = tie((context, up, down))
        down = pair_up(shard_down, *down)
        down_xy1 = gather_xy1(*down)
    out_part = nt_dot(context, w_ctx).astype(BF)
    out_other = exchange(out_part)

    if fast:
        out_other, down, down_xy1 = tie((out_other, down, down_xy1))
        down = gather_xy2(*down, *down_xy1)
    weight_up = place_blocks(up, dp_ref)
    hidden, normed_two, active, slope = up_project(
        core_ref,
        tokens,
        tokens_other,
        out_part,
        out_other,
        out_full,
        gain_two,
        shift_two,
        weight_up,
        up_own,
    )
    down_wgrad = wgrad(cot, active, dp_ref)
    if fast:
        down_wgrad, down, slope = tie((down_wgrad, down, slope))
        down_wgrad = scatter_xy1(down_wgrad)
    weight_down = place_blocks(down, dp_ref)
    upward_grad, up_bias_sums, normed_two_part = up_back(
        core_ref, cot, slope, weight_down, weight_up
    )
    up_wgrad = wgrad(normed_two, upward_grad, dp_ref)
    if fast:
        up_wgrad, down_wgrad, normed_two_part = tie((up_wgrad, down_wgrad, normed_two_part))
        up_wgrad = scatter_xy1(up_wgrad)
        down_sent = scatter_xy2(down_wgrad)
    normed_two_other = exchange(normed_two_part)

    hidden_grad, branch_grad, ctx_grad, second_sums = second_back(
        core_ref, hidden, normed_two_part, normed_two_other, cot, gain_two, w_ctx
    )
    parts = [attend_back_part(projected, ctx_grad, pair) for pair in range(2)]
    if fast:
        parts, up_wgrad, down_sent, ctx_grad = tie((parts, up_wgrad, down_sent, ctx_grad))
        up_sent = scatter_xy2(up_wgrad)
        down_wgrad = scatter_z(down_sent, down_wgrad)
    proj_grad, qkv_bias_own = attend_back_last(projected, ctx_grad, parts)
    one_wgrad = wgrad_one(normed_one, proj_grad, branch_grad, context, dp_ref)
    if fast:
        one_wgrad, proj_grad, up_sent, down_wgrad, active = tie(
            (one_wgrad, proj_grad, up_sent, down_wgrad, active)
        )
        one_wgrad = scatter_xy1(one_wgrad)
        up_wgrad = scatter_z(up_sent, up_wgrad)
    normed_one_part, sent = share(core_ref, proj_grad[None], w_proj[None])
    normed_one_other = swap(sent, "core", 1)
    tokens_grad, first_sums = first_back(
        core_ref, tokens, normed_one_part, normed_one_other, hidden_grad, gain_one
    )

    if fast:
        sums = pack(place_ref, first_sums, qkv_bias_own, second_sums, up_bias_sums, cot_sums)
    else:

        def spread_blocks(values):
            block = values.shape[-1] // 2
            own, other = values[..., :block], values[..., block:]
            cut = [jnp.where(y == 0, own, other), jnp.where(y == 0, other, own)]
            return jnp.concatenate(
                [jnp.where(core == index, half, 0.0) for half in cut for index in range(2)], -1
            )

        sums = [
            jnp.sum(first_sums, 1),
            spread_blocks(jnp.sum(qkv_bias_own, 0).reshape(3, 2 * heads_own)),
            0.5 * jnp.sum(second_sums, 1),
            spread_blocks(jnp.sum(up_bias_sums, 1).reshape(1, -1)),
            0.5 * jnp.sum(cot_sums, 0)[None],
        ]
        sums = [
            item.reshape(item.shape[0], dp_count, -1).transpose(1, 0, 2).reshape(dp_count, -1)
            for item in sums
        ]
        sums = jnp.concatenate(sums, 1)
        sums = jnp.broadcast_to(sums[:, None, :], (dp_count, 4, sums.shape[1]))
        sums = sums.reshape(dp_count * 4, -1)
    mlp_part, mlp_sent = share(core_ref, active, weight_down)
    if fast:
        one_wgrad, sums, up_wgrad, mlp_sent = tie((one_wgrad, sums, up_wgrad, mlp_sent))
        one_sent = scatter_xy2(one_wgrad)
        up_wgrad = scatter_end(*up_wgrad)
        down_wgrad = scatter_end(*down_wgrad)
    sums = lax.all_to_all(sums, ("dp", "y", "core"), 0, 0, tiled=True)
    if fast:
        one_sent, sums, mlp_sent = tie((one_sent, sums, mlp_sent))
        one_wgrad = scatter_z(one_sent, one_wgrad)
    sums = jnp.sum(sums, 0).reshape(-1)
    mlp_other = swap(mlp_sent, "core", 1).astype(F32)
    block_out = (own_half(hidden) + mlp_part + mlp_other + down_full).astype(BF)
    if fast:
        one_wgrad = scatter_end(*one_wgrad)
    else:
        one_wgrad, up_wgrad, down_wgrad = map(scatter_plain, (one_wgrad, up_wgrad, down_wgrad))

    def piece_of(position, count=1):
        return sums[position * piece : (position + count) * piece]

    return (
        block_out,
        tokens_grad,
        piece_of(0),
        piece_of(1),
        one_wgrad[:, : 3 * heads_own].reshape(piece, 3, heads_own).transpose(1, 0, 2),
        piece_of(2, 3).reshape(3, piece),
        one_wgrad[:, 3 * heads_own :].T,
        piece_of(5),
        piece_of(6),
        piece_of(7),
        up_wgrad,
        sums[8 * piece : 8 * piece + ff_piece],
        down_wgrad.T,
        sums[8 * piece + ff_piece :],
    )


def solution(mesh):
    devices = mesh.devices
    split = Mesh(devices.reshape(devices.shape[0], 2, 2), ("dp", "y", "core"))
    tensor = ("y", "core")
    rows = P(("dp", "y", "core"), None)
    specs = (
        P("dp"),
        P("dp"),
        P(None, "dp", tensor),
        P(None, "dp"),
        P(tensor, "dp"),
        P("dp"),
        P("dp"),
        P("dp"),
        P("dp", tensor),
        P("dp"),
        P(tensor, "dp"),
        P("dp"),
    )
    return jax.shard_map(
        body,
        mesh=split,
        in_specs=(rows, rows) + specs,
        out_specs=(rows, rows) + specs,
        check_vma=False,
    )
```

```python
import functools

import jax
import jax.numpy as jnp
from jax import lax
from jax.experimental import pallas as pl
from jax.experimental.pallas import tpu as pltpu
from jax.sharding import Mesh
from jax.sharding import PartitionSpec as P

HEAD_DIM = 64
LENGTH = 1024
EPS = 1e-05
BLOCK = 256
ROWS = 512
BF = jnp.bfloat16
F32 = jnp.float32
MEGABYTE = 1024 * 1024


def swap(value, axis, bit):
    size = lax.axis_size(axis)
    return lax.ppermute(value, axis, [(i, i ^ bit) for i in range(size)])


def nt_dot(left, right):
    return lax.dot_general(left, right, (((1,), (1,)), ((), ())), preferred_element_type=F32)


def tn_dot(left, right):
    return lax.dot_general(left, right, (((0,), (0,)), ((), ())), preferred_element_type=F32)


def nn_dot(left, right):
    return jnp.dot(left, right, preferred_element_type=F32)


def attend_pair(p_ref, pair, width):
    q = p_ref[:, pl.ds(pair, 128)] * BF(HEAD_DIM**-0.5)
    k = p_ref[:, pl.ds(width + pair, 128)]
    v = p_ref[:, pl.ds(2 * width + pair, 128)]
    lane = lax.broadcasted_iota(jnp.int32, (LENGTH, 128), 1)
    low_lane = lax.broadcasted_iota(jnp.int32, (BLOCK, 128), 1) < HEAD_DIM
    causal = lax.broadcasted_iota(jnp.int32, (BLOCK, BLOCK), 0) >= lax.broadcasted_iota(
        jnp.int32, (BLOCK, BLOCK), 1
    )
    for start in range(0, LENGTH, BLOCK):
        stop = start + BLOCK
        halves = []
        logs = []
        for head in range(2):
            mine = (lane < HEAD_DIM) if head == 0 else (lane >= HEAD_DIM)
            q_part = jnp.where(mine[start:stop], q[start:stop], BF(0))
            v_part = jnp.where(mine[:stop], v[:stop], BF(1))
            scores = nt_dot(q_part, k[:stop])
            last = jnp.where(causal, scores[:, start:], -1e30)
            scores = jnp.concatenate([scores[:, :start], last], 1) if start else last
            top = jnp.max(scores, 1, keepdims=True)
            weights = jnp.exp(scores - top).astype(BF)
            result = nn_dot(weights, v_part)
            total = pltpu.roll(result, HEAD_DIM, 1)
            halves.append(result / total)
            logs.append(top + jnp.log(total))
        yield (
            start,
            jnp.where(low_lane, halves[0], halves[1]).astype(BF),
            jnp.where(low_lane, logs[0], logs[1]),
        )


def attend_first_kernel(p_ref, c_ref, l_ref):
    for start, context, logs in attend_pair(p_ref, 0, p_ref.shape[1] // 3):
        c_ref[start : start + BLOCK] = context
        l_ref[start : start + BLOCK] = logs


def attend_rest_kernel(p_ref, first_ref, first_log_ref, c_ref, l_ref):
    width = c_ref.shape[1]
    pair = pl.multiple_of((pl.program_id(0) + 1) * 128, 128)
    for start, context, logs in attend_pair(p_ref, pair, width):
        c_ref[start : start + BLOCK, pl.ds(pair, 128)] = context
        l_ref[start : start + BLOCK, pl.ds(pair, 128)] = logs

    @pl.when(pl.program_id(0) == 0)
    def _():
        c_ref[:, :128] = first_ref[...]
        l_ref[:, :128] = first_log_ref[...]


def attend_first(projected):
    return pl.pallas_call(
        attend_first_kernel,
        out_shape=(
            jax.ShapeDtypeStruct((LENGTH, 128), BF),
            jax.ShapeDtypeStruct((LENGTH, 128), F32),
        ),
        in_specs=[pl.BlockSpec(memory_space=pltpu.VMEM)],
        out_specs=(pl.BlockSpec(memory_space=pltpu.VMEM),) * 2,
        compiler_params=params(12),
        cost_estimate=cost(),
        name="attend_first",
    )(projected)


def attend_rest(projected, first, first_log):
    width = projected.shape[1] // 3
    pairs = width // 128 - 1
    return pl.pallas_call(
        attend_rest_kernel,
        out_shape=(
            jax.ShapeDtypeStruct((LENGTH, width), BF),
            jax.ShapeDtypeStruct((LENGTH, width), F32),
        ),
        grid=(pairs,),
        in_specs=[
            pl.BlockSpec((LENGTH, 3 * width), lambda i: (0, 0)),
            pl.BlockSpec((LENGTH, 128), lambda i: (0, 0)),
            pl.BlockSpec((LENGTH, 128), lambda i: (0, 0)),
        ],
        out_specs=(pl.BlockSpec((LENGTH, width), lambda i: (0, 0)),) * 2,
        compiler_params=params(16),
        cost_estimate=cost(),
        name="attend_rest",
    )(projected, first, first_log)


def attend_back_pair(p_ref, g_ref, c_ref, l_ref, pair, dk_ref, dv_ref, dq_ref):
    width = g_ref.shape[1]
    q = p_ref[:, pair : pair + 128] * BF(HEAD_DIM**-0.5)
    k = p_ref[:, width + pair : width + pair + 128]
    v = p_ref[:, 2 * width + pair : 2 * width + pair + 128]
    g = g_ref[:, pair : pair + 128]
    low_lane = lax.broadcasted_iota(jnp.int32, (BLOCK, 128), 1) < HEAD_DIM
    causal = lax.broadcasted_iota(jnp.int32, (BLOCK, BLOCK), 0) <= lax.broadcasted_iota(
        jnp.int32, (BLOCK, BLOCK), 1
    )
    dk_ref[...] = jnp.zeros_like(dk_ref)
    dv_ref[...] = jnp.zeros_like(dv_ref)
    for start in range(0, LENGTH, BLOCK):
        stop = start + BLOCK
        logs = l_ref[start:stop, pair : pair + 128].T
        context = c_ref[start:stop, pair : pair + 128].astype(F32)
        product = (g[start:stop].astype(F32) * context).T
        query_grads = []
        for head in range(2):
            mine = low_lane if head == 0 else jnp.logical_not(low_lane)
            row = head * HEAD_DIM
            q_part = jnp.where(mine, q[start:stop], BF(0))
            g_part = jnp.where(mine, g[start:stop], BF(0))
            delta = jnp.sum(product[row : row + HEAD_DIM], 0, keepdims=True)
            scores = nt_dot(k[:stop], q_part)
            last = jnp.where(causal, scores[start:], -1e30)
            scores = jnp.concatenate([scores[:start], last], 0) if start else last
            probs = jnp.exp(scores - logs[row : row + 1])
            prob_grad = nt_dot(v[:stop], g_part)
            score_grad = (probs * (prob_grad - delta)).astype(BF)
            dv_ref[:stop] += nn_dot(probs.astype(BF), g_part)
            dk_ref[:stop] += nn_dot(score_grad, q_part)
            query_grads.append(tn_dot(score_grad, k[:stop]))
        dq_ref[start:stop] = jnp.where(low_lane, query_grads[0], query_grads[1]) * HEAD_DIM**-0.5
    return [ref[...].astype(BF) for ref in (dq_ref, dk_ref, dv_ref)]


def column_sums(values):
    return nn_dot(jnp.ones((8, values.shape[0]), BF), values)


def attend_back_part_kernel(pair, p_ref, g_ref, c_ref, l_ref, d_ref, dk_ref, dv_ref, dq_ref):
    results = attend_back_pair(p_ref, g_ref, c_ref, l_ref, pair * 128, dk_ref, dv_ref, dq_ref)
    for position, result in enumerate(results):
        d_ref[:, position * 128 : (position + 1) * 128] = result


def attend_back_last_kernel(p_ref, g_ref, c_ref, l_ref, *refs):
    parts, (d_ref, bias_ref, dk_ref, dv_ref, dq_ref) = refs[:-5], refs[-5:]
    width = g_ref.shape[1]
    results = attend_back_pair(
        p_ref, g_ref, c_ref, l_ref, len(parts) * 128, dk_ref, dv_ref, dq_ref
    )
    pieces = [[ref[:, i * 128 : (i + 1) * 128] for i in range(3)] for ref in parts]
    for pair, piece in enumerate(pieces + [results]):
        for position, result in enumerate(piece):
            columns = slice(position * width + pair * 128, position * width + pair * 128 + 128)
            d_ref[:, columns] = result
            bias_ref[:, columns] = column_sums(result)


def attend_back_part(projected, ctx_grad, context, logs, pair):
    return pl.pallas_call(
        functools.partial(attend_back_part_kernel, pair),
        out_shape=jax.ShapeDtypeStruct((LENGTH, 384), BF),
        in_specs=[pl.BlockSpec(memory_space=pltpu.VMEM)] * 4,
        out_specs=pl.BlockSpec(memory_space=pltpu.VMEM),
        scratch_shapes=[pltpu.VMEM((LENGTH, 128), F32)] * 3,
        compiler_params=params(14),
        cost_estimate=cost(),
        name="attend_back_part",
    )(projected, ctx_grad, context, logs)


def attend_back_last(projected, ctx_grad, context, logs, parts):
    width = projected.shape[1]
    return pl.pallas_call(
        attend_back_last_kernel,
        out_shape=(
            jax.ShapeDtypeStruct((LENGTH, width), BF),
            jax.ShapeDtypeStruct((8, width), F32),
        ),
        in_specs=[pl.BlockSpec(memory_space=pltpu.VMEM)] * (4 + len(parts)),
        out_specs=(pl.BlockSpec(memory_space=pltpu.VMEM),) * 2,
        scratch_shapes=[pltpu.VMEM((LENGTH, 128), F32)] * 3,
        compiler_params=params(18),
        cost_estimate=cost(),
        name="attend_back_last",
    )(projected, ctx_grad, context, logs, *parts)


def row_sums(values):
    return jnp.sum(values.reshape(values.shape[0] // 8, 8, values.shape[1]), 0)


def vmem_specs(count):
    return [pl.BlockSpec(memory_space=pltpu.VMEM)] * count


def hbm_specs(count):
    return [pl.BlockSpec(memory_space=pltpu.HBM)] * count


def fetch(pairs, sems):
    copies = [
        pltpu.make_async_copy(source, target, sems.at[i]) for i, (source, target) in enumerate(pairs)
    ]
    for copy in copies:
        copy.start()
    for copy in copies:
        copy.wait()


def smem_spec():
    return pl.BlockSpec(memory_space=pltpu.SMEM)


def params(megabytes):
    return pltpu.CompilerParams(vmem_limit_bytes=megabytes * MEGABYTE)


def cost():
    return pl.CostEstimate(flops=0, bytes_accessed=0, transcendentals=0)


def place_kernel(dp_ref, h1_ref, h2_ref, h1y_ref, h2x_ref, w_ref, sems):
    dp = dp_ref[0]
    pairs = []
    for low in range(2):
        for x in range(2):
            pairs.append((h1_ref.at[x * 2 + low], w_ref.at[0, dp ^ (low * 2 + x)]))
            pairs.append((h1y_ref.at[x * 2 + low], w_ref.at[1, dp ^ (low * 2 + x)]))
        for row in range(2):
            pairs.append((h2_ref.at[row * 2 + low], w_ref.at[row, dp ^ (4 + low * 2)]))
            pairs.append((h2x_ref.at[row * 2 + low], w_ref.at[row, dp ^ (4 + low * 2 + 1)]))
    fetch(pairs, sems)


def place_blocks(pieces, dp):
    if len(pieces) == 2:
        return jnp.stack(pieces)
    rows, columns = pieces[0].shape[1:]
    placed = pl.pallas_call(
        place_kernel,
        out_shape=jax.ShapeDtypeStruct((2, 8, rows, columns), BF),
        in_specs=[smem_spec()] + hbm_specs(4),
        out_specs=pl.BlockSpec(memory_space=pltpu.VMEM),
        scratch_shapes=[pltpu.SemaphoreType.DMA((16,))],
        compiler_params=params(6),
        cost_estimate=cost(),
        name="place",
    )(dp, *pieces)
    return placed.reshape(2, 8 * rows, columns)


def place_one_kernel(dp_ref, a_ref, b_ref, ay_ref, bx_ref, proj_ref, ctx_ref, *scratch):
    dp = dp_ref[0]
    *staged, sems = scratch
    fetch(list(zip((a_ref, b_ref, ay_ref, bx_ref), staged)), sems)
    h1_ref, h2_ref, h1y_ref, h2x_ref = staged
    block = h1_ref.shape[2] // 4

    def put(index, own, other):
        for kind in range(4):
            columns = slice(kind * block, (kind + 1) * block)
            both = jnp.concatenate([own[:, columns], other[:, columns]], 1)
            if kind < 3:
                proj_ref[dp ^ index, :, kind * 2 * block : (kind + 1) * 2 * block] = both
            else:
                ctx_ref[dp ^ index] = both

    for low in range(2):
        for x in range(2):
            put(low * 2 + x, h1_ref[x * 2 + low], h1y_ref[x * 2 + low])
        put(4 + low * 2, h2_ref[low], h2_ref[2 + low])
        put(4 + low * 2 + 1, h2x_ref[low], h2x_ref[2 + low])


def place_one(pieces, dp):
    if len(pieces) == 2:
        width = pieces[0].shape[0]
        cut = jnp.stack([piece.reshape(width, 4, -1) for piece in pieces], 2)
        return cut[:, :3].reshape(width, -1), cut[:, 3].reshape(width, -1)
    rows, columns = pieces[0].shape[1:]
    proj, ctx = pl.pallas_call(
        place_one_kernel,
        out_shape=(
            jax.ShapeDtypeStruct((8, rows, columns * 3 // 2), BF),
            jax.ShapeDtypeStruct((8, rows, columns // 2), BF),
        ),
        in_specs=[smem_spec()] + hbm_specs(4),
        out_specs=tuple(vmem_specs(2)),
        scratch_shapes=[pltpu.VMEM(pieces[0].shape, BF)] * 4 + [pltpu.SemaphoreType.DMA((4,))],
        compiler_params=params(8),
        cost_estimate=cost(),
        name="place_one",
    )(dp, *pieces)
    return proj.reshape(8 * rows, -1), ctx.reshape(8 * rows, -1)


def direct(shard):
    return lax.axis_size("dp") == 8 and shard.shape[0] % 16 == 0


def gather_z(shard):
    return swap(shard, "dp", 2), swap(shard, "dp", 4), swap(shard, "dp", 6)


def pair_up(shard, r1, r2, r3):
    return jnp.stack([shard, r1]), jnp.stack([r2, r3])


def gather_xy1(h1, h2):
    return swap(h1, "dp", 1), swap(h2, "y", 1)


def gather_xy2(h1, h2, h1x, h2y):
    h1 = jnp.concatenate([h1, h1x])
    h2 = jnp.concatenate([h2, h2y])
    return h1, h2, swap(h1, "y", 1), swap(h2, "dp", 1)


def gather_plain(shard):
    own = lax.all_gather(shard, "dp", axis=0, tiled=True)
    return own, swap(own, "y", 1)


def spread_put(dp, outs, result, row, columns=slice(None)):
    k1, s1, k2, s2, stage = outs
    rows = k1.shape[1]
    for index in range(8):
        stage[index] = result[index * rows : (index + 1) * rows].astype(BF)
    first = s1 if row else k1
    for low in range(2):
        for x in range(2):
            first[x * 2 + low, :, columns] = stage[dp ^ (low * 2 + x)]
        k2[row * 2 + low, :, columns] = stage[dp ^ (4 + low * 2)]
        s2[row * 2 + low, :, columns] = stage[dp ^ (4 + low * 2 + 1)]


def wgrad_kernel(dp_ref, left_ref, right_ref, k1, s1, k2, s2, stage):
    for row in range(2):

        @pl.when(pl.program_id(0) == row)
        def _():
            result = tn_dot(left_ref[...], right_ref[0])
            spread_put(dp_ref[0], (k1, s1, k2, s2, stage), result, row)


def wgrad(left, right, dp):
    width = left.shape[1]
    columns = right.shape[2]
    count = lax.axis_size("dp")
    if count != 8 or (width // count) % 16:
        return jnp.einsum("rd,yre->yde", left, right, preferred_element_type=F32).astype(BF)
    part = jax.ShapeDtypeStruct((4, width // 8, columns), BF)
    return pl.pallas_call(
        wgrad_kernel,
        out_shape=(part,) * 4,
        grid=(2,),
        in_specs=[
            smem_spec(),
            pl.BlockSpec((LENGTH, width), lambda i: (0, 0)),
            pl.BlockSpec((1, LENGTH, columns), lambda i: (i, 0, 0)),
        ],
        out_specs=(pl.BlockSpec(part.shape, lambda i: (0, 0, 0)),) * 4,
        scratch_shapes=[pltpu.VMEM((8, width // 8, columns), BF)],
        compiler_params=params(16),
        cost_estimate=cost(),
        name="wgrad",
    )(dp, left, right)


def wgrad_one_kernel(dp_ref, n_ref, d_ref, g_ref, c_ref, k1, s1, k2, s2, stage):
    block = c_ref.shape[1] // 2
    for kind in range(4):

        @pl.when(pl.program_id(0) == kind)
        def _():
            left, right = (n_ref, d_ref) if kind < 3 else (g_ref, c_ref)
            result = tn_dot(left[...], right[...])
            for row in range(2):
                spread_put(
                    dp_ref[0],
                    (k1, s1, k2, s2, stage),
                    result[:, row * block : (row + 1) * block],
                    row,
                    slice(kind * block, (kind + 1) * block),
                )


def wgrad_one(normed, proj_grad, branch_grad, context, dp):
    width = normed.shape[1]
    block = context.shape[1] // 2
    count = lax.axis_size("dp")
    if count != 8 or (width // count) % 16:
        proj = tn_dot(normed, proj_grad).reshape(width, 3, 2, block)
        out = tn_dot(branch_grad, context).reshape(width, 1, 2, block)
        both = jnp.concatenate([proj, out], 1).transpose(2, 0, 1, 3)
        return both.reshape(2, width, 4 * block).astype(BF)
    part = jax.ShapeDtypeStruct((4, width // 8, 4 * block), BF)
    return pl.pallas_call(
        wgrad_one_kernel,
        out_shape=(part,) * 4,
        grid=(4,),
        in_specs=[
            smem_spec(),
            pl.BlockSpec((LENGTH, width), lambda i: (0, 0)),
            pl.BlockSpec((LENGTH, 2 * block), lambda i: (0, jnp.minimum(i, 2))),
            pl.BlockSpec((LENGTH, width), lambda i: (0, 0)),
            pl.BlockSpec((LENGTH, 2 * block), lambda i: (0, 0)),
        ],
        out_specs=(pl.BlockSpec(part.shape, lambda i: (0, 0, 0)),) * 4,
        scratch_shapes=[pltpu.VMEM((8, width // 8, block), BF)],
        compiler_params=params(18),
        cost_estimate=cost(),
        name="wgrad_one",
    )(dp, normed, proj_grad, branch_grad, context)


def add_kernel(k1, t1, k2, t2, first, second, stage, sems):
    fetch([(ref.at[pl.ds(2, 2)], stage.at[i]) for i, ref in enumerate((k1, t1, k2, t2))], sems)
    first[...] = (stage[0].astype(F32) + stage[1].astype(F32)).astype(BF)
    second[...] = (stage[2].astype(F32) + stage[3].astype(F32)).astype(BF)


def sum_kernel(u1, u2, k1, t1, k2, t2, v, z1, z2, z3, stage, sems):
    parts = (u1, k1, t1, u2, k2, t2)
    fetch([(ref.at[pl.ds(0, 2)], stage.at[i]) for i, ref in enumerate(parts)], sems)

    def total(at, index):
        return sum(stage[at + i, index].astype(F32) for i in range(3))

    v[...] = total(0, 0)
    z1[...] = total(0, 1).astype(BF)
    z2[...] = total(3, 0).astype(BF)
    z3[...] = total(3, 1).astype(BF)


def scatter_xy1(parts):
    k1, s1, k2, s2 = parts
    return k1, swap(s1, "y", 1), k2, swap(s2, "dp", 1)


def scatter_xy2(item):
    _, rows, columns = item[0].shape
    half = jax.ShapeDtypeStruct((2, rows, columns), BF)
    first, second = pl.pallas_call(
        add_kernel,
        out_shape=(half, half),
        in_specs=hbm_specs(4),
        out_specs=tuple(vmem_specs(2)),
        scratch_shapes=[pltpu.VMEM((4, 2, rows, columns), BF), pltpu.SemaphoreType.DMA((4,))],
        compiler_params=params(4),
        cost_estimate=cost(),
        name="add_pairs",
    )(*item)
    return swap(first, "dp", 1), swap(second, "y", 1)


def scatter_z(sent, item):
    _, rows, columns = sent[0].shape
    low = jax.ShapeDtypeStruct((rows, columns), BF)
    v, z1, z2, z3 = pl.pallas_call(
        sum_kernel,
        out_shape=(jax.ShapeDtypeStruct((rows, columns), F32), low, low, low),
        in_specs=hbm_specs(6),
        out_specs=tuple(vmem_specs(4)),
        scratch_shapes=[pltpu.VMEM((6, 2, rows, columns), BF), pltpu.SemaphoreType.DMA((6,))],
        compiler_params=params(4),
        cost_estimate=cost(),
        name="sum_pairs",
    )(*sent, *item)
    return v, swap(z1, "dp", 2), swap(z2, "dp", 4), swap(z3, "dp", 6)


def last_sum_kernel(
    dp_ref, s_ref, u1, u2, k1, t1, k2, t2, v, own, z1, z2, z3, stage, blocks, sems
):
    dp = dp_ref[0]
    rows, columns = v.shape
    sum_kernel(u1, u2, k1, t1, k2, t2, v, *(ref.at[pl.ds(0, rows)] for ref in (z1, z2, z3)), stage, sems)
    piece = s_ref.shape[1] // 8
    for d in range(8):
        here = slice(d * piece, (d + 1) * piece)
        blocks[d, 0:8] = s_ref[0:8, here]
        blocks[d, 12:16] = s_ref[12:16, here]
        for j in range(4):
            at = d % 2 * 4 * piece + j * piece
            blocks[d, 8 + j : 9 + j] = s_ref[8 + d // 2 : 9 + d // 2, at : at + piece]
    own[...] = blocks[dp]
    for ref, bit in ((z1, 2), (z2, 4), (z3, 6)):
        value = blocks[dp ^ bit]
        high = value.astype(BF)
        ref[rows:, :] = jnp.zeros((16, columns), BF)
        ref[rows:, 0:piece] = high
        ref[rows:, 128 : 128 + piece] = (value - high.astype(F32)).astype(BF)


def scatter_last(sent, item, sums, dp):
    _, rows, columns = sent[0].shape
    low = jax.ShapeDtypeStruct((rows + 16, columns), BF)
    piece = sums.shape[1] // 8
    v, own, z1, z2, z3 = pl.pallas_call(
        last_sum_kernel,
        out_shape=(
            jax.ShapeDtypeStruct((rows, columns), F32),
            jax.ShapeDtypeStruct((16, piece), F32),
            low,
            low,
            low,
        ),
        in_specs=[smem_spec()] + vmem_specs(1) + hbm_specs(6),
        out_specs=tuple(vmem_specs(5)),
        scratch_shapes=[
            pltpu.VMEM((6, 2, rows, columns), BF),
            pltpu.VMEM((8, 16, piece), F32),
            pltpu.SemaphoreType.DMA((6,)),
        ],
        compiler_params=params(5),
        cost_estimate=cost(),
        name="sum_last",
    )(dp, sums, *sent, *item)
    return v, own, swap(z1, "dp", 2), swap(z2, "dp", 4), swap(z3, "dp", 6)


def end_kernel(v, r1, r2, r3, out, first, rest, sems):
    fetch([(v, first)] + [(ref, rest.at[i]) for i, ref in enumerate((r1, r2, r3))], sems)
    total = first[...] + sum(rest[i].astype(F32) for i in range(3))
    out[...] = total if out.shape == total.shape else total.T


def scatter_end(parts, shape):
    rows, columns = parts[0].shape
    return pl.pallas_call(
        end_kernel,
        out_shape=jax.ShapeDtypeStruct(shape, F32),
        in_specs=hbm_specs(4),
        out_specs=vmem_specs(1)[0],
        scratch_shapes=[
            pltpu.VMEM((rows, columns), F32),
            pltpu.VMEM((3, rows, columns), BF),
            pltpu.SemaphoreType.DMA((4,)),
        ],
        compiler_params=params(4),
        cost_estimate=cost(),
        name="scatter_end",
    )(*parts)


def end_last_kernel(v, own, r1, r2, r3, qkv, out, small, first, rest, sems):
    fetch([(v, first)] + [(ref, rest.at[i]) for i, ref in enumerate((r1, r2, r3))], sems)
    rows = first.shape[0]
    total = first[...] + sum(rest[i, :rows].astype(F32) for i in range(3))
    block, piece = qkv.shape[2], own.shape[1]
    for kind in range(3):
        qkv[kind] = total[:, kind * block : (kind + 1) * block]
    out[...] = total[:, 3 * block :].T
    sums = own[...]
    for i in range(3):
        sums = sums + rest[i, rows:, 0:piece].astype(F32)
        sums = sums + rest[i, rows:, 128 : 128 + piece].astype(F32)
    small[...] = sums


def scatter_end_last(parts, qkv_shape, out_shape):
    rows, columns = parts[0].shape
    return pl.pallas_call(
        end_last_kernel,
        out_shape=tuple(
            jax.ShapeDtypeStruct(shape, F32) for shape in (qkv_shape, out_shape, parts[1].shape)
        ),
        in_specs=hbm_specs(1) + vmem_specs(1) + hbm_specs(3),
        out_specs=tuple(vmem_specs(3)),
        scratch_shapes=[
            pltpu.VMEM((rows, columns), F32),
            pltpu.VMEM((3, rows + 16, columns), BF),
            pltpu.SemaphoreType.DMA((4,)),
        ],
        compiler_params=params(5),
        cost_estimate=cost(),
        name="scatter_end_last",
    )(*parts)


def scatter_plain(grad):
    both = grad[0].astype(F32) + swap(grad[1], "y", 1).astype(F32)
    return lax.psum_scatter(both, "dp", scatter_dimension=0, tiled=True)


def norm_parts(values):
    center = values - jnp.mean(values, -1, keepdims=True)
    spread = jnp.mean(center * center, -1, keepdims=True)
    scale = lax.rsqrt(spread + EPS)
    return center * scale, scale


def norm_back(xhat, scale, gain, grad):
    scaled = grad * gain
    first = jnp.mean(scaled, -1, keepdims=True)
    second = jnp.mean(scaled * xhat, -1, keepdims=True)
    return scale * (scaled - first - xhat * second)


def rows_spec(columns, lead=None):
    if lead is None:
        return pl.BlockSpec((ROWS, columns), lambda i, c: (i, 0))
    return pl.BlockSpec((lead, ROWS, columns), lambda i, c: (0, i, 0))


def whole_spec(shape):
    return pl.BlockSpec(shape, lambda i, c: (0,) * len(shape))


def half_spec(columns, mine):
    per_core = LENGTH // 2 // ROWS

    def index(i, c):
        inside = i // per_core == (c[0] if mine else 1 - c[0])
        return (jnp.where(inside, i % per_core, 0), 0)

    return pl.BlockSpec((ROWS, columns), index)


def pick_half(first_ref, second_ref):
    second = pl.program_id(0).astype(F32)
    return first_ref[...].astype(F32) * (1.0 - second) + second_ref[...].astype(F32) * second


def pick_rows(core_ref, own_ref, other_ref):
    per_core = LENGTH // 2 // ROWS
    mine = (pl.program_id(0) // per_core == core_ref[0]).astype(F32)
    return own_ref[...].astype(F32) * mine + other_ref[...].astype(F32) * (1.0 - mine)


def block_call(kernel, name, outs, specs, grid, megabytes):
    return pl.pallas_call(
        kernel,
        out_shape=tuple(shape for shape, _ in outs),
        grid_spec=pltpu.PrefetchScalarGridSpec(
            num_scalar_prefetch=1,
            grid=(grid,),
            in_specs=specs,
            out_specs=tuple(spec for _, spec in outs),
        ),
        compiler_params=params(megabytes),
        cost_estimate=cost(),
        name=name,
    )


def prepare_kernel(
    core_ref, own_ref, other_ref, cot_ref, cot_other_ref, gain_ref, shift_ref, n_ref, c_ref, s_ref
):
    cot = pick_rows(core_ref, cot_ref, cot_other_ref)
    c_ref[...] = cot.astype(BF)
    sums = row_sums(cot)

    @pl.when(pl.program_id(0) == 0)
    def _():
        s_ref[...] = sums

    @pl.when(pl.program_id(0) > 0)
    def _():
        s_ref[...] += sums

    xhat, _ = norm_parts(pick_rows(core_ref, own_ref, other_ref))
    n_ref[...] = (xhat * gain_ref[...] + shift_ref[...]).astype(BF)


def prepare(core, own, other, cot, cot_other, gain, shift):
    width = own.shape[1]
    rows = (jax.ShapeDtypeStruct((LENGTH, width), BF), rows_spec(width))
    return block_call(
        prepare_kernel,
        "prepare",
        [rows, rows, (jax.ShapeDtypeStruct((8, width), F32), whole_spec((8, width)))],
        [
            half_spec(width, True),
            half_spec(width, False),
            half_spec(width, True),
            half_spec(width, False),
            whole_spec((1, width)),
            whole_spec((1, width)),
        ],
        LENGTH // ROWS,
        16,
    )(core, own, other, cot, cot_other, gain, shift)


def project_kernel(core_ref, n_ref, w_ref, b_ref, p_ref):
    p_ref[...] = (nn_dot(n_ref[...], w_ref[...]) + b_ref[...]).astype(BF)


def project(core, normed, weight, bias):
    width, columns = weight.shape
    return block_call(
        project_kernel,
        "project",
        [(jax.ShapeDtypeStruct((LENGTH, columns), BF), rows_spec(columns))],
        [rows_spec(width), whole_spec((width, columns)), whole_spec((1, columns))],
        LENGTH // ROWS,
        14,
    )(core, normed, weight, bias)[0]


def middle_kernel(
    core_ref, own_ref, other_ref, part_ref, first_ref, second_ref, ob_ref, gain_ref, shift_ref,
    h_ref, n_ref,
):
    attended = part_ref[...].astype(F32) + pick_half(first_ref, second_ref)
    hidden = pick_rows(core_ref, own_ref, other_ref) + attended + ob_ref[...]
    h_ref[...] = hidden
    xhat, _ = norm_parts(hidden)
    n_ref[...] = (xhat * gain_ref[...] + shift_ref[...]).astype(BF)


def middle(core, own, other, part, part_other, out_bias, gain, shift):
    width = own.shape[1]
    return block_call(
        middle_kernel,
        "middle",
        [
            (jax.ShapeDtypeStruct((LENGTH, width), F32), rows_spec(width)),
            (jax.ShapeDtypeStruct((LENGTH, width), BF), rows_spec(width)),
        ],
        [half_spec(width, True), half_spec(width, False), rows_spec(width)]
        + [whole_spec((ROWS, width))] * 2
        + [whole_spec((1, width))] * 3,
        LENGTH // ROWS,
        16,
    )(core, own, other, part, *part_other, out_bias, gain, shift)


def up_kernel(core_ref, n_ref, w_ref, b_ref, a_ref, d_ref):
    slope = 0.7978845608028654
    for row in range(2):
        up = nn_dot(n_ref[...], w_ref[row]) + b_ref[row]
        square = up * up
        gate = 1.0 / (1.0 + jnp.exp(up * (-2.0 * slope - 2.0 * slope * 0.044715 * square)))
        gated = up * gate
        a_ref[row] = gated.astype(BF)
        inner = 2.0 * slope + 6.0 * slope * 0.044715 * square
        d_ref[row] = (gate + (gated - gated * gate) * inner).astype(BF)


def up_project(core, normed, weight, bias):
    width, columns = weight.shape[1:]
    both = (jax.ShapeDtypeStruct((2, LENGTH, columns), BF), rows_spec(columns, 2))
    return block_call(
        up_kernel,
        "up_project",
        [both, both],
        [rows_spec(width), whole_spec((2, width, columns)), whole_spec((2, 1, columns))],
        LENGTH // ROWS,
        20,
    )(core, normed, weight, bias[:, None])


def up_back_kernel(core_ref, cot_ref, d_ref, down_ref, up_ref, u_ref, b_ref, n_ref):
    total = None
    for row in range(2):
        grad = nn_dot(cot_ref[...], down_ref[row]) * d_ref[row].astype(F32)
        low = grad.astype(BF)
        u_ref[row] = low
        sums = row_sums(low.astype(F32))

        @pl.when(pl.program_id(0) == 0)
        def _():
            b_ref[row] = sums

        @pl.when(pl.program_id(0) > 0)
        def _():
            b_ref[row] += sums

        part = nt_dot(low, up_ref[row])
        total = part if total is None else total + part
    n_ref[...] = total.astype(BF)


def up_back(core, cot, slope, down, up):
    width, columns = down.shape[1:]
    return block_call(
        up_back_kernel,
        "up_back",
        [
            (jax.ShapeDtypeStruct((2, LENGTH, columns), BF), rows_spec(columns, 2)),
            (jax.ShapeDtypeStruct((2, 8, columns), F32), whole_spec((2, 8, columns))),
            (jax.ShapeDtypeStruct((LENGTH, width), BF), rows_spec(width)),
        ],
        [
            rows_spec(width),
            rows_spec(columns, 2),
            whole_spec((2, width, columns)),
            whole_spec((2, width, columns)),
        ],
        LENGTH // ROWS,
        24,
    )(core, cot, slope, down, up)


def second_back_kernel(
    core_ref, h_ref, part_ref, first_ref, second_ref, cot_ref, gain_ref, w_ref,
    dh_ref, do_ref, dc_ref, sum_ref,
):
    xhat, scale = norm_parts(h_ref[...])
    grad = part_ref[...].astype(F32) + pick_half(first_ref, second_ref)
    hidden_grad = cot_ref[...].astype(F32) + norm_back(xhat, scale, gain_ref[...], grad)
    low = hidden_grad.astype(BF)

    @pl.when(pl.program_id(0) == core_ref[0])
    def _():
        dh_ref[...] = hidden_grad

    do_ref[...] = low
    dc_ref[...] = nn_dot(low, w_ref[...]).astype(BF)
    sums = (row_sums(low.astype(F32)), row_sums(grad * xhat), row_sums(grad))
    for position, value in enumerate(sums):

        @pl.when(pl.program_id(0) == 0)
        def _():
            sum_ref[position] = value

        @pl.when(pl.program_id(0) > 0)
        def _():
            sum_ref[position] += value


def second_back(core, hidden, part, other, cot, gain, weight):
    width, columns = weight.shape
    return block_call(
        second_back_kernel,
        "second_back",
        [
            (jax.ShapeDtypeStruct((ROWS, width), F32), whole_spec((ROWS, width))),
            (jax.ShapeDtypeStruct((LENGTH, width), BF), rows_spec(width)),
            (jax.ShapeDtypeStruct((LENGTH, columns), BF), rows_spec(columns)),
            (jax.ShapeDtypeStruct((3, 8, width), F32), whole_spec((3, 8, width))),
        ],
        [rows_spec(width)] * 2
        + [whole_spec((ROWS, width))] * 2
        + [rows_spec(width), whole_spec((1, width)), whole_spec((width, columns))],
        LENGTH // ROWS,
        20,
    )(core, hidden, part, *other, cot, gain, weight)


def share(core, left, weight):
    count, _, depth = left.shape
    width = weight.shape[1]
    half = LENGTH // 2

    def kernel(core_ref, left_ref, weight_ref, own_ref, other_ref):
        total = nt_dot(left_ref[0], weight_ref[0])
        for index in range(1, count):
            total = total + nt_dot(left_ref[index], weight_ref[index])

        @pl.when(pl.program_id(0) == 0)
        def _():
            other_ref[...] = total.astype(BF)

        @pl.when(pl.program_id(0) == 1)
        def _():
            own_ref[...] = total

    def rows(i, c):
        return (0, jnp.where(i == 0, 1 - c[0], c[0]), 0)

    return block_call(
        kernel,
        "share",
        [
            (jax.ShapeDtypeStruct((half, width), F32), whole_spec((half, width))),
            (jax.ShapeDtypeStruct((half, width), BF), whole_spec((half, width))),
        ],
        [pl.BlockSpec((count, half, depth), rows), whole_spec(weight.shape)],
        2,
        16,
    )(core, left, weight)


def first_back_kernel(core_ref, x_ref, part_ref, first, second, dh_ref, gain_ref, t_ref, sum_ref):
    xhat, scale = norm_parts(x_ref[...].astype(F32))
    other = jnp.concatenate([first[...], second[...]], 0)
    grad = part_ref[...] + other.astype(F32)
    t_ref[...] = (dh_ref[...] + norm_back(xhat, scale, gain_ref[...], grad)).astype(BF)
    for position, value in enumerate((row_sums(grad * xhat), row_sums(grad))):

        @pl.when(pl.program_id(0) == 0)
        def _():
            sum_ref[position] = value

        @pl.when(pl.program_id(0) > 0)
        def _():
            sum_ref[position] += value


def first_back(core, own, part, other, hidden_grad, gain):
    width = own.shape[1]
    return block_call(
        first_back_kernel,
        "first_back",
        [
            (jax.ShapeDtypeStruct((LENGTH // 2, width), BF), rows_spec(width)),
            (jax.ShapeDtypeStruct((2, 8, width), F32), whole_spec((2, 8, width))),
        ],
        [rows_spec(width)] * 2
        + [whole_spec((ROWS // 2, width))] * 2
        + [rows_spec(width), whole_spec((1, width))],
        1,
        16,
    )(core, own, part, *other, hidden_grad, gain)


def unpack_kernel(place_ref, v_ref, g1, s1, qkv, ob, g2, s2, up, down, full):
    y, core = place_ref[0], place_ref[1]
    piece = g1.shape[1] // 8
    for d in range(8):
        rows = v_ref[d : d + 1]
        here = slice(d * piece, (d + 1) * piece)
        for ref, position in ((g1, 0), (s1, 1), (ob, 5), (g2, 6), (s2, 7), (down, 12)):
            ref[:, here] = rows[:, position * piece : (position + 1) * piece]
        for kind in range(3):
            full[kind : kind + 1, here] = rows[:, (2 + kind) * piece : (3 + kind) * piece]
        cut = slice(d % 2 * 4 * piece, (d % 2 + 1) * 4 * piece)
        full[3 + d // 2 : 4 + d // 2, cut] = rows[:, 8 * piece : 12 * piece]
    block = 2 * piece
    for kind in range(3):
        for y_index in range(2):
            cuts = []
            for core_index in range(2):
                at = (2 * y_index + core_index) * block
                cuts.append(full[kind : kind + 1, at : at + block])
            value = jnp.where(core == 0, cuts[0], cuts[1])
            for own in range(2):

                @pl.when((y ^ y_index) == own)
                def _():
                    at = (2 * kind + own) * block
                    qkv[:, at : at + block] = value

    for y_index in range(2):
        rows = [full[3 + 2 * y_index + i : 4 + 2 * y_index + i] for i in range(2)]
        value = jnp.where(core == 0, rows[0], rows[1])
        for own in range(2):

            @pl.when((y ^ y_index) == own)
            def _():
                up[own : own + 1] = value


def unpack(place, vectors, width):
    row = jax.ShapeDtypeStruct((1, width), F32)
    wide = jax.ShapeDtypeStruct((1, 3 * width // 2), F32)
    return pl.pallas_call(
        unpack_kernel,
        out_shape=(row, row, wide, row, row, row, jax.ShapeDtypeStruct((2, width), F32), row),
        in_specs=[smem_spec()] + vmem_specs(1),
        out_specs=tuple(vmem_specs(8)),
        scratch_shapes=[pltpu.VMEM((8, width), F32)],
        compiler_params=params(2),
        cost_estimate=cost(),
        name="unpack",
    )(place, vectors)


def pack_kernel(place_ref, first_ref, qkv_ref, second_ref, up_ref, cot_ref, full):
    y, core = place_ref[0], place_ref[1]
    width = full.shape[1]
    block = width // 4

    def column_sum(values):
        return jnp.sum(values, 0, keepdims=True)

    full[0:1] = column_sum(first_ref[0])
    full[1:2] = column_sum(first_ref[1])
    for position, index in ((5, 0), (6, 1), (7, 2)):
        full[position : position + 1] = 0.5 * column_sum(second_ref[index])
    full[12:13] = 0.5 * column_sum(cot_ref[...])
    qkv = qkv_ref[0:1]
    ups = [column_sum(up_ref[index]) for index in range(2)]
    for t in range(4):
        keep = (core == t % 2).astype(F32)
        mine = (y == t // 2).astype(F32)
        for kind in range(3):
            at = kind * 2 * block
            value = qkv[:, at : at + block] * mine + qkv[:, at + block : at + 2 * block] * (1.0 - mine)
            full[2 + kind : 3 + kind, t * block : (t + 1) * block] = value * keep
        full[8 + t : 9 + t] = (ups[0] * mine + ups[1] * (1.0 - mine)) * keep
    full[13:16] = jnp.zeros((3, width), F32)


def pack(place, first, qkv, second, up, cot):
    width = cot.shape[1]
    return pl.pallas_call(
        pack_kernel,
        out_shape=jax.ShapeDtypeStruct((16, width), F32),
        in_specs=[smem_spec()] + vmem_specs(5),
        out_specs=pl.BlockSpec(memory_space=pltpu.VMEM),
        compiler_params=params(4),
        cost_estimate=cost(),
        name="pack",
    )(place, first, qkv, second, up, cot)


def body(
    tokens,
    cotangent,
    first_gain,
    first_shift,
    w_qkv,
    qkv_bias,
    w_out,
    out_bias,
    second_gain,
    second_shift,
    w_up,
    up_bias,
    w_down,
    down_bias,
):
    dp_count = lax.axis_size("dp")
    dp = lax.axis_index("dp")
    y = lax.axis_index("y")
    core = lax.axis_index("core")
    dp_ref = dp.reshape(1).astype(jnp.int32)
    own_rows, width = tokens.shape
    piece = first_gain.shape[0]
    heads_own = w_qkv.shape[2]
    ff_own = w_up.shape[1]
    ff_piece = up_bias.shape[0]

    core_ref = core.reshape(1).astype(jnp.int32)
    place_ref = jnp.stack([y, core]).astype(jnp.int32)
    shard_one = jnp.concatenate([w_qkv[0], w_qkv[1], w_qkv[2], w_out.T], 1)
    fast = direct(shard_one)
    tie = lax.optimization_barrier
    tokens_other = swap(tokens, "core", 1)
    vectors = jnp.concatenate(
        [
            first_gain,
            first_shift,
            qkv_bias.reshape(-1),
            out_bias,
            second_gain,
            second_shift,
            up_bias,
            down_bias,
        ]
    )
    vectors = lax.all_to_all(
        jnp.broadcast_to(vectors[None], (dp_count, vectors.shape[0])), "dp", 0, 0, tiled=True
    )

    def own_half(rows):
        return lax.dynamic_slice_in_dim(rows, core * own_rows, own_rows, 0)

    def exchange(rows):
        half = rows.shape[0] // 2
        return [swap(rows[:half], "core", 1), swap(rows[half:], "core", 1)]

    if fast:
        one = gather_z(shard_one)
        shard_one, one, vectors, tokens_other, cotangent, w_up, w_down = tie(
            (shard_one, one, vectors, tokens_other, cotangent, w_up, w_down)
        )
        one = pair_up(shard_one, *one)
        one_xy1 = gather_xy1(*one)
        one, one_xy1, vectors, cotangent, w_up, w_down = tie(
            (one, one_xy1, vectors, cotangent, w_up, w_down)
        )
        one = gather_xy2(*one, *one_xy1)
        up = gather_z(w_up)
        cot_other = swap(cotangent, "core", 1)
        cot_other, vectors, w_down = tie((cot_other, vectors, w_down))
        shard_down = w_down.T
        gain_one, shift_one, qkv_own, out_full, gain_two, shift_two, up_own, down_full = unpack(
            place_ref, vectors, width
        )
    else:
        one, up, down = map(gather_plain, (shard_one, w_up, w_down.T))
        cot_other = swap(cotangent, "core", 1)

        def full(position, count=1):
            return vectors[:, position * piece : (position + count) * piece]

        def own_blocks(values):
            cut = values.reshape(values.shape[0], 2, 2, -1)
            cut = jnp.where(core == 0, cut[:, :, 0], cut[:, :, 1])
            both = [cut[:, 0], cut[:, 1]]
            first = jnp.where(y == 0, both[0], both[1])
            second = jnp.where(y == 0, both[1], both[0])
            return jnp.stack([first, second], 1)

        gain_one, shift_one, out_full, gain_two, shift_two = (
            full(position).reshape(1, -1) for position in (0, 1, 5, 6, 7)
        )
        qkv_full = full(2, 3).reshape(dp_count, 3, piece).transpose(1, 0, 2).reshape(3, width)
        qkv_own = own_blocks(qkv_full).reshape(1, -1)
        up_own = own_blocks(vectors[:, 8 * piece : 8 * piece + ff_piece].reshape(1, -1))[0]
        down_full = vectors[:, 8 * piece + ff_piece :].reshape(1, -1)
    normed_one, cot, cot_sums = prepare(
        core_ref, tokens, tokens_other, cotangent, cot_other, gain_one, shift_one
    )

    if fast:
        one, up, normed_one, cot, qkv_own, shard_down = tie(
            (one, up, normed_one, cot, qkv_own, shard_down)
        )
        up = pair_up(w_up, *up)
        up_xy1 = gather_xy1(*up)
        down = gather_z(shard_down)
    w_proj, w_ctx = place_one(one, dp_ref)
    projected = project(core_ref, normed_one, w_proj, qkv_own)
    context_first = attend_first(projected)
    if fast:
        context_first, up, up_xy1, down = tie((context_first, up, up_xy1, down))
        up = gather_xy2(*up, *up_xy1)
    context, logs = attend_rest(projected, *context_first)
    if fast:
        context, up, down = tie((context, up, down))
        down = pair_up(shard_down, *down)
        down_xy1 = gather_xy1(*down)
    out_part = nt_dot(context, w_ctx).astype(BF)
    out_other = exchange(out_part)

    hidden, normed_two = middle(
        core_ref, tokens, tokens_other, out_part, out_other, out_full, gain_two, shift_two
    )

    if fast:
        normed_two, down, down_xy1 = tie((normed_two, down, down_xy1))
        down = gather_xy2(*down, *down_xy1)
    weight_up = place_blocks(up, dp_ref)
    active, slope = up_project(core_ref, normed_two, weight_up, up_own)
    down_wgrad = wgrad(cot, active, dp_ref)
    if fast:
        down_wgrad, down, slope = tie((down_wgrad, down, slope))
        down_wgrad = scatter_xy1(down_wgrad)
    weight_down = place_blocks(down, dp_ref)
    upward_grad, up_bias_sums, normed_two_part = up_back(
        core_ref, cot, slope, weight_down, weight_up
    )
    up_wgrad = wgrad(normed_two, upward_grad, dp_ref)
    if fast:
        up_wgrad, down_wgrad, normed_two_part = tie((up_wgrad, down_wgrad, normed_two_part))
        up_wgrad = scatter_xy1(up_wgrad)
        down_sent = scatter_xy2(down_wgrad)
    normed_two_other = exchange(normed_two_part)

    hidden_grad, branch_grad, ctx_grad, second_sums = second_back(
        core_ref, hidden, normed_two_part, normed_two_other, cot, gain_two, w_ctx
    )
    parts = [attend_back_part(projected, ctx_grad, context, logs, pair) for pair in range(2)]
    if fast:
        parts, up_wgrad, down_sent, ctx_grad = tie((parts, up_wgrad, down_sent, ctx_grad))
        up_sent = scatter_xy2(up_wgrad)
        down_wgrad = scatter_z(down_sent, down_wgrad)
    proj_grad, qkv_bias_own = attend_back_last(projected, ctx_grad, context, logs, parts)
    one_wgrad = wgrad_one(normed_one, proj_grad, branch_grad, context, dp_ref)
    if fast:
        one_wgrad, proj_grad, up_sent, down_wgrad, active = tie(
            (one_wgrad, proj_grad, up_sent, down_wgrad, active)
        )
        one_wgrad = scatter_xy1(one_wgrad)
        up_wgrad = scatter_z(up_sent, up_wgrad)
    normed_one_part, sent = share(core_ref, proj_grad[None], w_proj[None])
    normed_one_other = exchange(sent)
    if fast:
        normed_one_other, active = tie((normed_one_other, active))
    tokens_grad, first_sums = first_back(
        core_ref, tokens, normed_one_part, normed_one_other, hidden_grad, gain_one
    )

    if fast:
        sums = pack(place_ref, first_sums, qkv_bias_own, second_sums, up_bias_sums, cot_sums)
        sums = sums + swap(sums, "core", 1)
        sums = sums + swap(sums, "y", 1)
    else:

        def spread_blocks(values):
            block = values.shape[-1] // 2
            own, other = values[..., :block], values[..., block:]
            cut = [jnp.where(y == 0, own, other), jnp.where(y == 0, other, own)]
            return jnp.concatenate(
                [jnp.where(core == index, half, 0.0) for half in cut for index in range(2)], -1
            )

        sums = [
            jnp.sum(first_sums, 1),
            spread_blocks(qkv_bias_own[0].reshape(3, 2 * heads_own)),
            0.5 * jnp.sum(second_sums, 1),
            spread_blocks(jnp.sum(up_bias_sums, 1).reshape(1, -1)),
            0.5 * jnp.sum(cot_sums, 0)[None],
        ]
        sums = [
            item.reshape(item.shape[0], dp_count, -1).transpose(1, 0, 2).reshape(dp_count, -1)
            for item in sums
        ]
        sums = jnp.concatenate(sums, 1)
        sums = jnp.broadcast_to(sums[:, None, :], (dp_count, 4, sums.shape[1]))
        sums = sums.reshape(dp_count * 4, -1)
    mlp_part, mlp_sent = share(core_ref, active, weight_down)
    mlp_other = swap(mlp_sent, "core", 1)
    if fast:
        one_wgrad, sums, mlp_other = tie((one_wgrad, sums, mlp_other))
        one_sent = scatter_xy2(one_wgrad)
        sums = sums + swap(sums, "dp", 1)
        up_wgrad = scatter_end(up_wgrad, w_up.shape)
        down_wgrad = scatter_end(down_wgrad, w_down.shape)
    block_out = (own_half(hidden) + mlp_part + mlp_other.astype(F32) + down_full).astype(BF)
    if fast:
        one_sent, sums, block_out, up_wgrad, down_wgrad = tie(
            (one_sent, sums, block_out, up_wgrad, down_wgrad)
        )
        one_wgrad = scatter_last(one_sent, one_wgrad, sums, dp_ref)
        qkv_wgrad, out_wgrad, sums = scatter_end_last(one_wgrad, w_qkv.shape, w_out.shape)
        small = (sums[0], sums[1], sums[2:5], sums[5], sums[6], sums[7], sums[8:12], sums[12])
    else:
        one_wgrad, up_wgrad, down_wgrad = map(scatter_plain, (one_wgrad, up_wgrad, down_wgrad))
        down_wgrad = down_wgrad.T
        qkv_wgrad = one_wgrad[:, : 3 * heads_own].reshape(piece, 3, heads_own).transpose(1, 0, 2)
        out_wgrad = one_wgrad[:, 3 * heads_own :].T
        sums = lax.all_to_all(sums, ("dp", "y", "core"), 0, 0, tiled=True)
        sums = jnp.sum(sums, 0).reshape(-1, piece)
        small = (sums[0], sums[1], sums[2:5], sums[5], sums[6], sums[7], sums[8:12], sums[12])
    vector_grads = small[:6] + (small[6].reshape(-1), small[7])

    return (
        block_out,
        tokens_grad,
        vector_grads[0],
        vector_grads[1],
        qkv_wgrad,
        vector_grads[2],
        out_wgrad,
        vector_grads[3],
        vector_grads[4],
        vector_grads[5],
        up_wgrad,
        vector_grads[6],
        down_wgrad,
        vector_grads[7],
    )


def solution(mesh):
    devices = mesh.devices
    split = Mesh(devices.reshape(devices.shape[0], 2, 2), ("dp", "y", "core"))
    tensor = ("y", "core")
    rows = P(("dp", "y", "core"), None)
    specs = (
        P("dp"),
        P("dp"),
        P(None, "dp", tensor),
        P(None, "dp"),
        P(tensor, "dp"),
        P("dp"),
        P("dp"),
        P("dp"),
        P("dp", tensor),
        P("dp"),
        P(tensor, "dp"),
        P("dp"),
    )
    return jax.shard_map(
        body,
        mesh=split,
        in_specs=(rows, rows) + specs,
        out_specs=(rows, rows) + specs,
        check_vma=False,
    )
```

```python
import functools

import jax
import jax.numpy as jnp
from jax import lax
from jax.experimental import pallas as pl
from jax.experimental.pallas import tpu as pltpu
from jax.sharding import Mesh
from jax.sharding import PartitionSpec as P

HEAD_DIM = 64
LENGTH = 1024
EPS = 1e-05
BLOCK = 256
ROWS = 512
BF = jnp.bfloat16
F32 = jnp.float32
MEGABYTE = 1024 * 1024


def swap(value, axis, bit):
    size = lax.axis_size(axis)
    return lax.ppermute(value, axis, [(i, i ^ bit) for i in range(size)])


def swap_both(value):
    size = lax.axis_size("dp") * 2
    return lax.ppermute(value, ("dp", "y"), [(i, i ^ 3) for i in range(size)])


def nt_dot(left, right):
    return lax.dot_general(left, right, (((1,), (1,)), ((), ())), preferred_element_type=F32)


def tn_dot(left, right):
    return lax.dot_general(left, right, (((0,), (0,)), ((), ())), preferred_element_type=F32)


def nn_dot(left, right):
    return jnp.dot(left, right, preferred_element_type=F32)


def attend_pair(p_ref, pair, width):
    q = p_ref[:, pl.ds(pair, 128)] * BF(HEAD_DIM**-0.5)
    k = p_ref[:, pl.ds(width + pair, 128)]
    v = p_ref[:, pl.ds(2 * width + pair, 128)]
    lane = lax.broadcasted_iota(jnp.int32, (LENGTH, 128), 1)
    low_lane = lax.broadcasted_iota(jnp.int32, (BLOCK, 128), 1) < HEAD_DIM
    causal = lax.broadcasted_iota(jnp.int32, (BLOCK, BLOCK), 0) >= lax.broadcasted_iota(
        jnp.int32, (BLOCK, BLOCK), 1
    )
    for start in range(0, LENGTH, BLOCK):
        stop = start + BLOCK
        halves = []
        logs = []
        for head in range(2):
            mine = (lane < HEAD_DIM) if head == 0 else (lane >= HEAD_DIM)
            q_part = jnp.where(mine[start:stop], q[start:stop], BF(0))
            v_part = jnp.where(mine[:stop], v[:stop], BF(1))
            scores = nt_dot(q_part, k[:stop])
            last = jnp.where(causal, scores[:, start:], -1e30)
            scores = jnp.concatenate([scores[:, :start], last], 1) if start else last
            top = jnp.max(scores, 1, keepdims=True)
            weights = jnp.exp(scores - top).astype(BF)
            result = nn_dot(weights, v_part)
            total = pltpu.roll(result, HEAD_DIM, 1)
            halves.append(result / total)
            logs.append(top + jnp.log(total))
        yield (
            start,
            jnp.where(low_lane, halves[0], halves[1]).astype(BF),
            jnp.where(low_lane, logs[0], logs[1]),
        )


def attend_first_kernel(p_ref, c_ref, l_ref):
    for start, context, logs in attend_pair(p_ref, 0, p_ref.shape[1] // 3):
        c_ref[start : start + BLOCK] = context
        l_ref[start : start + BLOCK] = logs


def attend_rest_kernel(p_ref, first_ref, first_log_ref, c_ref, l_ref):
    width = c_ref.shape[1]
    pair = pl.multiple_of((pl.program_id(0) + 1) * 128, 128)
    for start, context, logs in attend_pair(p_ref, pair, width):
        c_ref[start : start + BLOCK, pl.ds(pair, 128)] = context
        l_ref[start : start + BLOCK, pl.ds(pair, 128)] = logs

    @pl.when(pl.program_id(0) == 0)
    def _():
        c_ref[:, :128] = first_ref[...]
        l_ref[:, :128] = first_log_ref[...]


def attend_first(projected):
    return pl.pallas_call(
        attend_first_kernel,
        out_shape=(
            jax.ShapeDtypeStruct((LENGTH, 128), BF),
            jax.ShapeDtypeStruct((LENGTH, 128), F32),
        ),
        in_specs=[pl.BlockSpec(memory_space=pltpu.VMEM)],
        out_specs=(pl.BlockSpec(memory_space=pltpu.VMEM),) * 2,
        compiler_params=params(12),
        cost_estimate=cost(),
        name="attend_first",
    )(projected)


def attend_rest(projected, first, first_log):
    width = projected.shape[1] // 3
    pairs = width // 128 - 1
    return pl.pallas_call(
        attend_rest_kernel,
        out_shape=(
            jax.ShapeDtypeStruct((LENGTH, width), BF),
            jax.ShapeDtypeStruct((LENGTH, width), F32),
        ),
        grid=(pairs,),
        in_specs=[
            pl.BlockSpec((LENGTH, 3 * width), lambda i: (0, 0)),
            pl.BlockSpec((LENGTH, 128), lambda i: (0, 0)),
            pl.BlockSpec((LENGTH, 128), lambda i: (0, 0)),
        ],
        out_specs=(pl.BlockSpec((LENGTH, width), lambda i: (0, 0)),) * 2,
        compiler_params=params(16),
        cost_estimate=cost(),
        name="attend_rest",
    )(projected, first, first_log)


def attend_back_pair(p_ref, g_ref, c_ref, l_ref, pair, dk_ref, dv_ref, dq_ref):
    width = g_ref.shape[1]
    q = p_ref[:, pair : pair + 128] * BF(HEAD_DIM**-0.5)
    k = p_ref[:, width + pair : width + pair + 128]
    v = p_ref[:, 2 * width + pair : 2 * width + pair + 128]
    g = g_ref[:, pair : pair + 128]
    low_lane = lax.broadcasted_iota(jnp.int32, (BLOCK, 128), 1) < HEAD_DIM
    causal = lax.broadcasted_iota(jnp.int32, (BLOCK, BLOCK), 0) <= lax.broadcasted_iota(
        jnp.int32, (BLOCK, BLOCK), 1
    )
    dk_ref[...] = jnp.zeros_like(dk_ref)
    dv_ref[...] = jnp.zeros_like(dv_ref)
    for start in range(0, LENGTH, BLOCK):
        stop = start + BLOCK
        logs = l_ref[start:stop, pair : pair + 128].T
        context = c_ref[start:stop, pair : pair + 128].astype(F32)
        product = (g[start:stop].astype(F32) * context).T
        query_grads = []
        for head in range(2):
            mine = low_lane if head == 0 else jnp.logical_not(low_lane)
            row = head * HEAD_DIM
            q_part = jnp.where(mine, q[start:stop], BF(0))
            g_part = jnp.where(mine, g[start:stop], BF(0))
            delta = jnp.sum(product[row : row + HEAD_DIM], 0, keepdims=True)
            scores = nt_dot(k[:stop], q_part)
            last = jnp.where(causal, scores[start:], -1e30)
            scores = jnp.concatenate([scores[:start], last], 0) if start else last
            probs = jnp.exp(scores - logs[row : row + 1])
            prob_grad = nt_dot(v[:stop], g_part)
            score_grad = (probs * (prob_grad - delta)).astype(BF)
            dv_ref[:stop] += nn_dot(probs.astype(BF), g_part)
            dk_ref[:stop] += nn_dot(score_grad, q_part)
            query_grads.append(tn_dot(score_grad, k[:stop]))
        dq_ref[start:stop] = jnp.where(low_lane, query_grads[0], query_grads[1]) * HEAD_DIM**-0.5
    return [ref[...].astype(BF) for ref in (dq_ref, dk_ref, dv_ref)]


def column_sums(values):
    return nn_dot(jnp.ones((8, values.shape[0]), BF), values)


def attend_back_part_kernel(pair, p_ref, g_ref, c_ref, l_ref, d_ref, dk_ref, dv_ref, dq_ref):
    results = attend_back_pair(p_ref, g_ref, c_ref, l_ref, pair * 128, dk_ref, dv_ref, dq_ref)
    for position, result in enumerate(results):
        d_ref[:, position * 128 : (position + 1) * 128] = result


def attend_back_last_kernel(p_ref, g_ref, c_ref, l_ref, *refs):
    parts, (d_ref, bias_ref, dk_ref, dv_ref, dq_ref) = refs[:-5], refs[-5:]
    width = g_ref.shape[1]
    results = attend_back_pair(
        p_ref, g_ref, c_ref, l_ref, len(parts) * 128, dk_ref, dv_ref, dq_ref
    )
    pieces = [[ref[:, i * 128 : (i + 1) * 128] for i in range(3)] for ref in parts]
    for pair, piece in enumerate(pieces + [results]):
        for position, result in enumerate(piece):
            columns = slice(position * width + pair * 128, position * width + pair * 128 + 128)
            d_ref[:, columns] = result
            bias_ref[:, columns] = column_sums(result)


def attend_back_part(projected, ctx_grad, context, logs, pair):
    return pl.pallas_call(
        functools.partial(attend_back_part_kernel, pair),
        out_shape=jax.ShapeDtypeStruct((LENGTH, 384), BF),
        in_specs=[pl.BlockSpec(memory_space=pltpu.VMEM)] * 4,
        out_specs=pl.BlockSpec(memory_space=pltpu.VMEM),
        scratch_shapes=[pltpu.VMEM((LENGTH, 128), F32)] * 3,
        compiler_params=params(14),
        cost_estimate=cost(),
        name="attend_back_part",
    )(projected, ctx_grad, context, logs)


def attend_back_last(projected, ctx_grad, context, logs, parts):
    width = projected.shape[1]
    return pl.pallas_call(
        attend_back_last_kernel,
        out_shape=(
            jax.ShapeDtypeStruct((LENGTH, width), BF),
            jax.ShapeDtypeStruct((8, width), F32),
        ),
        in_specs=[pl.BlockSpec(memory_space=pltpu.VMEM)] * (4 + len(parts)),
        out_specs=(pl.BlockSpec(memory_space=pltpu.VMEM),) * 2,
        scratch_shapes=[pltpu.VMEM((LENGTH, 128), F32)] * 3,
        compiler_params=params(18),
        cost_estimate=cost(),
        name="attend_back_last",
    )(projected, ctx_grad, context, logs, *parts)


def row_sums(values):
    return jnp.sum(values.reshape(values.shape[0] // 8, 8, values.shape[1]), 0)


def vmem_specs(count):
    return [pl.BlockSpec(memory_space=pltpu.VMEM)] * count


def hbm_specs(count):
    return [pl.BlockSpec(memory_space=pltpu.HBM)] * count


def fetch(pairs, sems):
    copies = [
        pltpu.make_async_copy(source, target, sems.at[i]) for i, (source, target) in enumerate(pairs)
    ]
    for copy in copies:
        copy.start()
    for copy in copies:
        copy.wait()


def smem_spec():
    return pl.BlockSpec(memory_space=pltpu.SMEM)


def params(megabytes):
    return pltpu.CompilerParams(vmem_limit_bytes=megabytes * MEGABYTE)


def cost():
    return pl.CostEstimate(flops=0, bytes_accessed=0, transcendentals=0)


def place_kernel(dp_ref, h1_ref, h2_ref, h1y_ref, h2x_ref, w_ref, sems):
    dp = dp_ref[0]
    pairs = []
    for low in range(2):
        for x in range(2):
            pairs.append((h1_ref.at[x * 2 + low], w_ref.at[0, dp ^ (low * 2 + x)]))
            pairs.append((h1y_ref.at[x * 2 + low], w_ref.at[1, dp ^ (low * 2 + x)]))
        for row in range(2):
            pairs.append((h2_ref.at[row * 2 + low], w_ref.at[row, dp ^ (4 + low * 2)]))
            pairs.append((h2x_ref.at[row * 2 + low], w_ref.at[row, dp ^ (4 + low * 2 + 1)]))
    fetch(pairs, sems)


def place_blocks(pieces, dp):
    if len(pieces) == 2:
        return jnp.stack(pieces)
    rows, columns = pieces[0].shape[1:]
    placed = pl.pallas_call(
        place_kernel,
        out_shape=jax.ShapeDtypeStruct((2, 8, rows, columns), BF),
        in_specs=[smem_spec()] + hbm_specs(4),
        out_specs=pl.BlockSpec(memory_space=pltpu.VMEM),
        scratch_shapes=[pltpu.SemaphoreType.DMA((16,))],
        compiler_params=params(6),
        cost_estimate=cost(),
        name="place",
    )(dp, *pieces)
    return placed.reshape(2, 8 * rows, columns)


def place_one_kernel(dp_ref, a_ref, b_ref, ay_ref, bx_ref, proj_ref, ctx_ref, *scratch):
    dp = dp_ref[0]
    *staged, sems = scratch
    fetch(list(zip((a_ref, b_ref, ay_ref, bx_ref), staged)), sems)
    h1_ref, h2_ref, h1y_ref, h2x_ref = staged
    block = h1_ref.shape[2] // 4

    def put(index, own, other):
        for kind in range(4):
            columns = slice(kind * block, (kind + 1) * block)
            both = jnp.concatenate([own[:, columns], other[:, columns]], 1)
            if kind < 3:
                proj_ref[dp ^ index, :, kind * 2 * block : (kind + 1) * 2 * block] = both
            else:
                ctx_ref[dp ^ index] = both

    for low in range(2):
        for x in range(2):
            put(low * 2 + x, h1_ref[x * 2 + low], h1y_ref[x * 2 + low])
        put(4 + low * 2, h2_ref[low], h2_ref[2 + low])
        put(4 + low * 2 + 1, h2x_ref[low], h2x_ref[2 + low])


def place_one(pieces, dp):
    if len(pieces) == 2:
        width = pieces[0].shape[0]
        cut = jnp.stack([piece.reshape(width, 4, -1) for piece in pieces], 2)
        return cut[:, :3].reshape(width, -1), cut[:, 3].reshape(width, -1)
    rows, columns = pieces[0].shape[1:]
    proj, ctx = pl.pallas_call(
        place_one_kernel,
        out_shape=(
            jax.ShapeDtypeStruct((8, rows, columns * 3 // 2), BF),
            jax.ShapeDtypeStruct((8, rows, columns // 2), BF),
        ),
        in_specs=[smem_spec()] + hbm_specs(4),
        out_specs=tuple(vmem_specs(2)),
        scratch_shapes=[pltpu.VMEM(pieces[0].shape, BF)] * 4 + [pltpu.SemaphoreType.DMA((4,))],
        compiler_params=params(8),
        cost_estimate=cost(),
        name="place_one",
    )(dp, *pieces)
    return proj.reshape(8 * rows, -1), ctx.reshape(8 * rows, -1)


def direct(shard):
    return lax.axis_size("dp") == 8 and shard.shape[0] % 16 == 0


def gather_z(shard):
    return swap(shard, "dp", 2), swap(shard, "dp", 4), swap(shard, "dp", 6)


def pair_up(shard, r1, r2, r3):
    return jnp.stack([shard, r1]), jnp.stack([r2, r3])


def gather_xy1(h1, h2):
    return swap(h1, "dp", 1), swap(h2, "y", 1)


def gather_xy2(h1, h2, h1x, h2y):
    h1 = jnp.concatenate([h1, h1x])
    h2 = jnp.concatenate([h2, h2y])
    return h1, h2, swap(h1, "y", 1), swap(h2, "dp", 1)


def gather_plain(shard):
    own = lax.all_gather(shard, "dp", axis=0, tiled=True)
    return own, swap(own, "y", 1)


def spread_put(dp, outs, result, row, columns=slice(None)):
    k1, s1, k2, s2, stage = outs
    rows = k1.shape[1]
    for index in range(8):
        stage[index] = result[index * rows : (index + 1) * rows].astype(BF)
    first = s1 if row else k1
    for low in range(2):
        for x in range(2):
            first[x * 2 + low, :, columns] = stage[dp ^ (low * 2 + x)]
        k2[row * 2 + low, :, columns] = stage[dp ^ (4 + low * 2)]
        s2[row * 2 + low, :, columns] = stage[dp ^ (4 + low * 2 + 1)]


def wgrad_kernel(dp_ref, left_ref, right_ref, k1, s1, k2, s2, stage):
    for row in range(2):

        @pl.when(pl.program_id(0) == row)
        def _():
            result = tn_dot(left_ref[...], right_ref[0])
            spread_put(dp_ref[0], (k1, s1, k2, s2, stage), result, row)


def wgrad(left, right, dp):
    width = left.shape[1]
    columns = right.shape[2]
    count = lax.axis_size("dp")
    if count != 8 or (width // count) % 16:
        return jnp.einsum("rd,yre->yde", left, right, preferred_element_type=F32).astype(BF)
    part = jax.ShapeDtypeStruct((4, width // 8, columns), BF)
    return pl.pallas_call(
        wgrad_kernel,
        out_shape=(part,) * 4,
        grid=(2,),
        in_specs=[
            smem_spec(),
            pl.BlockSpec((LENGTH, width), lambda i: (0, 0)),
            pl.BlockSpec((1, LENGTH, columns), lambda i: (i, 0, 0)),
        ],
        out_specs=(pl.BlockSpec(part.shape, lambda i: (0, 0, 0)),) * 4,
        scratch_shapes=[pltpu.VMEM((8, width // 8, columns), BF)],
        compiler_params=params(16),
        cost_estimate=cost(),
        name="wgrad",
    )(dp, left, right)


def wgrad_one_kernel(dp_ref, n_ref, d_ref, g_ref, c_ref, k1, s1, k2, s2, stage):
    block = c_ref.shape[1] // 2
    for kind in range(4):

        @pl.when(pl.program_id(0) == kind)
        def _():
            left, right = (n_ref, d_ref) if kind < 3 else (g_ref, c_ref)
            result = tn_dot(left[...], right[...])
            for row in range(2):
                spread_put(
                    dp_ref[0],
                    (k1, s1, k2, s2, stage),
                    result[:, row * block : (row + 1) * block],
                    row,
                    slice(kind * block, (kind + 1) * block),
                )


def wgrad_one(normed, proj_grad, branch_grad, context, dp):
    width = normed.shape[1]
    block = context.shape[1] // 2
    count = lax.axis_size("dp")
    if count != 8 or (width // count) % 16:
        proj = tn_dot(normed, proj_grad).reshape(width, 3, 2, block)
        out = tn_dot(branch_grad, context).reshape(width, 1, 2, block)
        both = jnp.concatenate([proj, out], 1).transpose(2, 0, 1, 3)
        return both.reshape(2, width, 4 * block).astype(BF)
    part = jax.ShapeDtypeStruct((4, width // 8, 4 * block), BF)
    return pl.pallas_call(
        wgrad_one_kernel,
        out_shape=(part,) * 4,
        grid=(4,),
        in_specs=[
            smem_spec(),
            pl.BlockSpec((LENGTH, width), lambda i: (0, 0)),
            pl.BlockSpec((LENGTH, 2 * block), lambda i: (0, jnp.minimum(i, 2))),
            pl.BlockSpec((LENGTH, width), lambda i: (0, 0)),
            pl.BlockSpec((LENGTH, 2 * block), lambda i: (0, 0)),
        ],
        out_specs=(pl.BlockSpec(part.shape, lambda i: (0, 0, 0)),) * 4,
        scratch_shapes=[pltpu.VMEM((8, width // 8, block), BF)],
        compiler_params=params(18),
        cost_estimate=cost(),
        name="wgrad_one",
    )(dp, normed, proj_grad, branch_grad, context)


def add_kernel(k1, t1, k2, t2, first, second, stage, sems):
    fetch([(ref.at[pl.ds(2, 2)], stage.at[i]) for i, ref in enumerate((k1, t1, k2, t2))], sems)
    first[...] = (stage[0].astype(F32) + stage[1].astype(F32)).astype(BF)
    second[...] = (stage[2].astype(F32) + stage[3].astype(F32)).astype(BF)


def sum_kernel(u1, u2, k1, t1, k2, t2, v, z1, z2, z3, stage, sems):
    parts = (u1, k1, t1, u2, k2, t2)
    fetch([(ref.at[pl.ds(0, 2)], stage.at[i]) for i, ref in enumerate(parts)], sems)

    def total(at, index):
        return sum(stage[at + i, index].astype(F32) for i in range(3))

    v[...] = total(0, 0)
    z1[...] = total(0, 1).astype(BF)
    z2[...] = total(3, 0).astype(BF)
    z3[...] = total(3, 1).astype(BF)


def scatter_xy1(parts):
    k1, s1, k2, s2 = parts
    return k1, swap(s1, "y", 1), k2, swap(s2, "dp", 1)


def scatter_xy2(item):
    _, rows, columns = item[0].shape
    half = jax.ShapeDtypeStruct((2, rows, columns), BF)
    first, second = pl.pallas_call(
        add_kernel,
        out_shape=(half, half),
        in_specs=hbm_specs(4),
        out_specs=tuple(vmem_specs(2)),
        scratch_shapes=[pltpu.VMEM((4, 2, rows, columns), BF), pltpu.SemaphoreType.DMA((4,))],
        compiler_params=params(4),
        cost_estimate=cost(),
        name="add_pairs",
    )(*item)
    return swap(first, "dp", 1), swap(second, "y", 1)


def scatter_z(sent, item):
    _, rows, columns = sent[0].shape
    low = jax.ShapeDtypeStruct((rows, columns), BF)
    v, z1, z2, z3 = pl.pallas_call(
        sum_kernel,
        out_shape=(jax.ShapeDtypeStruct((rows, columns), F32), low, low, low),
        in_specs=hbm_specs(6),
        out_specs=tuple(vmem_specs(4)),
        scratch_shapes=[pltpu.VMEM((6, 2, rows, columns), BF), pltpu.SemaphoreType.DMA((6,))],
        compiler_params=params(4),
        cost_estimate=cost(),
        name="sum_pairs",
    )(*sent, *item)
    return v, swap(z1, "dp", 2), swap(z2, "dp", 4), swap(z3, "dp", 6)


def last_sum_kernel(
    dp_ref, s_ref, u1, u2, k1, t1, k2, t2, v, own, z1, z2, z3, stage, blocks, sems
):
    dp = dp_ref[0]
    rows, columns = v.shape
    sum_kernel(u1, u2, k1, t1, k2, t2, v, *(ref.at[pl.ds(0, rows)] for ref in (z1, z2, z3)), stage, sems)
    piece = s_ref.shape[1] // 8
    for d in range(8):
        here = slice(d * piece, (d + 1) * piece)
        blocks[d, 0:8] = s_ref[0:8, here]
        blocks[d, 12:16] = s_ref[12:16, here]
        for j in range(4):
            at = d % 2 * 4 * piece + j * piece
            blocks[d, 8 + j : 9 + j] = s_ref[8 + d // 2 : 9 + d // 2, at : at + piece]
    own[...] = blocks[dp]
    for ref, bit in ((z1, 2), (z2, 4), (z3, 6)):
        value = blocks[dp ^ bit]
        high = value.astype(BF)
        ref[rows:, :] = jnp.zeros((16, columns), BF)
        ref[rows:, 0:piece] = high
        ref[rows:, 128 : 128 + piece] = (value - high.astype(F32)).astype(BF)


def scatter_last(sent, item, sums, dp):
    _, rows, columns = sent[0].shape
    low = jax.ShapeDtypeStruct((rows + 16, columns), BF)
    piece = sums.shape[1] // 8
    v, own, z1, z2, z3 = pl.pallas_call(
        last_sum_kernel,
        out_shape=(
            jax.ShapeDtypeStruct((rows, columns), F32),
            jax.ShapeDtypeStruct((16, piece), F32),
            low,
            low,
            low,
        ),
        in_specs=[smem_spec()] + vmem_specs(1) + hbm_specs(6),
        out_specs=tuple(vmem_specs(5)),
        scratch_shapes=[
            pltpu.VMEM((6, 2, rows, columns), BF),
            pltpu.VMEM((8, 16, piece), F32),
            pltpu.SemaphoreType.DMA((6,)),
        ],
        compiler_params=params(5),
        cost_estimate=cost(),
        name="sum_last",
    )(dp, sums, *sent, *item)
    return v, own, swap(z1, "dp", 2), swap(z2, "dp", 4), swap(z3, "dp", 6)


def end_kernel(own, *refs):
    ins, (qkv, out, small, up, down), (first, last, rest, sems) = refs[:12], refs[12:17], refs[17:]
    pairs = []
    for i in range(3):
        v, *sent = ins[4 * i : 4 * i + 4]
        pairs.append((v, first.at[i]))
        for j, ref in enumerate(sent):
            pairs.append((ref, last.at[j] if i == 0 else rest.at[i - 1, j]))
    fetch(pairs, sems)
    rows = first.shape[1]
    total = first[0] + sum(last[j, :rows].astype(F32) for j in range(3))
    block, piece = qkv.shape[2], own.shape[1]
    for kind in range(3):
        qkv[kind] = total[:, kind * block : (kind + 1) * block]
    out[...] = total[:, 3 * block :].T
    sums = own[...]
    for j in range(3):
        sums = sums + last[j, rows:, 0:piece].astype(F32)
        sums = sums + last[j, rows:, 128 : 128 + piece].astype(F32)
    small[...] = sums
    up[...] = first[1] + sum(rest[0, j].astype(F32) for j in range(3))
    down[...] = (first[2] + sum(rest[1, j].astype(F32) for j in range(3))).T


def scatter_end(one, up, down, shapes):
    v, own, *sent = one
    rows, columns = v.shape
    return pl.pallas_call(
        end_kernel,
        out_shape=tuple(jax.ShapeDtypeStruct(shape, F32) for shape in shapes),
        in_specs=vmem_specs(1) + hbm_specs(12),
        out_specs=tuple(vmem_specs(5)),
        scratch_shapes=[
            pltpu.VMEM((3, rows, columns), F32),
            pltpu.VMEM((3, rows + 16, columns), BF),
            pltpu.VMEM((2, 3, rows, columns), BF),
            pltpu.SemaphoreType.DMA((12,)),
        ],
        compiler_params=params(8),
        cost_estimate=cost(),
        name="scatter_end",
    )(own, v, *sent, *up, *down)


def scatter_plain(grad):
    both = grad[0].astype(F32) + swap(grad[1], "y", 1).astype(F32)
    return lax.psum_scatter(both, "dp", scatter_dimension=0, tiled=True)


def norm_parts(values):
    center = values - jnp.mean(values, -1, keepdims=True)
    spread = jnp.mean(center * center, -1, keepdims=True)
    scale = lax.rsqrt(spread + EPS)
    return center * scale, scale


def norm_back(xhat, scale, gain, grad):
    scaled = grad * gain
    first = jnp.mean(scaled, -1, keepdims=True)
    second = jnp.mean(scaled * xhat, -1, keepdims=True)
    return scale * (scaled - first - xhat * second)


def rows_spec(columns, lead=None):
    if lead is None:
        return pl.BlockSpec((ROWS, columns), lambda i, c: (i, 0))
    return pl.BlockSpec((lead, ROWS, columns), lambda i, c: (0, i, 0))


def whole_spec(shape):
    return pl.BlockSpec(shape, lambda i, c: (0,) * len(shape))


def half_spec(columns, mine):
    per_core = LENGTH // 2 // ROWS

    def index(i, c):
        inside = i // per_core == (c[0] if mine else 1 - c[0])
        return (jnp.where(inside, i % per_core, 0), 0)

    return pl.BlockSpec((ROWS, columns), index)


def pick_half(first_ref, second_ref):
    second = pl.program_id(0).astype(F32)
    return first_ref[...].astype(F32) * (1.0 - second) + second_ref[...].astype(F32) * second


def pick_rows(core_ref, own_ref, other_ref):
    per_core = LENGTH // 2 // ROWS
    mine = (pl.program_id(0) // per_core == core_ref[0]).astype(F32)
    return own_ref[...].astype(F32) * mine + other_ref[...].astype(F32) * (1.0 - mine)


def block_call(kernel, name, outs, specs, grid, megabytes):
    return pl.pallas_call(
        kernel,
        out_shape=tuple(shape for shape, _ in outs),
        grid_spec=pltpu.PrefetchScalarGridSpec(
            num_scalar_prefetch=1,
            grid=(grid,),
            in_specs=specs,
            out_specs=tuple(spec for _, spec in outs),
        ),
        compiler_params=params(megabytes),
        cost_estimate=cost(),
        name=name,
    )


def prepare_kernel(
    core_ref, own_ref, other_ref, cot_ref, cot_other_ref, gain_ref, shift_ref, n_ref, c_ref, s_ref
):
    cot = pick_rows(core_ref, cot_ref, cot_other_ref)
    c_ref[...] = cot.astype(BF)
    sums = row_sums(cot)

    @pl.when(pl.program_id(0) == 0)
    def _():
        s_ref[...] = sums

    @pl.when(pl.program_id(0) > 0)
    def _():
        s_ref[...] += sums

    xhat, _ = norm_parts(pick_rows(core_ref, own_ref, other_ref))
    n_ref[...] = (xhat * gain_ref[...] + shift_ref[...]).astype(BF)


def prepare(core, own, other, cot, cot_other, gain, shift):
    width = own.shape[1]
    rows = (jax.ShapeDtypeStruct((LENGTH, width), BF), rows_spec(width))
    return block_call(
        prepare_kernel,
        "prepare",
        [rows, rows, (jax.ShapeDtypeStruct((8, width), F32), whole_spec((8, width)))],
        [
            half_spec(width, True),
            half_spec(width, False),
            half_spec(width, True),
            half_spec(width, False),
            whole_spec((1, width)),
            whole_spec((1, width)),
        ],
        LENGTH // ROWS,
        16,
    )(core, own, other, cot, cot_other, gain, shift)


def project_kernel(core_ref, n_ref, w_ref, b_ref, p_ref):
    p_ref[...] = (nn_dot(n_ref[...], w_ref[...]) + b_ref[...]).astype(BF)


def project(core, normed, weight, bias):
    width, columns = weight.shape
    return block_call(
        project_kernel,
        "project",
        [(jax.ShapeDtypeStruct((LENGTH, columns), BF), rows_spec(columns))],
        [rows_spec(width), whole_spec((width, columns)), whole_spec((1, columns))],
        LENGTH // ROWS,
        14,
    )(core, normed, weight, bias)[0]


def middle_kernel(
    core_ref, own_ref, other_ref, part_ref, first_ref, second_ref, ob_ref, gain_ref, shift_ref,
    h_ref, n_ref,
):
    attended = part_ref[...].astype(F32) + pick_half(first_ref, second_ref)
    hidden = pick_rows(core_ref, own_ref, other_ref) + attended + ob_ref[...]
    h_ref[...] = hidden
    xhat, _ = norm_parts(hidden)
    n_ref[...] = (xhat * gain_ref[...] + shift_ref[...]).astype(BF)


def middle(core, own, other, part, part_other, out_bias, gain, shift):
    width = own.shape[1]
    return block_call(
        middle_kernel,
        "middle",
        [
            (jax.ShapeDtypeStruct((LENGTH, width), F32), rows_spec(width)),
            (jax.ShapeDtypeStruct((LENGTH, width), BF), rows_spec(width)),
        ],
        [half_spec(width, True), half_spec(width, False), rows_spec(width)]
        + [whole_spec((ROWS, width))] * 2
        + [whole_spec((1, width))] * 3,
        LENGTH // ROWS,
        16,
    )(core, own, other, part, *part_other, out_bias, gain, shift)


def up_kernel(core_ref, n_ref, w_ref, b_ref, a_ref, d_ref):
    slope = 0.7978845608028654
    for row in range(2):
        up = nn_dot(n_ref[...], w_ref[row]) + b_ref[row]
        square = up * up
        gate = 1.0 / (1.0 + jnp.exp(up * (-2.0 * slope - 2.0 * slope * 0.044715 * square)))
        gated = up * gate
        a_ref[row] = gated.astype(BF)
        inner = 2.0 * slope + 6.0 * slope * 0.044715 * square
        d_ref[row] = (gate + (gated - gated * gate) * inner).astype(BF)


def up_project(core, normed, weight, bias):
    width, columns = weight.shape[1:]
    both = (jax.ShapeDtypeStruct((2, LENGTH, columns), BF), rows_spec(columns, 2))
    return block_call(
        up_kernel,
        "up_project",
        [both, both],
        [rows_spec(width), whole_spec((2, width, columns)), whole_spec((2, 1, columns))],
        LENGTH // ROWS,
        20,
    )(core, normed, weight, bias[:, None])


def up_back_kernel(core_ref, cot_ref, d_ref, down_ref, up_ref, u_ref, b_ref, n_ref):
    total = None
    for row in range(2):
        grad = nn_dot(cot_ref[...], down_ref[row]) * d_ref[row].astype(F32)
        low = grad.astype(BF)
        u_ref[row] = low
        sums = row_sums(low.astype(F32))

        @pl.when(pl.program_id(0) == 0)
        def _():
            b_ref[row] = sums

        @pl.when(pl.program_id(0) > 0)
        def _():
            b_ref[row] += sums

        part = nt_dot(low, up_ref[row])
        total = part if total is None else total + part
    n_ref[...] = total.astype(BF)


def up_back(core, cot, slope, down, up):
    width, columns = down.shape[1:]
    return block_call(
        up_back_kernel,
        "up_back",
        [
            (jax.ShapeDtypeStruct((2, LENGTH, columns), BF), rows_spec(columns, 2)),
            (jax.ShapeDtypeStruct((2, 8, columns), F32), whole_spec((2, 8, columns))),
            (jax.ShapeDtypeStruct((LENGTH, width), BF), rows_spec(width)),
        ],
        [
            rows_spec(width),
            rows_spec(columns, 2),
            whole_spec((2, width, columns)),
            whole_spec((2, width, columns)),
        ],
        LENGTH // ROWS,
        24,
    )(core, cot, slope, down, up)


def second_back_kernel(
    core_ref, h_ref, part_ref, first_ref, second_ref, cot_ref, gain_ref, w_ref,
    dh_ref, do_ref, dc_ref, sum_ref,
):
    xhat, scale = norm_parts(h_ref[...])
    grad = part_ref[...].astype(F32) + pick_half(first_ref, second_ref)
    hidden_grad = cot_ref[...].astype(F32) + norm_back(xhat, scale, gain_ref[...], grad)
    low = hidden_grad.astype(BF)

    @pl.when(pl.program_id(0) == core_ref[0])
    def _():
        dh_ref[...] = hidden_grad

    do_ref[...] = low
    dc_ref[...] = nn_dot(low, w_ref[...]).astype(BF)
    sums = (row_sums(low.astype(F32)), row_sums(grad * xhat), row_sums(grad))
    for position, value in enumerate(sums):

        @pl.when(pl.program_id(0) == 0)
        def _():
            sum_ref[position] = value

        @pl.when(pl.program_id(0) > 0)
        def _():
            sum_ref[position] += value


def second_back(core, hidden, part, other, cot, gain, weight):
    width, columns = weight.shape
    return block_call(
        second_back_kernel,
        "second_back",
        [
            (jax.ShapeDtypeStruct((ROWS, width), F32), whole_spec((ROWS, width))),
            (jax.ShapeDtypeStruct((LENGTH, width), BF), rows_spec(width)),
            (jax.ShapeDtypeStruct((LENGTH, columns), BF), rows_spec(columns)),
            (jax.ShapeDtypeStruct((3, 8, width), F32), whole_spec((3, 8, width))),
        ],
        [rows_spec(width)] * 2
        + [whole_spec((ROWS, width))] * 2
        + [rows_spec(width), whole_spec((1, width)), whole_spec((width, columns))],
        LENGTH // ROWS,
        20,
    )(core, hidden, part, *other, cot, gain, weight)


def share(core, left, weight):
    count, _, depth = left.shape
    width = weight.shape[1]
    half = LENGTH // 2

    def kernel(core_ref, left_ref, weight_ref, own_ref, other_ref):
        total = nt_dot(left_ref[0], weight_ref[0])
        for index in range(1, count):
            total = total + nt_dot(left_ref[index], weight_ref[index])

        @pl.when(pl.program_id(0) == 0)
        def _():
            other_ref[...] = total.astype(BF)

        @pl.when(pl.program_id(0) == 1)
        def _():
            own_ref[...] = total

    def rows(i, c):
        return (0, jnp.where(i == 0, 1 - c[0], c[0]), 0)

    return block_call(
        kernel,
        "share",
        [
            (jax.ShapeDtypeStruct((half, width), F32), whole_spec((half, width))),
            (jax.ShapeDtypeStruct((half, width), BF), whole_spec((half, width))),
        ],
        [pl.BlockSpec((count, half, depth), rows), whole_spec(weight.shape)],
        2,
        16,
    )(core, left, weight)


def first_back_kernel(core_ref, x_ref, part_ref, first, second, dh_ref, gain_ref, t_ref, sum_ref):
    xhat, scale = norm_parts(x_ref[...].astype(F32))
    other = jnp.concatenate([first[...], second[...]], 0)
    grad = part_ref[...] + other.astype(F32)
    t_ref[...] = (dh_ref[...] + norm_back(xhat, scale, gain_ref[...], grad)).astype(BF)
    for position, value in enumerate((row_sums(grad * xhat), row_sums(grad))):

        @pl.when(pl.program_id(0) == 0)
        def _():
            sum_ref[position] = value

        @pl.when(pl.program_id(0) > 0)
        def _():
            sum_ref[position] += value


def first_back(core, own, part, other, hidden_grad, gain):
    width = own.shape[1]
    return block_call(
        first_back_kernel,
        "first_back",
        [
            (jax.ShapeDtypeStruct((LENGTH // 2, width), BF), rows_spec(width)),
            (jax.ShapeDtypeStruct((2, 8, width), F32), whole_spec((2, 8, width))),
        ],
        [rows_spec(width)] * 2
        + [whole_spec((ROWS // 2, width))] * 2
        + [rows_spec(width), whole_spec((1, width))],
        1,
        16,
    )(core, own, part, *other, hidden_grad, gain)


def unpack_kernel(place_ref, v_ref, g1, s1, qkv, ob, g2, s2, up, down, full):
    y, core = place_ref[0], place_ref[1]
    piece = g1.shape[1] // 8
    for d in range(8):
        rows = v_ref[d : d + 1]
        here = slice(d * piece, (d + 1) * piece)
        for ref, position in ((g1, 0), (s1, 1), (ob, 5), (g2, 6), (s2, 7), (down, 12)):
            ref[:, here] = rows[:, position * piece : (position + 1) * piece]
        for kind in range(3):
            full[kind : kind + 1, here] = rows[:, (2 + kind) * piece : (3 + kind) * piece]
        cut = slice(d % 2 * 4 * piece, (d % 2 + 1) * 4 * piece)
        full[3 + d // 2 : 4 + d // 2, cut] = rows[:, 8 * piece : 12 * piece]
    block = 2 * piece
    for kind in range(3):
        for y_index in range(2):
            cuts = []
            for core_index in range(2):
                at = (2 * y_index + core_index) * block
                cuts.append(full[kind : kind + 1, at : at + block])
            value = jnp.where(core == 0, cuts[0], cuts[1])
            for own in range(2):

                @pl.when((y ^ y_index) == own)
                def _():
                    at = (2 * kind + own) * block
                    qkv[:, at : at + block] = value

    for y_index in range(2):
        rows = [full[3 + 2 * y_index + i : 4 + 2 * y_index + i] for i in range(2)]
        value = jnp.where(core == 0, rows[0], rows[1])
        for own in range(2):

            @pl.when((y ^ y_index) == own)
            def _():
                up[own : own + 1] = value


def unpack(place, vectors, width):
    row = jax.ShapeDtypeStruct((1, width), F32)
    wide = jax.ShapeDtypeStruct((1, 3 * width // 2), F32)
    return pl.pallas_call(
        unpack_kernel,
        out_shape=(row, row, wide, row, row, row, jax.ShapeDtypeStruct((2, width), F32), row),
        in_specs=[smem_spec()] + vmem_specs(1),
        out_specs=tuple(vmem_specs(8)),
        scratch_shapes=[pltpu.VMEM((8, width), F32)],
        compiler_params=params(2),
        cost_estimate=cost(),
        name="unpack",
    )(place, vectors)


def pack_kernel(place_ref, first_ref, qkv_ref, second_ref, up_ref, cot_ref, full):
    y, core = place_ref[0], place_ref[1]
    width = full.shape[1]
    block = width // 4

    def column_sum(values):
        return jnp.sum(values, 0, keepdims=True)

    full[0:1] = column_sum(first_ref[0])
    full[1:2] = column_sum(first_ref[1])
    for position, index in ((5, 0), (6, 1), (7, 2)):
        full[position : position + 1] = 0.5 * column_sum(second_ref[index])
    full[12:13] = 0.5 * column_sum(cot_ref[...])
    qkv = qkv_ref[0:1]
    ups = [column_sum(up_ref[index]) for index in range(2)]
    for t in range(4):
        keep = (core == t % 2).astype(F32)
        mine = (y == t // 2).astype(F32)
        for kind in range(3):
            at = kind * 2 * block
            value = qkv[:, at : at + block] * mine + qkv[:, at + block : at + 2 * block] * (1.0 - mine)
            full[2 + kind : 3 + kind, t * block : (t + 1) * block] = value * keep
        full[8 + t : 9 + t] = (ups[0] * mine + ups[1] * (1.0 - mine)) * keep
    full[13:16] = jnp.zeros((3, width), F32)


def pack(place, first, qkv, second, up, cot):
    width = cot.shape[1]
    return pl.pallas_call(
        pack_kernel,
        out_shape=jax.ShapeDtypeStruct((16, width), F32),
        in_specs=[smem_spec()] + vmem_specs(5),
        out_specs=pl.BlockSpec(memory_space=pltpu.VMEM),
        compiler_params=params(4),
        cost_estimate=cost(),
        name="pack",
    )(place, first, qkv, second, up, cot)


def body(
    tokens,
    cotangent,
    first_gain,
    first_shift,
    w_qkv,
    qkv_bias,
    w_out,
    out_bias,
    second_gain,
    second_shift,
    w_up,
    up_bias,
    w_down,
    down_bias,
):
    dp_count = lax.axis_size("dp")
    dp = lax.axis_index("dp")
    y = lax.axis_index("y")
    core = lax.axis_index("core")
    dp_ref = dp.reshape(1).astype(jnp.int32)
    own_rows, width = tokens.shape
    piece = first_gain.shape[0]
    heads_own = w_qkv.shape[2]
    ff_own = w_up.shape[1]
    ff_piece = up_bias.shape[0]

    core_ref = core.reshape(1).astype(jnp.int32)
    place_ref = jnp.stack([y, core]).astype(jnp.int32)
    shard_one = jnp.concatenate([w_qkv[0], w_qkv[1], w_qkv[2], w_out.T], 1)
    fast = direct(shard_one)
    tie = lax.optimization_barrier
    tokens_other = swap(tokens, "core", 1)
    vectors = jnp.concatenate(
        [
            first_gain,
            first_shift,
            qkv_bias.reshape(-1),
            out_bias,
            second_gain,
            second_shift,
            up_bias,
            down_bias,
        ]
    )
    vectors = lax.all_to_all(
        jnp.broadcast_to(vectors[None], (dp_count, vectors.shape[0])), "dp", 0, 0, tiled=True
    )

    def own_half(rows):
        return lax.dynamic_slice_in_dim(rows, core * own_rows, own_rows, 0)

    def exchange(rows):
        half = rows.shape[0] // 2
        return [swap(rows[:half], "core", 1), swap(rows[half:], "core", 1)]

    if fast:
        one = gather_z(shard_one)
        shard_one, one, vectors, tokens_other, cotangent, w_up, w_down = tie(
            (shard_one, one, vectors, tokens_other, cotangent, w_up, w_down)
        )
        one = pair_up(shard_one, *one)
        one_xy1 = gather_xy1(*one)
        one, one_xy1, vectors, cotangent, w_up, w_down = tie(
            (one, one_xy1, vectors, cotangent, w_up, w_down)
        )
        one = gather_xy2(*one, *one_xy1)
        up = gather_z(w_up)
        cot_other = swap(cotangent, "core", 1)
        cot_other, vectors, w_down = tie((cot_other, vectors, w_down))
        shard_down = w_down.T
        gain_one, shift_one, qkv_own, out_full, gain_two, shift_two, up_own, down_full = unpack(
            place_ref, vectors, width
        )
    else:
        one, up, down = map(gather_plain, (shard_one, w_up, w_down.T))
        cot_other = swap(cotangent, "core", 1)

        def full(position, count=1):
            return vectors[:, position * piece : (position + count) * piece]

        def own_blocks(values):
            cut = values.reshape(values.shape[0], 2, 2, -1)
            cut = jnp.where(core == 0, cut[:, :, 0], cut[:, :, 1])
            both = [cut[:, 0], cut[:, 1]]
            first = jnp.where(y == 0, both[0], both[1])
            second = jnp.where(y == 0, both[1], both[0])
            return jnp.stack([first, second], 1)

        gain_one, shift_one, out_full, gain_two, shift_two = (
            full(position).reshape(1, -1) for position in (0, 1, 5, 6, 7)
        )
        qkv_full = full(2, 3).reshape(dp_count, 3, piece).transpose(1, 0, 2).reshape(3, width)
        qkv_own = own_blocks(qkv_full).reshape(1, -1)
        up_own = own_blocks(vectors[:, 8 * piece : 8 * piece + ff_piece].reshape(1, -1))[0]
        down_full = vectors[:, 8 * piece + ff_piece :].reshape(1, -1)
    normed_one, cot, cot_sums = prepare(
        core_ref, tokens, tokens_other, cotangent, cot_other, gain_one, shift_one
    )

    if fast:
        one, up, normed_one, cot, qkv_own, shard_down = tie(
            (one, up, normed_one, cot, qkv_own, shard_down)
        )
        up = pair_up(w_up, *up)
        up_xy1 = gather_xy1(*up)
        down = gather_z(shard_down)
    w_proj, w_ctx = place_one(one, dp_ref)
    projected = project(core_ref, normed_one, w_proj, qkv_own)
    context_first = attend_first(projected)
    if fast:
        context_first, up, up_xy1, down = tie((context_first, up, up_xy1, down))
        up = gather_xy2(*up, *up_xy1)
    context, logs = attend_rest(projected, *context_first)
    if fast:
        context, up, down = tie((context, up, down))
        down = pair_up(shard_down, *down)
        down_xy1 = gather_xy1(*down)
    out_part = nt_dot(context, w_ctx).astype(BF)
    out_other = exchange(out_part)

    hidden, normed_two = middle(
        core_ref, tokens, tokens_other, out_part, out_other, out_full, gain_two, shift_two
    )

    if fast:
        normed_two, down, down_xy1 = tie((normed_two, down, down_xy1))
        down = gather_xy2(*down, *down_xy1)
    weight_up = place_blocks(up, dp_ref)
    active, slope = up_project(core_ref, normed_two, weight_up, up_own)
    down_wgrad = wgrad(cot, active, dp_ref)
    if fast:
        down_wgrad, down, slope = tie((down_wgrad, down, slope))
        down_wgrad = scatter_xy1(down_wgrad)
    weight_down = place_blocks(down, dp_ref)
    upward_grad, up_bias_sums, normed_two_part = up_back(
        core_ref, cot, slope, weight_down, weight_up
    )
    up_wgrad = wgrad(normed_two, upward_grad, dp_ref)
    if fast:
        up_wgrad, down_wgrad, normed_two_part = tie((up_wgrad, down_wgrad, normed_two_part))
        up_wgrad = scatter_xy1(up_wgrad)
        down_sent = scatter_xy2(down_wgrad)
    normed_two_other = exchange(normed_two_part)

    hidden_grad, branch_grad, ctx_grad, second_sums = second_back(
        core_ref, hidden, normed_two_part, normed_two_other, cot, gain_two, w_ctx
    )
    parts = [attend_back_part(projected, ctx_grad, context, logs, pair) for pair in range(2)]
    mlp_part, mlp_sent = share(core_ref, active, weight_down)
    if fast:
        parts, up_wgrad, down_sent, ctx_grad, mlp_sent = tie(
            (parts, up_wgrad, down_sent, ctx_grad, mlp_sent)
        )
        up_sent = scatter_xy2(up_wgrad)
        down_wgrad = scatter_z(down_sent, down_wgrad)
    proj_grad, qkv_bias_own = attend_back_last(projected, ctx_grad, context, logs, parts)
    normed_one_part, sent = share(core_ref, proj_grad[None], w_proj[None])
    if fast:
        proj_grad, sent = tie((proj_grad, sent))
    one_wgrad = wgrad_one(normed_one, proj_grad, branch_grad, context, dp_ref)
    if fast:
        one_wgrad, up_sent, down_wgrad, sent = tie((one_wgrad, up_sent, down_wgrad, sent))
        one_wgrad = scatter_xy1(one_wgrad)
        up_wgrad = scatter_z(up_sent, up_wgrad)
    normed_one_other = exchange(sent)
    tokens_grad, first_sums = first_back(
        core_ref, tokens, normed_one_part, normed_one_other, hidden_grad, gain_one
    )

    if fast:
        sums = pack(place_ref, first_sums, qkv_bias_own, second_sums, up_bias_sums, cot_sums)
        sums = sums + swap(sums, "core", 1)
    else:

        def spread_blocks(values):
            block = values.shape[-1] // 2
            own, other = values[..., :block], values[..., block:]
            cut = [jnp.where(y == 0, own, other), jnp.where(y == 0, other, own)]
            return jnp.concatenate(
                [jnp.where(core == index, half, 0.0) for half in cut for index in range(2)], -1
            )

        sums = [
            jnp.sum(first_sums, 1),
            spread_blocks(qkv_bias_own[0].reshape(3, 2 * heads_own)),
            0.5 * jnp.sum(second_sums, 1),
            spread_blocks(jnp.sum(up_bias_sums, 1).reshape(1, -1)),
            0.5 * jnp.sum(cot_sums, 0)[None],
        ]
        sums = [
            item.reshape(item.shape[0], dp_count, -1).transpose(1, 0, 2).reshape(dp_count, -1)
            for item in sums
        ]
        sums = jnp.concatenate(sums, 1)
        sums = jnp.broadcast_to(sums[:, None, :], (dp_count, 4, sums.shape[1]))
        sums = sums.reshape(dp_count * 4, -1)
    if fast:
        one_wgrad, sums, up_wgrad, mlp_sent = tie((one_wgrad, sums, up_wgrad, mlp_sent))
        one_sent = scatter_xy2(one_wgrad)
        sums = sums + (swap(sums, "dp", 1) + swap(sums, "y", 1) + swap_both(sums))
    mlp_other = swap(mlp_sent, "core", 1)
    if fast:
        one_sent, sums, mlp_other = tie((one_sent, sums, mlp_other))
        one_wgrad = scatter_last(one_sent, one_wgrad, sums, dp_ref)
    block_out = (own_half(hidden) + mlp_part + mlp_other.astype(F32) + down_full).astype(BF)
    if fast:
        one_wgrad, block_out = tie((one_wgrad, block_out))
        shapes = (w_qkv.shape, w_out.shape, one_wgrad[1].shape, w_up.shape, w_down.shape)
        qkv_wgrad, out_wgrad, sums, up_wgrad, down_wgrad = scatter_end(
            one_wgrad, up_wgrad, down_wgrad, shapes
        )
        small = (sums[0], sums[1], sums[2:5], sums[5], sums[6], sums[7], sums[8:12], sums[12])
    else:
        one_wgrad, up_wgrad, down_wgrad = map(scatter_plain, (one_wgrad, up_wgrad, down_wgrad))
        down_wgrad = down_wgrad.T
        qkv_wgrad = one_wgrad[:, : 3 * heads_own].reshape(piece, 3, heads_own).transpose(1, 0, 2)
        out_wgrad = one_wgrad[:, 3 * heads_own :].T
        sums = lax.all_to_all(sums, ("dp", "y", "core"), 0, 0, tiled=True)
        sums = jnp.sum(sums, 0).reshape(-1, piece)
        small = (sums[0], sums[1], sums[2:5], sums[5], sums[6], sums[7], sums[8:12], sums[12])
    vector_grads = small[:6] + (small[6].reshape(-1), small[7])

    return (
        block_out,
        tokens_grad,
        vector_grads[0],
        vector_grads[1],
        qkv_wgrad,
        vector_grads[2],
        out_wgrad,
        vector_grads[3],
        vector_grads[4],
        vector_grads[5],
        up_wgrad,
        vector_grads[6],
        down_wgrad,
        vector_grads[7],
    )


def solution(mesh):
    devices = mesh.devices
    split = Mesh(devices.reshape(devices.shape[0], 2, 2), ("dp", "y", "core"))
    tensor = ("y", "core")
    rows = P(("dp", "y", "core"), None)
    specs = (
        P("dp"),
        P("dp"),
        P(None, "dp", tensor),
        P(None, "dp"),
        P(tensor, "dp"),
        P("dp"),
        P("dp"),
        P("dp"),
        P("dp", tensor),
        P("dp"),
        P(tensor, "dp"),
        P("dp"),
    )
    return jax.shard_map(
        body,
        mesh=split,
        in_specs=(rows, rows) + specs,
        out_specs=(rows, rows) + specs,
        check_vma=False,
    )
```

```python
import functools

import jax
import jax.numpy as jnp
from jax import lax
from jax.experimental import pallas as pl
from jax.experimental.pallas import tpu as pltpu
from jax.sharding import Mesh
from jax.sharding import PartitionSpec as P

HEAD_DIM = 64
LENGTH = 1024
EPS = 1e-05
BLOCK = 256
ROWS = 512
BF = jnp.bfloat16
F32 = jnp.float32
MEGABYTE = 1024 * 1024


def swap(value, axis, bit):
    size = lax.axis_size(axis)
    return lax.ppermute(value, axis, [(i, i ^ bit) for i in range(size)])


def swap_both(value):
    size = lax.axis_size("dp") * 2
    return lax.ppermute(value, ("dp", "y"), [(i, i ^ 3) for i in range(size)])


def nt_dot(left, right):
    return lax.dot_general(left, right, (((1,), (1,)), ((), ())), preferred_element_type=F32)


def tn_dot(left, right):
    return lax.dot_general(left, right, (((0,), (0,)), ((), ())), preferred_element_type=F32)


def nn_dot(left, right):
    return jnp.dot(left, right, preferred_element_type=F32)


def attend_pair(p_ref, pair, width):
    q = p_ref[:, pl.ds(pair, 128)] * BF(HEAD_DIM**-0.5)
    k = p_ref[:, pl.ds(width + pair, 128)]
    v = p_ref[:, pl.ds(2 * width + pair, 128)]
    lane = lax.broadcasted_iota(jnp.int32, (LENGTH, 128), 1)
    low_lane = lax.broadcasted_iota(jnp.int32, (BLOCK, 128), 1) < HEAD_DIM
    causal = lax.broadcasted_iota(jnp.int32, (BLOCK, BLOCK), 0) >= lax.broadcasted_iota(
        jnp.int32, (BLOCK, BLOCK), 1
    )
    for start in range(0, LENGTH, BLOCK):
        stop = start + BLOCK
        halves = []
        logs = []
        for head in range(2):
            mine = (lane < HEAD_DIM) if head == 0 else (lane >= HEAD_DIM)
            q_part = jnp.where(mine[start:stop], q[start:stop], BF(0))
            v_part = jnp.where(mine[:stop], v[:stop], BF(1))
            scores = nt_dot(q_part, k[:stop])
            last = jnp.where(causal, scores[:, start:], -1e30)
            scores = jnp.concatenate([scores[:, :start], last], 1) if start else last
            top = jnp.max(scores, 1, keepdims=True)
            weights = jnp.exp(scores - top).astype(BF)
            result = nn_dot(weights, v_part)
            total = pltpu.roll(result, HEAD_DIM, 1)
            halves.append(result / total)
            logs.append(top + jnp.log(total))
        yield (
            start,
            jnp.where(low_lane, halves[0], halves[1]).astype(BF),
            jnp.where(low_lane, logs[0], logs[1]),
        )


def attend_first_kernel(p_ref, c_ref, l_ref):
    for start, context, logs in attend_pair(p_ref, 0, p_ref.shape[1] // 3):
        c_ref[start : start + BLOCK] = context
        l_ref[start : start + BLOCK] = logs


def attend_rest_kernel(p_ref, first_ref, first_log_ref, c_ref, l_ref):
    width = c_ref.shape[1]
    pair = pl.multiple_of((pl.program_id(0) + 1) * 128, 128)
    for start, context, logs in attend_pair(p_ref, pair, width):
        c_ref[start : start + BLOCK, pl.ds(pair, 128)] = context
        l_ref[start : start + BLOCK, pl.ds(pair, 128)] = logs

    @pl.when(pl.program_id(0) == 0)
    def _():
        c_ref[:, :128] = first_ref[...]
        l_ref[:, :128] = first_log_ref[...]


def attend_first(projected):
    return pl.pallas_call(
        attend_first_kernel,
        out_shape=(
            jax.ShapeDtypeStruct((LENGTH, 128), BF),
            jax.ShapeDtypeStruct((LENGTH, 128), F32),
        ),
        in_specs=[pl.BlockSpec(memory_space=pltpu.VMEM)],
        out_specs=(pl.BlockSpec(memory_space=pltpu.VMEM),) * 2,
        compiler_params=params(12),
        cost_estimate=cost(),
        name="attend_first",
    )(projected)


def attend_rest(projected, first, first_log):
    width = projected.shape[1] // 3
    pairs = width // 128 - 1
    return pl.pallas_call(
        attend_rest_kernel,
        out_shape=(
            jax.ShapeDtypeStruct((LENGTH, width), BF),
            jax.ShapeDtypeStruct((LENGTH, width), F32),
        ),
        grid=(pairs,),
        in_specs=[
            pl.BlockSpec((LENGTH, 3 * width), lambda i: (0, 0)),
            pl.BlockSpec((LENGTH, 128), lambda i: (0, 0)),
            pl.BlockSpec((LENGTH, 128), lambda i: (0, 0)),
        ],
        out_specs=(pl.BlockSpec((LENGTH, width), lambda i: (0, 0)),) * 2,
        compiler_params=params(16),
        cost_estimate=cost(),
        name="attend_rest",
    )(projected, first, first_log)


def attend_back_pair(p_ref, g_ref, c_ref, l_ref, pair, dk_ref, dv_ref, dq_ref):
    width = g_ref.shape[1]
    q = p_ref[:, pair : pair + 128] * BF(HEAD_DIM**-0.5)
    k = p_ref[:, width + pair : width + pair + 128]
    v = p_ref[:, 2 * width + pair : 2 * width + pair + 128]
    g = g_ref[:, pair : pair + 128]
    low_lane = lax.broadcasted_iota(jnp.int32, (BLOCK, 128), 1) < HEAD_DIM
    causal = lax.broadcasted_iota(jnp.int32, (BLOCK, BLOCK), 0) <= lax.broadcasted_iota(
        jnp.int32, (BLOCK, BLOCK), 1
    )
    dk_ref[...] = jnp.zeros_like(dk_ref)
    dv_ref[...] = jnp.zeros_like(dv_ref)
    for start in range(0, LENGTH, BLOCK):
        stop = start + BLOCK
        logs = l_ref[start:stop, pair : pair + 128].T
        context = c_ref[start:stop, pair : pair + 128].astype(F32)
        product = (g[start:stop].astype(F32) * context).T
        query_grads = []
        for head in range(2):
            mine = low_lane if head == 0 else jnp.logical_not(low_lane)
            row = head * HEAD_DIM
            q_part = jnp.where(mine, q[start:stop], BF(0))
            g_part = jnp.where(mine, g[start:stop], BF(0))
            delta = jnp.sum(product[row : row + HEAD_DIM], 0, keepdims=True)
            scores = nt_dot(k[:stop], q_part)
            last = jnp.where(causal, scores[start:], -1e30)
            scores = jnp.concatenate([scores[:start], last], 0) if start else last
            probs = jnp.exp(scores - logs[row : row + 1])
            prob_grad = nt_dot(v[:stop], g_part)
            score_grad = (probs * (prob_grad - delta)).astype(BF)
            dv_ref[:stop] += nn_dot(probs.astype(BF), g_part)
            dk_ref[:stop] += nn_dot(score_grad, q_part)
            query_grads.append(tn_dot(score_grad, k[:stop]))
        dq_ref[start:stop] = jnp.where(low_lane, query_grads[0], query_grads[1]) * HEAD_DIM**-0.5
    return [ref[...].astype(BF) for ref in (dq_ref, dk_ref, dv_ref)]


def column_sums(values):
    return nn_dot(jnp.ones((8, values.shape[0]), BF), values)


def attend_back_part_kernel(pair, p_ref, g_ref, c_ref, l_ref, d_ref, dk_ref, dv_ref, dq_ref):
    results = attend_back_pair(p_ref, g_ref, c_ref, l_ref, pair * 128, dk_ref, dv_ref, dq_ref)
    for position, result in enumerate(results):
        d_ref[:, position * 128 : (position + 1) * 128] = result


def attend_back_last_kernel(p_ref, g_ref, c_ref, l_ref, *refs):
    parts, (d_ref, bias_ref, dk_ref, dv_ref, dq_ref) = refs[:-5], refs[-5:]
    width = g_ref.shape[1]
    results = attend_back_pair(
        p_ref, g_ref, c_ref, l_ref, len(parts) * 128, dk_ref, dv_ref, dq_ref
    )
    pieces = [[ref[:, i * 128 : (i + 1) * 128] for i in range(3)] for ref in parts]
    for pair, piece in enumerate(pieces + [results]):
        for position, result in enumerate(piece):
            columns = slice(position * width + pair * 128, position * width + pair * 128 + 128)
            d_ref[:, columns] = result
            bias_ref[:, columns] = column_sums(result)


def attend_back_part(projected, ctx_grad, context, logs, pair):
    return pl.pallas_call(
        functools.partial(attend_back_part_kernel, pair),
        out_shape=jax.ShapeDtypeStruct((LENGTH, 384), BF),
        in_specs=[pl.BlockSpec(memory_space=pltpu.VMEM)] * 4,
        out_specs=pl.BlockSpec(memory_space=pltpu.VMEM),
        scratch_shapes=[pltpu.VMEM((LENGTH, 128), F32)] * 3,
        compiler_params=params(14),
        cost_estimate=cost(),
        name="attend_back_part",
    )(projected, ctx_grad, context, logs)


def attend_back_last(projected, ctx_grad, context, logs, parts):
    width = projected.shape[1]
    return pl.pallas_call(
        attend_back_last_kernel,
        out_shape=(
            jax.ShapeDtypeStruct((LENGTH, width), BF),
            jax.ShapeDtypeStruct((8, width), F32),
        ),
        in_specs=[pl.BlockSpec(memory_space=pltpu.VMEM)] * (4 + len(parts)),
        out_specs=(pl.BlockSpec(memory_space=pltpu.VMEM),) * 2,
        scratch_shapes=[pltpu.VMEM((LENGTH, 128), F32)] * 3,
        compiler_params=params(18),
        cost_estimate=cost(),
        name="attend_back_last",
    )(projected, ctx_grad, context, logs, *parts)


def row_sums(values):
    return jnp.sum(values.reshape(values.shape[0] // 8, 8, values.shape[1]), 0)


def vmem_specs(count):
    return [pl.BlockSpec(memory_space=pltpu.VMEM)] * count


def hbm_specs(count):
    return [pl.BlockSpec(memory_space=pltpu.HBM)] * count


def fetch(pairs, sems):
    copies = [
        pltpu.make_async_copy(source, target, sems.at[i]) for i, (source, target) in enumerate(pairs)
    ]
    for copy in copies:
        copy.start()
    for copy in copies:
        copy.wait()


def smem_spec():
    return pl.BlockSpec(memory_space=pltpu.SMEM)


def params(megabytes):
    return pltpu.CompilerParams(vmem_limit_bytes=megabytes * MEGABYTE)


def cost():
    return pl.CostEstimate(flops=0, bytes_accessed=0, transcendentals=0)


def place_kernel(dp_ref, h1_ref, h2_ref, h1y_ref, h2x_ref, w_ref):
    dp = dp_ref[0]
    for low in range(2):
        for x in range(2):
            w_ref[0, dp ^ (low * 2 + x)] = h1_ref[x * 2 + low]
            w_ref[1, dp ^ (low * 2 + x)] = h1y_ref[x * 2 + low]
        for row in range(2):
            w_ref[row, dp ^ (4 + low * 2)] = h2_ref[row * 2 + low]
            w_ref[row, dp ^ (4 + low * 2 + 1)] = h2x_ref[row * 2 + low]


def place_blocks(pieces, dp):
    if len(pieces) == 2:
        return jnp.stack(pieces)
    rows, columns = pieces[0].shape[1:]
    placed = pl.pallas_call(
        place_kernel,
        out_shape=jax.ShapeDtypeStruct((2, 8, rows, columns), BF),
        in_specs=[smem_spec()] + vmem_specs(4),
        out_specs=pl.BlockSpec(memory_space=pltpu.VMEM),
        compiler_params=params(10),
        cost_estimate=cost(),
        name="place",
    )(dp, *pieces)
    return placed.reshape(2, 8 * rows, columns)


def place_one_kernel(dp_ref, a_ref, b_ref, ay_ref, bx_ref, proj_ref, ctx_ref, *scratch):
    dp = dp_ref[0]
    *staged, sems = scratch
    fetch(list(zip((a_ref, b_ref, ay_ref, bx_ref), staged)), sems)
    h1_ref, h2_ref, h1y_ref, h2x_ref = staged
    block = h1_ref.shape[2] // 4

    def put(index, own, other):
        for kind in range(4):
            columns = slice(kind * block, (kind + 1) * block)
            both = jnp.concatenate([own[:, columns], other[:, columns]], 1)
            if kind < 3:
                proj_ref[dp ^ index, :, kind * 2 * block : (kind + 1) * 2 * block] = both
            else:
                ctx_ref[dp ^ index] = both

    for low in range(2):
        for x in range(2):
            put(low * 2 + x, h1_ref[x * 2 + low], h1y_ref[x * 2 + low])
        put(4 + low * 2, h2_ref[low], h2_ref[2 + low])
        put(4 + low * 2 + 1, h2x_ref[low], h2x_ref[2 + low])


def place_one(pieces, dp):
    if len(pieces) == 2:
        width = pieces[0].shape[0]
        cut = jnp.stack([piece.reshape(width, 4, -1) for piece in pieces], 2)
        return cut[:, :3].reshape(width, -1), cut[:, 3].reshape(width, -1)
    rows, columns = pieces[0].shape[1:]
    proj, ctx = pl.pallas_call(
        place_one_kernel,
        out_shape=(
            jax.ShapeDtypeStruct((8, rows, columns * 3 // 2), BF),
            jax.ShapeDtypeStruct((8, rows, columns // 2), BF),
        ),
        in_specs=[smem_spec()] + hbm_specs(4),
        out_specs=tuple(vmem_specs(2)),
        scratch_shapes=[pltpu.VMEM(pieces[0].shape, BF)] * 4 + [pltpu.SemaphoreType.DMA((4,))],
        compiler_params=params(8),
        cost_estimate=cost(),
        name="place_one",
    )(dp, *pieces)
    return proj.reshape(8 * rows, -1), ctx.reshape(8 * rows, -1)


def direct(shard):
    return lax.axis_size("dp") == 8 and shard.shape[0] % 16 == 0


def gather_z(shard):
    return swap(shard, "dp", 2), swap(shard, "dp", 4), swap(shard, "dp", 6)


def pair_up(shard, r1, r2, r3):
    return jnp.stack([shard, r1]), jnp.stack([r2, r3])


def gather_xy1(h1, h2):
    return swap(h1, "dp", 1), swap(h2, "y", 1)


def gather_xy2(h1, h2, h1x, h2y):
    h1 = jnp.concatenate([h1, h1x])
    h2 = jnp.concatenate([h2, h2y])
    return h1, h2, swap(h1, "y", 1), swap(h2, "dp", 1)


def gather_plain(shard):
    own = lax.all_gather(shard, "dp", axis=0, tiled=True)
    return own, swap(own, "y", 1)


def spread_put(dp, outs, result, row, columns=slice(None)):
    k1, s1, k2, s2, stage = outs
    rows = k1.shape[1]
    for index in range(8):
        stage[index] = result[index * rows : (index + 1) * rows].astype(BF)
    first = s1 if row else k1
    for low in range(2):
        for x in range(2):
            first[x * 2 + low, :, columns] = stage[dp ^ (low * 2 + x)]
        k2[row * 2 + low, :, columns] = stage[dp ^ (4 + low * 2)]
        s2[row * 2 + low, :, columns] = stage[dp ^ (4 + low * 2 + 1)]


def wgrad_kernel(dp_ref, left_ref, right_ref, k1, s1, k2, s2, stage):
    for row in range(2):

        @pl.when(pl.program_id(0) == row)
        def _():
            result = tn_dot(left_ref[...], right_ref[0])
            spread_put(dp_ref[0], (k1, s1, k2, s2, stage), result, row)


def wgrad(left, right, dp):
    width = left.shape[1]
    columns = right.shape[2]
    count = lax.axis_size("dp")
    if count != 8 or (width // count) % 16:
        return jnp.einsum("rd,yre->yde", left, right, preferred_element_type=F32).astype(BF)
    part = jax.ShapeDtypeStruct((4, width // 8, columns), BF)
    return pl.pallas_call(
        wgrad_kernel,
        out_shape=(part,) * 4,
        grid=(2,),
        in_specs=[
            smem_spec(),
            pl.BlockSpec((LENGTH, width), lambda i: (0, 0)),
            pl.BlockSpec((1, LENGTH, columns), lambda i: (i, 0, 0)),
        ],
        out_specs=(pl.BlockSpec(part.shape, lambda i: (0, 0, 0)),) * 4,
        scratch_shapes=[pltpu.VMEM((8, width // 8, columns), BF)],
        compiler_params=params(16),
        cost_estimate=cost(),
        name="wgrad",
    )(dp, left, right)


def wgrad_one_kernel(dp_ref, n_ref, d_ref, g_ref, c_ref, k1, s1, k2, s2, stage):
    block = c_ref.shape[1] // 2
    for kind in range(4):

        @pl.when(pl.program_id(0) == kind)
        def _():
            left, right = (n_ref, d_ref) if kind < 3 else (g_ref, c_ref)
            result = tn_dot(left[...], right[...])
            for row in range(2):
                spread_put(
                    dp_ref[0],
                    (k1, s1, k2, s2, stage),
                    result[:, row * block : (row + 1) * block],
                    row,
                    slice(kind * block, (kind + 1) * block),
                )


def wgrad_one(normed, proj_grad, branch_grad, context, dp):
    width = normed.shape[1]
    block = context.shape[1] // 2
    count = lax.axis_size("dp")
    if count != 8 or (width // count) % 16:
        proj = tn_dot(normed, proj_grad).reshape(width, 3, 2, block)
        out = tn_dot(branch_grad, context).reshape(width, 1, 2, block)
        both = jnp.concatenate([proj, out], 1).transpose(2, 0, 1, 3)
        return both.reshape(2, width, 4 * block).astype(BF)
    part = jax.ShapeDtypeStruct((4, width // 8, 4 * block), BF)
    return pl.pallas_call(
        wgrad_one_kernel,
        out_shape=(part,) * 4,
        grid=(4,),
        in_specs=[
            smem_spec(),
            pl.BlockSpec((LENGTH, width), lambda i: (0, 0)),
            pl.BlockSpec((LENGTH, 2 * block), lambda i: (0, jnp.minimum(i, 2))),
            pl.BlockSpec((LENGTH, width), lambda i: (0, 0)),
            pl.BlockSpec((LENGTH, 2 * block), lambda i: (0, 0)),
        ],
        out_specs=(pl.BlockSpec(part.shape, lambda i: (0, 0, 0)),) * 4,
        scratch_shapes=[pltpu.VMEM((8, width // 8, block), BF)],
        compiler_params=params(18),
        cost_estimate=cost(),
        name="wgrad_one",
    )(dp, normed, proj_grad, branch_grad, context)


def add_kernel(k1, t1, k2, t2, first, second, stage, sems):
    fetch([(ref.at[pl.ds(2, 2)], stage.at[i]) for i, ref in enumerate((k1, t1, k2, t2))], sems)
    first[...] = (stage[0].astype(F32) + stage[1].astype(F32)).astype(BF)
    second[...] = (stage[2].astype(F32) + stage[3].astype(F32)).astype(BF)


def sum_kernel(u1, u2, k1, t1, k2, t2, v, z1, z2, z3, stage, sems):
    parts = (u1, k1, t1, u2, k2, t2)
    fetch([(ref.at[pl.ds(0, 2)], stage.at[i]) for i, ref in enumerate(parts)], sems)

    def total(at, index):
        return sum(stage[at + i, index].astype(F32) for i in range(3))

    v[...] = total(0, 0)
    z1[...] = total(0, 1).astype(BF)
    z2[...] = total(3, 0).astype(BF)
    z3[...] = total(3, 1).astype(BF)


def scatter_xy1(parts):
    k1, s1, k2, s2 = parts
    return k1, swap(s1, "y", 1), k2, swap(s2, "dp", 1)


def scatter_xy2(item):
    _, rows, columns = item[0].shape
    half = jax.ShapeDtypeStruct((2, rows, columns), BF)
    first, second = pl.pallas_call(
        add_kernel,
        out_shape=(half, half),
        in_specs=hbm_specs(4),
        out_specs=tuple(vmem_specs(2)),
        scratch_shapes=[pltpu.VMEM((4, 2, rows, columns), BF), pltpu.SemaphoreType.DMA((4,))],
        compiler_params=params(4),
        cost_estimate=cost(),
        name="add_pairs",
    )(*item)
    return swap(first, "dp", 1), swap(second, "y", 1)


def scatter_z(sent, item):
    _, rows, columns = sent[0].shape
    low = jax.ShapeDtypeStruct((rows, columns), BF)
    v, z1, z2, z3 = pl.pallas_call(
        sum_kernel,
        out_shape=(jax.ShapeDtypeStruct((rows, columns), F32), low, low, low),
        in_specs=hbm_specs(6),
        out_specs=tuple(vmem_specs(4)),
        scratch_shapes=[pltpu.VMEM((6, 2, rows, columns), BF), pltpu.SemaphoreType.DMA((6,))],
        compiler_params=params(4),
        cost_estimate=cost(),
        name="sum_pairs",
    )(*sent, *item)
    return v, swap(z1, "dp", 2), swap(z2, "dp", 4), swap(z3, "dp", 6)


def last_sum_kernel(
    dp_ref, s_ref, u1, u2, k1, t1, k2, t2, v, own, z1, z2, z3, stage, blocks, sems
):
    dp = dp_ref[0]
    rows, columns = v.shape
    sum_kernel(u1, u2, k1, t1, k2, t2, v, *(ref.at[pl.ds(0, rows)] for ref in (z1, z2, z3)), stage, sems)
    piece = s_ref.shape[1] // 8
    for d in range(8):
        here = slice(d * piece, (d + 1) * piece)
        blocks[d, 0:8] = s_ref[0:8, here]
        blocks[d, 12:16] = s_ref[12:16, here]
        for j in range(4):
            at = d % 2 * 4 * piece + j * piece
            blocks[d, 8 + j : 9 + j] = s_ref[8 + d // 2 : 9 + d // 2, at : at + piece]
    own[...] = blocks[dp]
    for ref, bit in ((z1, 2), (z2, 4), (z3, 6)):
        value = blocks[dp ^ bit]
        high = value.astype(BF)
        ref[rows:, :] = jnp.zeros((16, columns), BF)
        ref[rows:, 0:piece] = high
        ref[rows:, 128 : 128 + piece] = (value - high.astype(F32)).astype(BF)


def scatter_last(sent, item, sums, dp):
    _, rows, columns = sent[0].shape
    low = jax.ShapeDtypeStruct((rows + 16, columns), BF)
    piece = sums.shape[1] // 8
    v, own, z1, z2, z3 = pl.pallas_call(
        last_sum_kernel,
        out_shape=(
            jax.ShapeDtypeStruct((rows, columns), F32),
            jax.ShapeDtypeStruct((16, piece), F32),
            low,
            low,
            low,
        ),
        in_specs=[smem_spec()] + vmem_specs(1) + hbm_specs(6),
        out_specs=tuple(vmem_specs(5)),
        scratch_shapes=[
            pltpu.VMEM((6, 2, rows, columns), BF),
            pltpu.VMEM((8, 16, piece), F32),
            pltpu.SemaphoreType.DMA((6,)),
        ],
        compiler_params=params(5),
        cost_estimate=cost(),
        name="sum_last",
    )(dp, sums, *sent, *item)
    return v, own, swap(z1, "dp", 2), swap(z2, "dp", 4), swap(z3, "dp", 6)


def end_kernel(own, *refs):
    ins, (qkv, out, small, up, down), (first, last, rest, sems) = refs[:12], refs[12:17], refs[17:]
    pairs = []
    for i in range(3):
        v, *sent = ins[4 * i : 4 * i + 4]
        pairs.append((v, first.at[i]))
        for j, ref in enumerate(sent):
            pairs.append((ref, last.at[j] if i == 0 else rest.at[i - 1, j]))
    fetch(pairs, sems)
    rows = first.shape[1]
    total = first[0] + sum(last[j, :rows].astype(F32) for j in range(3))
    block, piece = qkv.shape[2], own.shape[1]
    for kind in range(3):
        qkv[kind] = total[:, kind * block : (kind + 1) * block]
    out[...] = total[:, 3 * block :].T
    sums = own[...]
    for j in range(3):
        sums = sums + last[j, rows:, 0:piece].astype(F32)
        sums = sums + last[j, rows:, 128 : 128 + piece].astype(F32)
    small[...] = sums
    up[...] = first[1] + sum(rest[0, j].astype(F32) for j in range(3))
    down[...] = (first[2] + sum(rest[1, j].astype(F32) for j in range(3))).T


def scatter_end(one, up, down, shapes):
    v, own, *sent = one
    rows, columns = v.shape
    return pl.pallas_call(
        end_kernel,
        out_shape=tuple(jax.ShapeDtypeStruct(shape, F32) for shape in shapes),
        in_specs=vmem_specs(1) + hbm_specs(12),
        out_specs=tuple(vmem_specs(5)),
        scratch_shapes=[
            pltpu.VMEM((3, rows, columns), F32),
            pltpu.VMEM((3, rows + 16, columns), BF),
            pltpu.VMEM((2, 3, rows, columns), BF),
            pltpu.SemaphoreType.DMA((12,)),
        ],
        compiler_params=params(8),
        cost_estimate=cost(),
        name="scatter_end",
    )(own, v, *sent, *up, *down)


def scatter_plain(grad):
    both = grad[0].astype(F32) + swap(grad[1], "y", 1).astype(F32)
    return lax.psum_scatter(both, "dp", scatter_dimension=0, tiled=True)


def norm_parts(values):
    center = values - jnp.mean(values, -1, keepdims=True)
    spread = jnp.mean(center * center, -1, keepdims=True)
    scale = lax.rsqrt(spread + EPS)
    return center * scale, scale


def norm_back(xhat, scale, gain, grad):
    scaled = grad * gain
    first = jnp.mean(scaled, -1, keepdims=True)
    second = jnp.mean(scaled * xhat, -1, keepdims=True)
    return scale * (scaled - first - xhat * second)


def rows_spec(columns, lead=None):
    if lead is None:
        return pl.BlockSpec((ROWS, columns), lambda i, c: (i, 0))
    return pl.BlockSpec((lead, ROWS, columns), lambda i, c: (0, i, 0))


def whole_spec(shape):
    return pl.BlockSpec(shape, lambda i, c: (0,) * len(shape))


def half_spec(columns, mine):
    per_core = LENGTH // 2 // ROWS

    def index(i, c):
        inside = i // per_core == (c[0] if mine else 1 - c[0])
        return (jnp.where(inside, i % per_core, 0), 0)

    return pl.BlockSpec((ROWS, columns), index)


def pick_half(first_ref, second_ref):
    second = pl.program_id(0).astype(F32)
    return first_ref[...].astype(F32) * (1.0 - second) + second_ref[...].astype(F32) * second


def pick_rows(core_ref, own_ref, other_ref):
    per_core = LENGTH // 2 // ROWS
    mine = (pl.program_id(0) // per_core == core_ref[0]).astype(F32)
    return own_ref[...].astype(F32) * mine + other_ref[...].astype(F32) * (1.0 - mine)


def block_call(kernel, name, outs, specs, grid, megabytes):
    return pl.pallas_call(
        kernel,
        out_shape=tuple(shape for shape, _ in outs),
        grid_spec=pltpu.PrefetchScalarGridSpec(
            num_scalar_prefetch=1,
            grid=(grid,),
            in_specs=specs,
            out_specs=tuple(spec for _, spec in outs),
        ),
        compiler_params=params(megabytes),
        cost_estimate=cost(),
        name=name,
    )


def prepare_kernel(
    core_ref, own_ref, other_ref, cot_ref, cot_other_ref, gain_ref, shift_ref, n_ref, c_ref, s_ref
):
    cot = pick_rows(core_ref, cot_ref, cot_other_ref)
    c_ref[...] = cot.astype(BF)
    sums = row_sums(cot)

    @pl.when(pl.program_id(0) == 0)
    def _():
        s_ref[...] = sums

    @pl.when(pl.program_id(0) > 0)
    def _():
        s_ref[...] += sums

    xhat, _ = norm_parts(pick_rows(core_ref, own_ref, other_ref))
    n_ref[...] = (xhat * gain_ref[...] + shift_ref[...]).astype(BF)


def prepare(core, own, other, cot, cot_other, gain, shift):
    width = own.shape[1]
    rows = (jax.ShapeDtypeStruct((LENGTH, width), BF), rows_spec(width))
    return block_call(
        prepare_kernel,
        "prepare",
        [rows, rows, (jax.ShapeDtypeStruct((8, width), F32), whole_spec((8, width)))],
        [
            half_spec(width, True),
            half_spec(width, False),
            half_spec(width, True),
            half_spec(width, False),
            whole_spec((1, width)),
            whole_spec((1, width)),
        ],
        LENGTH // ROWS,
        16,
    )(core, own, other, cot, cot_other, gain, shift)


def project_kernel(core_ref, n_ref, w_ref, b_ref, p_ref):
    p_ref[...] = (nn_dot(n_ref[...], w_ref[...]) + b_ref[...]).astype(BF)


def project(core, normed, weight, bias):
    width, columns = weight.shape
    return block_call(
        project_kernel,
        "project",
        [(jax.ShapeDtypeStruct((LENGTH, columns), BF), rows_spec(columns))],
        [rows_spec(width), whole_spec((width, columns)), whole_spec((1, columns))],
        LENGTH // ROWS,
        14,
    )(core, normed, weight, bias)[0]


def middle_kernel(
    core_ref, own_ref, other_ref, part_ref, first_ref, second_ref, ob_ref, gain_ref, shift_ref,
    h_ref, n_ref,
):
    attended = part_ref[...].astype(F32) + pick_half(first_ref, second_ref)
    hidden = pick_rows(core_ref, own_ref, other_ref) + attended + ob_ref[...]
    h_ref[...] = hidden
    xhat, _ = norm_parts(hidden)
    n_ref[...] = (xhat * gain_ref[...] + shift_ref[...]).astype(BF)


def middle(core, own, other, part, part_other, out_bias, gain, shift):
    width = own.shape[1]
    return block_call(
        middle_kernel,
        "middle",
        [
            (jax.ShapeDtypeStruct((LENGTH, width), F32), rows_spec(width)),
            (jax.ShapeDtypeStruct((LENGTH, width), BF), rows_spec(width)),
        ],
        [half_spec(width, True), half_spec(width, False), rows_spec(width)]
        + [whole_spec((ROWS, width))] * 2
        + [whole_spec((1, width))] * 3,
        LENGTH // ROWS,
        16,
    )(core, own, other, part, *part_other, out_bias, gain, shift)


def up_kernel(core_ref, n_ref, w_ref, b_ref, a_ref, d_ref):
    slope = 0.7978845608028654
    for row in range(2):
        up = nn_dot(n_ref[...], w_ref[row]) + b_ref[row]
        square = up * up
        gate = 1.0 / (1.0 + jnp.exp(up * (-2.0 * slope - 2.0 * slope * 0.044715 * square)))
        gated = up * gate
        a_ref[row] = gated.astype(BF)
        inner = 2.0 * slope + 6.0 * slope * 0.044715 * square
        d_ref[row] = (gate + (gated - gated * gate) * inner).astype(BF)


def up_project(core, normed, weight, bias):
    width, columns = weight.shape[1:]
    both = (jax.ShapeDtypeStruct((2, LENGTH, columns), BF), rows_spec(columns, 2))
    return block_call(
        up_kernel,
        "up_project",
        [both, both],
        [rows_spec(width), whole_spec((2, width, columns)), whole_spec((2, 1, columns))],
        LENGTH // ROWS,
        20,
    )(core, normed, weight, bias[:, None])


def up_back_kernel(core_ref, cot_ref, d_ref, down_ref, up_ref, u_ref, b_ref, n_ref):
    total = None
    for row in range(2):
        grad = nn_dot(cot_ref[...], down_ref[row]) * d_ref[row].astype(F32)
        low = grad.astype(BF)
        u_ref[row] = low
        sums = row_sums(low.astype(F32))

        @pl.when(pl.program_id(0) == 0)
        def _():
            b_ref[row] = sums

        @pl.when(pl.program_id(0) > 0)
        def _():
            b_ref[row] += sums

        part = nt_dot(low, up_ref[row])
        total = part if total is None else total + part
    n_ref[...] = total.astype(BF)


def up_back(core, cot, slope, down, up):
    width, columns = down.shape[1:]
    return block_call(
        up_back_kernel,
        "up_back",
        [
            (jax.ShapeDtypeStruct((2, LENGTH, columns), BF), rows_spec(columns, 2)),
            (jax.ShapeDtypeStruct((2, 8, columns), F32), whole_spec((2, 8, columns))),
            (jax.ShapeDtypeStruct((LENGTH, width), BF), rows_spec(width)),
        ],
        [
            rows_spec(width),
            rows_spec(columns, 2),
            whole_spec((2, width, columns)),
            whole_spec((2, width, columns)),
        ],
        LENGTH // ROWS,
        24,
    )(core, cot, slope, down, up)


def second_back_kernel(
    core_ref, h_ref, part_ref, first_ref, second_ref, cot_ref, gain_ref, w_ref,
    dh_ref, do_ref, dc_ref, sum_ref,
):
    xhat, scale = norm_parts(h_ref[...])
    grad = part_ref[...].astype(F32) + pick_half(first_ref, second_ref)
    hidden_grad = cot_ref[...].astype(F32) + norm_back(xhat, scale, gain_ref[...], grad)
    low = hidden_grad.astype(BF)

    @pl.when(pl.program_id(0) == core_ref[0])
    def _():
        dh_ref[...] = hidden_grad

    do_ref[...] = low
    dc_ref[...] = nn_dot(low, w_ref[...]).astype(BF)
    sums = (row_sums(low.astype(F32)), row_sums(grad * xhat), row_sums(grad))
    for position, value in enumerate(sums):

        @pl.when(pl.program_id(0) == 0)
        def _():
            sum_ref[position] = value

        @pl.when(pl.program_id(0) > 0)
        def _():
            sum_ref[position] += value


def second_back(core, hidden, part, other, cot, gain, weight):
    width, columns = weight.shape
    return block_call(
        second_back_kernel,
        "second_back",
        [
            (jax.ShapeDtypeStruct((ROWS, width), F32), whole_spec((ROWS, width))),
            (jax.ShapeDtypeStruct((LENGTH, width), BF), rows_spec(width)),
            (jax.ShapeDtypeStruct((LENGTH, columns), BF), rows_spec(columns)),
            (jax.ShapeDtypeStruct((3, 8, width), F32), whole_spec((3, 8, width))),
        ],
        [rows_spec(width)] * 2
        + [whole_spec((ROWS, width))] * 2
        + [rows_spec(width), whole_spec((1, width)), whole_spec((width, columns))],
        LENGTH // ROWS,
        20,
    )(core, hidden, part, *other, cot, gain, weight)


def share(core, left, weight):
    count, _, depth = left.shape
    width = weight.shape[1]
    half = LENGTH // 2

    def kernel(core_ref, left_ref, weight_ref, own_ref, other_ref):
        total = nt_dot(left_ref[0], weight_ref[0])
        for index in range(1, count):
            total = total + nt_dot(left_ref[index], weight_ref[index])

        @pl.when(pl.program_id(0) == 0)
        def _():
            other_ref[...] = total.astype(BF)

        @pl.when(pl.program_id(0) == 1)
        def _():
            own_ref[...] = total

    def rows(i, c):
        return (0, jnp.where(i == 0, 1 - c[0], c[0]), 0)

    return block_call(
        kernel,
        "share",
        [
            (jax.ShapeDtypeStruct((half, width), F32), whole_spec((half, width))),
            (jax.ShapeDtypeStruct((half, width), BF), whole_spec((half, width))),
        ],
        [pl.BlockSpec((count, half, depth), rows), whole_spec(weight.shape)],
        2,
        16,
    )(core, left, weight)


def first_back_kernel(core_ref, x_ref, part_ref, first, second, dh_ref, gain_ref, t_ref, sum_ref):
    xhat, scale = norm_parts(x_ref[...].astype(F32))
    other = jnp.concatenate([first[...], second[...]], 0)
    grad = part_ref[...] + other.astype(F32)
    t_ref[...] = (dh_ref[...] + norm_back(xhat, scale, gain_ref[...], grad)).astype(BF)
    for position, value in enumerate((row_sums(grad * xhat), row_sums(grad))):

        @pl.when(pl.program_id(0) == 0)
        def _():
            sum_ref[position] = value

        @pl.when(pl.program_id(0) > 0)
        def _():
            sum_ref[position] += value


def first_back(core, own, part, other, hidden_grad, gain):
    width = own.shape[1]
    return block_call(
        first_back_kernel,
        "first_back",
        [
            (jax.ShapeDtypeStruct((LENGTH // 2, width), BF), rows_spec(width)),
            (jax.ShapeDtypeStruct((2, 8, width), F32), whole_spec((2, 8, width))),
        ],
        [rows_spec(width)] * 2
        + [whole_spec((ROWS // 2, width))] * 2
        + [rows_spec(width), whole_spec((1, width))],
        1,
        16,
    )(core, own, part, *other, hidden_grad, gain)


def unpack_kernel(place_ref, v_ref, g1, s1, qkv, ob, g2, s2, up, down, full):
    y, core = place_ref[0], place_ref[1]
    piece = g1.shape[1] // 8
    for d in range(8):
        rows = v_ref[d : d + 1]
        here = slice(d * piece, (d + 1) * piece)
        for ref, position in ((g1, 0), (s1, 1), (ob, 5), (g2, 6), (s2, 7), (down, 12)):
            ref[:, here] = rows[:, position * piece : (position + 1) * piece]
        for kind in range(3):
            full[kind : kind + 1, here] = rows[:, (2 + kind) * piece : (3 + kind) * piece]
        cut = slice(d % 2 * 4 * piece, (d % 2 + 1) * 4 * piece)
        full[3 + d // 2 : 4 + d // 2, cut] = rows[:, 8 * piece : 12 * piece]
    block = 2 * piece
    for kind in range(3):
        for y_index in range(2):
            cuts = []
            for core_index in range(2):
                at = (2 * y_index + core_index) * block
                cuts.append(full[kind : kind + 1, at : at + block])
            value = jnp.where(core == 0, cuts[0], cuts[1])
            for own in range(2):

                @pl.when((y ^ y_index) == own)
                def _():
                    at = (2 * kind + own) * block
                    qkv[:, at : at + block] = value

    for y_index in range(2):
        rows = [full[3 + 2 * y_index + i : 4 + 2 * y_index + i] for i in range(2)]
        value = jnp.where(core == 0, rows[0], rows[1])
        for own in range(2):

            @pl.when((y ^ y_index) == own)
            def _():
                up[own : own + 1] = value


def unpack(place, vectors, width):
    row = jax.ShapeDtypeStruct((1, width), F32)
    wide = jax.ShapeDtypeStruct((1, 3 * width // 2), F32)
    return pl.pallas_call(
        unpack_kernel,
        out_shape=(row, row, wide, row, row, row, jax.ShapeDtypeStruct((2, width), F32), row),
        in_specs=[smem_spec()] + vmem_specs(1),
        out_specs=tuple(vmem_specs(8)),
        scratch_shapes=[pltpu.VMEM((8, width), F32)],
        compiler_params=params(2),
        cost_estimate=cost(),
        name="unpack",
    )(place, vectors)


def pack_kernel(place_ref, first_ref, qkv_ref, second_ref, up_ref, cot_ref, full):
    y, core = place_ref[0], place_ref[1]
    width = full.shape[1]
    block = width // 4

    def column_sum(values):
        return jnp.sum(values, 0, keepdims=True)

    full[0:1] = column_sum(first_ref[0])
    full[1:2] = column_sum(first_ref[1])
    for position, index in ((5, 0), (6, 1), (7, 2)):
        full[position : position + 1] = 0.5 * column_sum(second_ref[index])
    full[12:13] = 0.5 * column_sum(cot_ref[...])
    qkv = qkv_ref[0:1]
    ups = [column_sum(up_ref[index]) for index in range(2)]
    for t in range(4):
        keep = (core == t % 2).astype(F32)
        mine = (y == t // 2).astype(F32)
        for kind in range(3):
            at = kind * 2 * block
            value = qkv[:, at : at + block] * mine + qkv[:, at + block : at + 2 * block] * (1.0 - mine)
            full[2 + kind : 3 + kind, t * block : (t + 1) * block] = value * keep
        full[8 + t : 9 + t] = (ups[0] * mine + ups[1] * (1.0 - mine)) * keep
    full[13:16] = jnp.zeros((3, width), F32)


def pack(place, first, qkv, second, up, cot):
    width = cot.shape[1]
    return pl.pallas_call(
        pack_kernel,
        out_shape=jax.ShapeDtypeStruct((16, width), F32),
        in_specs=[smem_spec()] + vmem_specs(5),
        out_specs=pl.BlockSpec(memory_space=pltpu.VMEM),
        compiler_params=params(4),
        cost_estimate=cost(),
        name="pack",
    )(place, first, qkv, second, up, cot)


def body(
    tokens,
    cotangent,
    first_gain,
    first_shift,
    w_qkv,
    qkv_bias,
    w_out,
    out_bias,
    second_gain,
    second_shift,
    w_up,
    up_bias,
    w_down,
    down_bias,
):
    dp_count = lax.axis_size("dp")
    dp = lax.axis_index("dp")
    y = lax.axis_index("y")
    core = lax.axis_index("core")
    dp_ref = dp.reshape(1).astype(jnp.int32)
    own_rows, width = tokens.shape
    piece = first_gain.shape[0]
    heads_own = w_qkv.shape[2]
    ff_own = w_up.shape[1]
    ff_piece = up_bias.shape[0]

    core_ref = core.reshape(1).astype(jnp.int32)
    place_ref = jnp.stack([y, core]).astype(jnp.int32)
    shard_one = jnp.concatenate([w_qkv[0], w_qkv[1], w_qkv[2], w_out.T], 1)
    fast = direct(shard_one)
    tie = lax.optimization_barrier
    tokens_other = swap(tokens, "core", 1)
    vectors = jnp.concatenate(
        [
            first_gain,
            first_shift,
            qkv_bias.reshape(-1),
            out_bias,
            second_gain,
            second_shift,
            up_bias,
            down_bias,
        ]
    )
    vectors = lax.all_to_all(
        jnp.broadcast_to(vectors[None], (dp_count, vectors.shape[0])), "dp", 0, 0, tiled=True
    )

    def own_half(rows):
        return lax.dynamic_slice_in_dim(rows, core * own_rows, own_rows, 0)

    def exchange(rows):
        half = rows.shape[0] // 2
        return [swap(rows[:half], "core", 1), swap(rows[half:], "core", 1)]

    if fast:
        one = gather_z(shard_one)
        shard_one, one, vectors, tokens_other, cotangent, w_up, w_down = tie(
            (shard_one, one, vectors, tokens_other, cotangent, w_up, w_down)
        )
        one = pair_up(shard_one, *one)
        one_xy1 = gather_xy1(*one)
        one, one_xy1, vectors, cotangent, w_up, w_down = tie(
            (one, one_xy1, vectors, cotangent, w_up, w_down)
        )
        one = gather_xy2(*one, *one_xy1)
        up = gather_z(w_up)
        cot_other = swap(cotangent, "core", 1)
        cot_other, vectors, w_down = tie((cot_other, vectors, w_down))
        shard_down = w_down.T
        gain_one, shift_one, qkv_own, out_full, gain_two, shift_two, up_own, down_full = unpack(
            place_ref, vectors, width
        )
    else:
        one, up, down = map(gather_plain, (shard_one, w_up, w_down.T))
        cot_other = swap(cotangent, "core", 1)

        def full(position, count=1):
            return vectors[:, position * piece : (position + count) * piece]

        def own_blocks(values):
            cut = values.reshape(values.shape[0], 2, 2, -1)
            cut = jnp.where(core == 0, cut[:, :, 0], cut[:, :, 1])
            both = [cut[:, 0], cut[:, 1]]
            first = jnp.where(y == 0, both[0], both[1])
            second = jnp.where(y == 0, both[1], both[0])
            return jnp.stack([first, second], 1)

        gain_one, shift_one, out_full, gain_two, shift_two = (
            full(position).reshape(1, -1) for position in (0, 1, 5, 6, 7)
        )
        qkv_full = full(2, 3).reshape(dp_count, 3, piece).transpose(1, 0, 2).reshape(3, width)
        qkv_own = own_blocks(qkv_full).reshape(1, -1)
        up_own = own_blocks(vectors[:, 8 * piece : 8 * piece + ff_piece].reshape(1, -1))[0]
        down_full = vectors[:, 8 * piece + ff_piece :].reshape(1, -1)
    normed_one, cot, cot_sums = prepare(
        core_ref, tokens, tokens_other, cotangent, cot_other, gain_one, shift_one
    )

    if fast:
        one, up, normed_one, cot, qkv_own, shard_down = tie(
            (one, up, normed_one, cot, qkv_own, shard_down)
        )
        up = pair_up(w_up, *up)
        up_xy1 = gather_xy1(*up)
        down = gather_z(shard_down)
    w_proj, w_ctx = place_one(one, dp_ref)
    projected = project(core_ref, normed_one, w_proj, qkv_own)
    context_first = attend_first(projected)
    if fast:
        context_first, up, up_xy1, down = tie((context_first, up, up_xy1, down))
        up = gather_xy2(*up, *up_xy1)
    context, logs = attend_rest(projected, *context_first)
    if fast:
        down = pair_up(shard_down, *down)
        context, up, down = tie((context, up, down))
        down_xy1 = gather_xy1(*down)
    out_part = nt_dot(context, w_ctx).astype(BF)
    out_other = exchange(out_part)

    hidden, normed_two = middle(
        core_ref, tokens, tokens_other, out_part, out_other, out_full, gain_two, shift_two
    )

    if fast:
        normed_two, down, down_xy1 = tie((normed_two, down, down_xy1))
        down = gather_xy2(*down, *down_xy1)
    weight_up = place_blocks(up, dp_ref)
    active, slope = up_project(core_ref, normed_two, weight_up, up_own)
    down_wgrad = wgrad(cot, active, dp_ref)
    if fast:
        down_wgrad, down, slope = tie((down_wgrad, down, slope))
        down_wgrad = scatter_xy1(down_wgrad)
    weight_down = place_blocks(down, dp_ref)
    upward_grad, up_bias_sums, normed_two_part = up_back(
        core_ref, cot, slope, weight_down, weight_up
    )
    up_wgrad = wgrad(normed_two, upward_grad, dp_ref)
    if fast:
        up_wgrad, down_wgrad, normed_two_part = tie((up_wgrad, down_wgrad, normed_two_part))
        up_wgrad = scatter_xy1(up_wgrad)
        down_sent = scatter_xy2(down_wgrad)
    normed_two_other = exchange(normed_two_part)

    hidden_grad, branch_grad, ctx_grad, second_sums = second_back(
        core_ref, hidden, normed_two_part, normed_two_other, cot, gain_two, w_ctx
    )
    parts = [attend_back_part(projected, ctx_grad, context, logs, pair) for pair in range(2)]
    mlp_part, mlp_sent = share(core_ref, active, weight_down)
    if fast:
        parts, up_wgrad, down_sent, ctx_grad, mlp_sent = tie(
            (parts, up_wgrad, down_sent, ctx_grad, mlp_sent)
        )
        up_sent = scatter_xy2(up_wgrad)
        down_wgrad = scatter_z(down_sent, down_wgrad)
    proj_grad, qkv_bias_own = attend_back_last(projected, ctx_grad, context, logs, parts)
    normed_one_part, sent = share(core_ref, proj_grad[None], w_proj[None])
    if fast:
        proj_grad, sent = tie((proj_grad, sent))
    one_wgrad = wgrad_one(normed_one, proj_grad, branch_grad, context, dp_ref)
    if fast:
        one_wgrad, up_sent, down_wgrad, sent = tie((one_wgrad, up_sent, down_wgrad, sent))
        one_wgrad = scatter_xy1(one_wgrad)
        up_wgrad = scatter_z(up_sent, up_wgrad)
    normed_one_other = exchange(sent)
    tokens_grad, first_sums = first_back(
        core_ref, tokens, normed_one_part, normed_one_other, hidden_grad, gain_one
    )

    if fast:
        sums = pack(place_ref, first_sums, qkv_bias_own, second_sums, up_bias_sums, cot_sums)
        sums = sums + swap(sums, "core", 1)
    else:

        def spread_blocks(values):
            block = values.shape[-1] // 2
            own, other = values[..., :block], values[..., block:]
            cut = [jnp.where(y == 0, own, other), jnp.where(y == 0, other, own)]
            return jnp.concatenate(
                [jnp.where(core == index, half, 0.0) for half in cut for index in range(2)], -1
            )

        sums = [
            jnp.sum(first_sums, 1),
            spread_blocks(qkv_bias_own[0].reshape(3, 2 * heads_own)),
            0.5 * jnp.sum(second_sums, 1),
            spread_blocks(jnp.sum(up_bias_sums, 1).reshape(1, -1)),
            0.5 * jnp.sum(cot_sums, 0)[None],
        ]
        sums = [
            item.reshape(item.shape[0], dp_count, -1).transpose(1, 0, 2).reshape(dp_count, -1)
            for item in sums
        ]
        sums = jnp.concatenate(sums, 1)
        sums = jnp.broadcast_to(sums[:, None, :], (dp_count, 4, sums.shape[1]))
        sums = sums.reshape(dp_count * 4, -1)
    if fast:
        one_wgrad, sums, up_wgrad, mlp_sent = tie((one_wgrad, sums, up_wgrad, mlp_sent))
        one_sent = scatter_xy2(one_wgrad)
        sums = sums + (swap(sums, "dp", 1) + swap(sums, "y", 1) + swap_both(sums))
    mlp_other = swap(mlp_sent, "core", 1)
    if fast:
        one_sent, sums, mlp_other = tie((one_sent, sums, mlp_other))
        one_wgrad = scatter_last(one_sent, one_wgrad, sums, dp_ref)
    block_out = (own_half(hidden) + mlp_part + mlp_other.astype(F32) + down_full).astype(BF)
    if fast:
        one_wgrad, block_out = tie((one_wgrad, block_out))
        shapes = (w_qkv.shape, w_out.shape, one_wgrad[1].shape, w_up.shape, w_down.shape)
        qkv_wgrad, out_wgrad, sums, up_wgrad, down_wgrad = scatter_end(
            one_wgrad, up_wgrad, down_wgrad, shapes
        )
        small = (sums[0], sums[1], sums[2:5], sums[5], sums[6], sums[7], sums[8:12], sums[12])
    else:
        one_wgrad, up_wgrad, down_wgrad = map(scatter_plain, (one_wgrad, up_wgrad, down_wgrad))
        down_wgrad = down_wgrad.T
        qkv_wgrad = one_wgrad[:, : 3 * heads_own].reshape(piece, 3, heads_own).transpose(1, 0, 2)
        out_wgrad = one_wgrad[:, 3 * heads_own :].T
        sums = lax.all_to_all(sums, ("dp", "y", "core"), 0, 0, tiled=True)
        sums = jnp.sum(sums, 0).reshape(-1, piece)
        small = (sums[0], sums[1], sums[2:5], sums[5], sums[6], sums[7], sums[8:12], sums[12])
    vector_grads = small[:6] + (small[6].reshape(-1), small[7])

    return (
        block_out,
        tokens_grad,
        vector_grads[0],
        vector_grads[1],
        qkv_wgrad,
        vector_grads[2],
        out_wgrad,
        vector_grads[3],
        vector_grads[4],
        vector_grads[5],
        up_wgrad,
        vector_grads[6],
        down_wgrad,
        vector_grads[7],
    )


def solution(mesh):
    devices = mesh.devices
    split = Mesh(devices.reshape(devices.shape[0], 2, 2), ("dp", "y", "core"))
    tensor = ("y", "core")
    rows = P(("dp", "y", "core"), None)
    specs = (
        P("dp"),
        P("dp"),
        P(None, "dp", tensor),
        P(None, "dp"),
        P(tensor, "dp"),
        P("dp"),
        P("dp"),
        P("dp"),
        P("dp", tensor),
        P("dp"),
        P(tensor, "dp"),
        P("dp"),
    )
    return jax.shard_map(
        body,
        mesh=split,
        in_specs=(rows, rows) + specs,
        out_specs=(rows, rows) + specs,
        check_vma=False,
    )
```

```python
import functools

import jax
import jax.numpy as jnp
from jax import lax
from jax.experimental import pallas as pl
from jax.experimental.pallas import tpu as pltpu
from jax.sharding import Mesh
from jax.sharding import PartitionSpec as P

HEAD_DIM = 64
LENGTH = 1024
EPS = 1e-05
BLOCK = 256
ROWS = 512
BF = jnp.bfloat16
F32 = jnp.float32
MEGABYTE = 1024 * 1024


def swap(value, axis, bit):
    size = lax.axis_size(axis)
    return lax.ppermute(value, axis, [(i, i ^ bit) for i in range(size)])


def swap_both(value):
    size = lax.axis_size("dp") * 2
    return lax.ppermute(value, ("dp", "y"), [(i, i ^ 3) for i in range(size)])


def nt_dot(left, right):
    return lax.dot_general(left, right, (((1,), (1,)), ((), ())), preferred_element_type=F32)


def tn_dot(left, right):
    return lax.dot_general(left, right, (((0,), (0,)), ((), ())), preferred_element_type=F32)


def nn_dot(left, right):
    return jnp.dot(left, right, preferred_element_type=F32)


def attend_pair(p_ref, pair, width):
    q = p_ref[:, pl.ds(pair, 128)] * BF(HEAD_DIM**-0.5)
    k = p_ref[:, pl.ds(width + pair, 128)]
    v = p_ref[:, pl.ds(2 * width + pair, 128)]
    lane = lax.broadcasted_iota(jnp.int32, (LENGTH, 128), 1)
    low_lane = lax.broadcasted_iota(jnp.int32, (BLOCK, 128), 1) < HEAD_DIM
    causal = lax.broadcasted_iota(jnp.int32, (BLOCK, BLOCK), 0) >= lax.broadcasted_iota(
        jnp.int32, (BLOCK, BLOCK), 1
    )
    for start in range(0, LENGTH, BLOCK):
        stop = start + BLOCK
        halves = []
        logs = []
        for head in range(2):
            mine = (lane < HEAD_DIM) if head == 0 else (lane >= HEAD_DIM)
            q_part = jnp.where(mine[start:stop], q[start:stop], BF(0))
            v_part = jnp.where(mine[:stop], v[:stop], BF(1))
            scores = nt_dot(q_part, k[:stop])
            last = jnp.where(causal, scores[:, start:], -1e30)
            scores = jnp.concatenate([scores[:, :start], last], 1) if start else last
            top = jnp.max(scores, 1, keepdims=True)
            weights = jnp.exp(scores - top).astype(BF)
            result = nn_dot(weights, v_part)
            total = pltpu.roll(result, HEAD_DIM, 1)
            halves.append(result / total)
            logs.append(top + jnp.log(total))
        yield (
            start,
            jnp.where(low_lane, halves[0], halves[1]).astype(BF),
            jnp.where(low_lane, logs[0], logs[1]),
        )


def attend_first_kernel(p_ref, c_ref, l_ref):
    for start, context, logs in attend_pair(p_ref, 0, p_ref.shape[1] // 3):
        c_ref[start : start + BLOCK] = context
        l_ref[start : start + BLOCK] = logs


def attend_rest_kernel(p_ref, first_ref, first_log_ref, c_ref, l_ref):
    width = c_ref.shape[1]
    pair = pl.multiple_of((pl.program_id(0) + 1) * 128, 128)
    for start, context, logs in attend_pair(p_ref, pair, width):
        c_ref[start : start + BLOCK, pl.ds(pair, 128)] = context
        l_ref[start : start + BLOCK, pl.ds(pair, 128)] = logs

    @pl.when(pl.program_id(0) == 0)
    def _():
        c_ref[:, :128] = first_ref[...]
        l_ref[:, :128] = first_log_ref[...]


def attend_first(projected):
    return pl.pallas_call(
        attend_first_kernel,
        out_shape=(
            jax.ShapeDtypeStruct((LENGTH, 128), BF),
            jax.ShapeDtypeStruct((LENGTH, 128), F32),
        ),
        in_specs=[pl.BlockSpec(memory_space=pltpu.VMEM)],
        out_specs=(pl.BlockSpec(memory_space=pltpu.VMEM),) * 2,
        compiler_params=params(12),
        cost_estimate=cost(),
        name="attend_first",
    )(projected)


def attend_rest(projected, first, first_log):
    width = projected.shape[1] // 3
    pairs = width // 128 - 1
    return pl.pallas_call(
        attend_rest_kernel,
        out_shape=(
            jax.ShapeDtypeStruct((LENGTH, width), BF),
            jax.ShapeDtypeStruct((LENGTH, width), F32),
        ),
        grid=(pairs,),
        in_specs=[
            pl.BlockSpec((LENGTH, 3 * width), lambda i: (0, 0)),
            pl.BlockSpec((LENGTH, 128), lambda i: (0, 0)),
            pl.BlockSpec((LENGTH, 128), lambda i: (0, 0)),
        ],
        out_specs=(pl.BlockSpec((LENGTH, width), lambda i: (0, 0)),) * 2,
        compiler_params=params(16),
        cost_estimate=cost(),
        name="attend_rest",
    )(projected, first, first_log)


def attend_back_pair(p_ref, g_ref, c_ref, l_ref, pair, dk_ref, dv_ref, dq_ref):
    width = g_ref.shape[1]
    q = p_ref[:, pair : pair + 128] * BF(HEAD_DIM**-0.5)
    k = p_ref[:, width + pair : width + pair + 128]
    v = p_ref[:, 2 * width + pair : 2 * width + pair + 128]
    g = g_ref[:, pair : pair + 128]
    low_lane = lax.broadcasted_iota(jnp.int32, (BLOCK, 128), 1) < HEAD_DIM
    causal = lax.broadcasted_iota(jnp.int32, (BLOCK, BLOCK), 0) <= lax.broadcasted_iota(
        jnp.int32, (BLOCK, BLOCK), 1
    )
    dk_ref[...] = jnp.zeros_like(dk_ref)
    dv_ref[...] = jnp.zeros_like(dv_ref)
    for start in range(0, LENGTH, BLOCK):
        stop = start + BLOCK
        logs = l_ref[start:stop, pair : pair + 128].T
        context = c_ref[start:stop, pair : pair + 128].astype(F32)
        product = (g[start:stop].astype(F32) * context).T
        query_grads = []
        for head in range(2):
            mine = low_lane if head == 0 else jnp.logical_not(low_lane)
            row = head * HEAD_DIM
            q_part = jnp.where(mine, q[start:stop], BF(0))
            g_part = jnp.where(mine, g[start:stop], BF(0))
            delta = jnp.sum(product[row : row + HEAD_DIM], 0, keepdims=True)
            scores = nt_dot(k[:stop], q_part)
            last = jnp.where(causal, scores[start:], -1e30)
            scores = jnp.concatenate([scores[:start], last], 0) if start else last
            probs = jnp.exp(scores - logs[row : row + 1])
            prob_grad = nt_dot(v[:stop], g_part)
            score_grad = (probs * (prob_grad - delta)).astype(BF)
            dv_ref[:stop] += nn_dot(probs.astype(BF), g_part)
            dk_ref[:stop] += nn_dot(score_grad, q_part)
            query_grads.append(tn_dot(score_grad, k[:stop]))
        dq_ref[start:stop] = jnp.where(low_lane, query_grads[0], query_grads[1]) * HEAD_DIM**-0.5
    return [ref[...].astype(BF) for ref in (dq_ref, dk_ref, dv_ref)]


def column_sums(values):
    return nn_dot(jnp.ones((8, values.shape[0]), BF), values)


def attend_back_part_kernel(pair, p_ref, g_ref, c_ref, l_ref, d_ref, dk_ref, dv_ref, dq_ref):
    results = attend_back_pair(p_ref, g_ref, c_ref, l_ref, pair * 128, dk_ref, dv_ref, dq_ref)
    for position, result in enumerate(results):
        d_ref[:, position * 128 : (position + 1) * 128] = result


def attend_back_last_kernel(p_ref, g_ref, c_ref, l_ref, *refs):
    parts, (d_ref, bias_ref, dk_ref, dv_ref, dq_ref) = refs[:-5], refs[-5:]
    width = g_ref.shape[1]
    results = attend_back_pair(
        p_ref, g_ref, c_ref, l_ref, len(parts) * 128, dk_ref, dv_ref, dq_ref
    )
    pieces = [[ref[:, i * 128 : (i + 1) * 128] for i in range(3)] for ref in parts]
    for pair, piece in enumerate(pieces + [results]):
        for position, result in enumerate(piece):
            columns = slice(position * width + pair * 128, position * width + pair * 128 + 128)
            d_ref[:, columns] = result
            bias_ref[:, columns] = column_sums(result)


def attend_back_part(projected, ctx_grad, context, logs, pair):
    return pl.pallas_call(
        functools.partial(attend_back_part_kernel, pair),
        out_shape=jax.ShapeDtypeStruct((LENGTH, 384), BF),
        in_specs=[pl.BlockSpec(memory_space=pltpu.VMEM)] * 4,
        out_specs=pl.BlockSpec(memory_space=pltpu.VMEM),
        scratch_shapes=[pltpu.VMEM((LENGTH, 128), F32)] * 3,
        compiler_params=params(14),
        cost_estimate=cost(),
        name="attend_back_part",
    )(projected, ctx_grad, context, logs)


def attend_back_last(projected, ctx_grad, context, logs, parts):
    width = projected.shape[1]
    return pl.pallas_call(
        attend_back_last_kernel,
        out_shape=(
            jax.ShapeDtypeStruct((LENGTH, width), BF),
            jax.ShapeDtypeStruct((8, width), F32),
        ),
        in_specs=[pl.BlockSpec(memory_space=pltpu.VMEM)] * (4 + len(parts)),
        out_specs=(pl.BlockSpec(memory_space=pltpu.VMEM),) * 2,
        scratch_shapes=[pltpu.VMEM((LENGTH, 128), F32)] * 3,
        compiler_params=params(18),
        cost_estimate=cost(),
        name="attend_back_last",
    )(projected, ctx_grad, context, logs, *parts)


def row_sums(values):
    return jnp.sum(values.reshape(values.shape[0] // 8, 8, values.shape[1]), 0)


def vmem_specs(count):
    return [pl.BlockSpec(memory_space=pltpu.VMEM)] * count


def hbm_specs(count):
    return [pl.BlockSpec(memory_space=pltpu.HBM)] * count


def fetch(pairs, sems):
    copies = [
        pltpu.make_async_copy(source, target, sems.at[i]) for i, (source, target) in enumerate(pairs)
    ]
    for copy in copies:
        copy.start()
    for copy in copies:
        copy.wait()


def smem_spec():
    return pl.BlockSpec(memory_space=pltpu.SMEM)


def params(megabytes):
    return pltpu.CompilerParams(vmem_limit_bytes=megabytes * MEGABYTE)


def cost():
    return pl.CostEstimate(flops=0, bytes_accessed=0, transcendentals=0)


def place_kernel(dp_ref, h1_ref, h2_ref, h1y_ref, h2x_ref, w_ref):
    dp = dp_ref[0]
    for low in range(2):
        for x in range(2):
            w_ref[0, dp ^ (low * 2 + x)] = h1_ref[x * 2 + low]
            w_ref[1, dp ^ (low * 2 + x)] = h1y_ref[x * 2 + low]
        for row in range(2):
            w_ref[row, dp ^ (4 + low * 2)] = h2_ref[row * 2 + low]
            w_ref[row, dp ^ (4 + low * 2 + 1)] = h2x_ref[row * 2 + low]


def place_blocks(pieces, dp):
    if len(pieces) == 2:
        return jnp.stack(pieces)
    rows, columns = pieces[0].shape[1:]
    placed = pl.pallas_call(
        place_kernel,
        out_shape=jax.ShapeDtypeStruct((2, 8, rows, columns), BF),
        in_specs=[smem_spec()] + vmem_specs(4),
        out_specs=pl.BlockSpec(memory_space=pltpu.VMEM),
        compiler_params=params(10),
        cost_estimate=cost(),
        name="place",
    )(dp, *pieces)
    return placed.reshape(2, 8 * rows, columns)


def place_one_kernel(dp_ref, a_ref, b_ref, ay_ref, bx_ref, proj_ref, ctx_ref, *scratch):
    dp = dp_ref[0]
    *staged, sems = scratch
    fetch(list(zip((a_ref, b_ref, ay_ref, bx_ref), staged)), sems)
    h1_ref, h2_ref, h1y_ref, h2x_ref = staged
    block = h1_ref.shape[2] // 4

    def put(index, own, other):
        for kind in range(4):
            columns = slice(kind * block, (kind + 1) * block)
            both = jnp.concatenate([own[:, columns], other[:, columns]], 1)
            if kind < 3:
                proj_ref[dp ^ index, :, kind * 2 * block : (kind + 1) * 2 * block] = both
            else:
                ctx_ref[dp ^ index] = both

    for low in range(2):
        for x in range(2):
            put(low * 2 + x, h1_ref[x * 2 + low], h1y_ref[x * 2 + low])
        put(4 + low * 2, h2_ref[low], h2_ref[2 + low])
        put(4 + low * 2 + 1, h2x_ref[low], h2x_ref[2 + low])


def place_one(pieces, dp):
    if len(pieces) == 2:
        width = pieces[0].shape[0]
        cut = jnp.stack([piece.reshape(width, 4, -1) for piece in pieces], 2)
        return cut[:, :3].reshape(width, -1), cut[:, 3].reshape(width, -1)
    rows, columns = pieces[0].shape[1:]
    proj, ctx = pl.pallas_call(
        place_one_kernel,
        out_shape=(
            jax.ShapeDtypeStruct((8, rows, columns * 3 // 2), BF),
            jax.ShapeDtypeStruct((8, rows, columns // 2), BF),
        ),
        in_specs=[smem_spec()] + hbm_specs(4),
        out_specs=tuple(vmem_specs(2)),
        scratch_shapes=[pltpu.VMEM(pieces[0].shape, BF)] * 4 + [pltpu.SemaphoreType.DMA((4,))],
        compiler_params=params(8),
        cost_estimate=cost(),
        name="place_one",
    )(dp, *pieces)
    return proj.reshape(8 * rows, -1), ctx.reshape(8 * rows, -1)


def direct(shard):
    return lax.axis_size("dp") == 8 and shard.shape[0] % 16 == 0


def gather_z(shard):
    return swap(shard, "dp", 2), swap(shard, "dp", 4), swap(shard, "dp", 6)


def pair_up(shard, r1, r2, r3):
    return jnp.stack([shard, r1]), jnp.stack([r2, r3])


def gather_xy1(h1, h2):
    return swap(h1, "dp", 1), swap(h2, "y", 1)


def gather_xy2(h1, h2, h1x, h2y):
    h1 = jnp.concatenate([h1, h1x])
    h2 = jnp.concatenate([h2, h2y])
    return h1, h2, swap(h1, "y", 1), swap(h2, "dp", 1)


def gather_plain(shard):
    own = lax.all_gather(shard, "dp", axis=0, tiled=True)
    return own, swap(own, "y", 1)


def spread_put(dp, outs, result, row, columns=slice(None)):
    k1, s1, k2, s2, stage = outs
    rows = k1.shape[1]
    for index in range(8):
        stage[index] = result[index * rows : (index + 1) * rows].astype(BF)
    first = s1 if row else k1
    for low in range(2):
        for x in range(2):
            first[x * 2 + low, :, columns] = stage[dp ^ (low * 2 + x)]
        k2[row * 2 + low, :, columns] = stage[dp ^ (4 + low * 2)]
        s2[row * 2 + low, :, columns] = stage[dp ^ (4 + low * 2 + 1)]


def wgrad_kernel(dp_ref, left_ref, right_ref, k1, s1, k2, s2, stage):
    for row in range(2):

        @pl.when(pl.program_id(0) == row)
        def _():
            result = tn_dot(left_ref[...], right_ref[0])
            spread_put(dp_ref[0], (k1, s1, k2, s2, stage), result, row)


def wgrad(left, right, dp):
    width = left.shape[1]
    columns = right.shape[2]
    count = lax.axis_size("dp")
    if count != 8 or (width // count) % 16:
        return jnp.einsum("rd,yre->yde", left, right, preferred_element_type=F32).astype(BF)
    part = jax.ShapeDtypeStruct((4, width // 8, columns), BF)
    return pl.pallas_call(
        wgrad_kernel,
        out_shape=(part,) * 4,
        grid=(2,),
        in_specs=[
            smem_spec(),
            pl.BlockSpec((LENGTH, width), lambda i: (0, 0)),
            pl.BlockSpec((1, LENGTH, columns), lambda i: (i, 0, 0)),
        ],
        out_specs=(pl.BlockSpec(part.shape, lambda i: (0, 0, 0)),) * 4,
        scratch_shapes=[pltpu.VMEM((8, width // 8, columns), BF)],
        compiler_params=params(16),
        cost_estimate=cost(),
        name="wgrad",
    )(dp, left, right)


def wgrad_one_kernel(dp_ref, n_ref, d_ref, g_ref, c_ref, k1, s1, k2, s2, stage):
    block = c_ref.shape[1] // 2
    for kind in range(4):

        @pl.when(pl.program_id(0) == kind)
        def _():
            left, right = (n_ref, d_ref) if kind < 3 else (g_ref, c_ref)
            result = tn_dot(left[...], right[...])
            for row in range(2):
                spread_put(
                    dp_ref[0],
                    (k1, s1, k2, s2, stage),
                    result[:, row * block : (row + 1) * block],
                    row,
                    slice(kind * block, (kind + 1) * block),
                )


def wgrad_one(normed, proj_grad, branch_grad, context, dp):
    width = normed.shape[1]
    block = context.shape[1] // 2
    count = lax.axis_size("dp")
    if count != 8 or (width // count) % 16:
        proj = tn_dot(normed, proj_grad).reshape(width, 3, 2, block)
        out = tn_dot(branch_grad, context).reshape(width, 1, 2, block)
        both = jnp.concatenate([proj, out], 1).transpose(2, 0, 1, 3)
        return both.reshape(2, width, 4 * block).astype(BF)
    part = jax.ShapeDtypeStruct((4, width // 8, 4 * block), BF)
    return pl.pallas_call(
        wgrad_one_kernel,
        out_shape=(part,) * 4,
        grid=(4,),
        in_specs=[
            smem_spec(),
            pl.BlockSpec((LENGTH, width), lambda i: (0, 0)),
            pl.BlockSpec((LENGTH, 2 * block), lambda i: (0, jnp.minimum(i, 2))),
            pl.BlockSpec((LENGTH, width), lambda i: (0, 0)),
            pl.BlockSpec((LENGTH, 2 * block), lambda i: (0, 0)),
        ],
        out_specs=(pl.BlockSpec(part.shape, lambda i: (0, 0, 0)),) * 4,
        scratch_shapes=[pltpu.VMEM((8, width // 8, block), BF)],
        compiler_params=params(18),
        cost_estimate=cost(),
        name="wgrad_one",
    )(dp, normed, proj_grad, branch_grad, context)


def add_kernel(k1, t1, k2, t2, first, second, stage, sems):
    fetch([(ref.at[pl.ds(2, 2)], stage.at[i]) for i, ref in enumerate((k1, t1, k2, t2))], sems)
    first[...] = (stage[0].astype(F32) + stage[1].astype(F32)).astype(BF)
    second[...] = (stage[2].astype(F32) + stage[3].astype(F32)).astype(BF)


def sum_kernel(u1, u2, k1, t1, k2, t2, v, z1, z2, z3, stage, sems):
    parts = (u1, k1, t1, u2, k2, t2)
    fetch([(ref.at[pl.ds(0, 2)], stage.at[i]) for i, ref in enumerate(parts)], sems)

    def total(at, index):
        return sum(stage[at + i, index].astype(F32) for i in range(3))

    v[...] = total(0, 0)
    z1[...] = total(0, 1).astype(BF)
    z2[...] = total(3, 0).astype(BF)
    z3[...] = total(3, 1).astype(BF)


def scatter_xy1(parts):
    k1, s1, k2, s2 = parts
    return k1, swap(s1, "y", 1), k2, swap(s2, "dp", 1)


def scatter_xy2(item):
    _, rows, columns = item[0].shape
    half = jax.ShapeDtypeStruct((2, rows, columns), BF)
    first, second = pl.pallas_call(
        add_kernel,
        out_shape=(half, half),
        in_specs=hbm_specs(4),
        out_specs=tuple(vmem_specs(2)),
        scratch_shapes=[pltpu.VMEM((4, 2, rows, columns), BF), pltpu.SemaphoreType.DMA((4,))],
        compiler_params=params(4),
        cost_estimate=cost(),
        name="add_pairs",
    )(*item)
    return swap(first, "dp", 1), swap(second, "y", 1)


def scatter_z(sent, item):
    _, rows, columns = sent[0].shape
    low = jax.ShapeDtypeStruct((rows, columns), BF)
    v, z1, z2, z3 = pl.pallas_call(
        sum_kernel,
        out_shape=(jax.ShapeDtypeStruct((rows, columns), F32), low, low, low),
        in_specs=hbm_specs(6),
        out_specs=tuple(vmem_specs(4)),
        scratch_shapes=[pltpu.VMEM((6, 2, rows, columns), BF), pltpu.SemaphoreType.DMA((6,))],
        compiler_params=params(4),
        cost_estimate=cost(),
        name="sum_pairs",
    )(*sent, *item)
    return v, swap(z1, "dp", 2), swap(z2, "dp", 4), swap(z3, "dp", 6)


def last_sum_kernel(
    dp_ref, s_ref, u1, u2, k1, t1, k2, t2, v, own, z1, z2, z3, stage, blocks, sems
):
    dp = dp_ref[0]
    rows, columns = v.shape
    sum_kernel(u1, u2, k1, t1, k2, t2, v, *(ref.at[pl.ds(0, rows)] for ref in (z1, z2, z3)), stage, sems)
    piece = s_ref.shape[1] // 8
    for d in range(8):
        here = slice(d * piece, (d + 1) * piece)
        blocks[d, 0:8] = s_ref[0:8, here]
        blocks[d, 12:16] = s_ref[12:16, here]
        for j in range(4):
            at = d % 2 * 4 * piece + j * piece
            blocks[d, 8 + j : 9 + j] = s_ref[8 + d // 2 : 9 + d // 2, at : at + piece]
    own[...] = blocks[dp]
    for ref, bit in ((z1, 2), (z2, 4), (z3, 6)):
        value = blocks[dp ^ bit]
        high = value.astype(BF)
        ref[rows:, :] = jnp.zeros((16, columns), BF)
        ref[rows:, 0:piece] = high
        ref[rows:, 128 : 128 + piece] = (value - high.astype(F32)).astype(BF)


def scatter_last(sent, item, sums, dp):
    _, rows, columns = sent[0].shape
    low = jax.ShapeDtypeStruct((rows + 16, columns), BF)
    piece = sums.shape[1] // 8
    v, own, z1, z2, z3 = pl.pallas_call(
        last_sum_kernel,
        out_shape=(
            jax.ShapeDtypeStruct((rows, columns), F32),
            jax.ShapeDtypeStruct((16, piece), F32),
            low,
            low,
            low,
        ),
        in_specs=[smem_spec()] + vmem_specs(1) + hbm_specs(6),
        out_specs=tuple(vmem_specs(5)),
        scratch_shapes=[
            pltpu.VMEM((6, 2, rows, columns), BF),
            pltpu.VMEM((8, 16, piece), F32),
            pltpu.SemaphoreType.DMA((6,)),
        ],
        compiler_params=params(5),
        cost_estimate=cost(),
        name="sum_last",
    )(dp, sums, *sent, *item)
    return v, own, swap(z1, "dp", 2), swap(z2, "dp", 4), swap(z3, "dp", 6)


def end_kernel(own, *refs):
    ins, (qkv, out, small, up, down), (first, last, rest, sems) = refs[:12], refs[12:17], refs[17:]
    pairs = []
    for i in range(3):
        v, *sent = ins[4 * i : 4 * i + 4]
        pairs.append((v, first.at[i]))
        for j, ref in enumerate(sent):
            pairs.append((ref, last.at[j] if i == 0 else rest.at[i - 1, j]))
    fetch(pairs, sems)
    rows = first.shape[1]
    total = first[0] + sum(last[j, :rows].astype(F32) for j in range(3))
    block, piece = qkv.shape[2], own.shape[1]
    for kind in range(3):
        qkv[kind] = total[:, kind * block : (kind + 1) * block]
    out[...] = total[:, 3 * block :].T
    sums = own[...]
    for j in range(3):
        sums = sums + last[j, rows:, 0:piece].astype(F32)
        sums = sums + last[j, rows:, 128 : 128 + piece].astype(F32)
    small[...] = sums
    up[...] = first[1] + sum(rest[0, j].astype(F32) for j in range(3))
    down[...] = (first[2] + sum(rest[1, j].astype(F32) for j in range(3))).T


def scatter_end(one, up, down, shapes):
    v, own, *sent = one
    rows, columns = v.shape
    return pl.pallas_call(
        end_kernel,
        out_shape=tuple(jax.ShapeDtypeStruct(shape, F32) for shape in shapes),
        in_specs=vmem_specs(1) + hbm_specs(12),
        out_specs=tuple(vmem_specs(5)),
        scratch_shapes=[
            pltpu.VMEM((3, rows, columns), F32),
            pltpu.VMEM((3, rows + 16, columns), BF),
            pltpu.VMEM((2, 3, rows, columns), BF),
            pltpu.SemaphoreType.DMA((12,)),
        ],
        compiler_params=params(8),
        cost_estimate=cost(),
        name="scatter_end",
    )(own, v, *sent, *up, *down)


def scatter_plain(grad):
    both = grad[0].astype(F32) + swap(grad[1], "y", 1).astype(F32)
    return lax.psum_scatter(both, "dp", scatter_dimension=0, tiled=True)


def norm_parts(values):
    center = values - jnp.mean(values, -1, keepdims=True)
    spread = jnp.mean(center * center, -1, keepdims=True)
    scale = lax.rsqrt(spread + EPS)
    return center * scale, scale


def norm_back(xhat, scale, gain, grad):
    scaled = grad * gain
    first = jnp.mean(scaled, -1, keepdims=True)
    second = jnp.mean(scaled * xhat, -1, keepdims=True)
    return scale * (scaled - first - xhat * second)


def rows_spec(columns, lead=None):
    if lead is None:
        return pl.BlockSpec((ROWS, columns), lambda i, c: (i, 0))
    return pl.BlockSpec((lead, ROWS, columns), lambda i, c: (0, i, 0))


def whole_spec(shape):
    return pl.BlockSpec(shape, lambda i, c: (0,) * len(shape))


def half_spec(columns, mine):
    per_core = LENGTH // 2 // ROWS

    def index(i, c):
        inside = i // per_core == (c[0] if mine else 1 - c[0])
        return (jnp.where(inside, i % per_core, 0), 0)

    return pl.BlockSpec((ROWS, columns), index)


def pick_half(first_ref, second_ref):
    second = pl.program_id(0).astype(F32)
    return first_ref[...].astype(F32) * (1.0 - second) + second_ref[...].astype(F32) * second


def pick_rows(core_ref, own_ref, other_ref):
    per_core = LENGTH // 2 // ROWS
    mine = (pl.program_id(0) // per_core == core_ref[0]).astype(F32)
    return own_ref[...].astype(F32) * mine + other_ref[...].astype(F32) * (1.0 - mine)


def block_call(kernel, name, outs, specs, grid, megabytes):
    return pl.pallas_call(
        kernel,
        out_shape=tuple(shape for shape, _ in outs),
        grid_spec=pltpu.PrefetchScalarGridSpec(
            num_scalar_prefetch=1,
            grid=(grid,),
            in_specs=specs,
            out_specs=tuple(spec for _, spec in outs),
        ),
        compiler_params=params(megabytes),
        cost_estimate=cost(),
        name=name,
    )


def prepare_kernel(
    core_ref, own_ref, other_ref, cot_ref, cot_other_ref, gain_ref, shift_ref, n_ref, c_ref, s_ref
):
    cot = pick_rows(core_ref, cot_ref, cot_other_ref)
    c_ref[...] = cot.astype(BF)
    sums = row_sums(cot)

    @pl.when(pl.program_id(0) == 0)
    def _():
        s_ref[...] = sums

    @pl.when(pl.program_id(0) > 0)
    def _():
        s_ref[...] += sums

    xhat, _ = norm_parts(pick_rows(core_ref, own_ref, other_ref))
    n_ref[...] = (xhat * gain_ref[...] + shift_ref[...]).astype(BF)


def prepare(core, own, other, cot, cot_other, gain, shift):
    width = own.shape[1]
    rows = (jax.ShapeDtypeStruct((LENGTH, width), BF), rows_spec(width))
    return block_call(
        prepare_kernel,
        "prepare",
        [rows, rows, (jax.ShapeDtypeStruct((8, width), F32), whole_spec((8, width)))],
        [
            half_spec(width, True),
            half_spec(width, False),
            half_spec(width, True),
            half_spec(width, False),
            whole_spec((1, width)),
            whole_spec((1, width)),
        ],
        LENGTH // ROWS,
        16,
    )(core, own, other, cot, cot_other, gain, shift)


def project_kernel(core_ref, n_ref, w_ref, b_ref, p_ref):
    p_ref[...] = (nn_dot(n_ref[...], w_ref[...]) + b_ref[...]).astype(BF)


def project(core, normed, weight, bias):
    width, columns = weight.shape
    return block_call(
        project_kernel,
        "project",
        [(jax.ShapeDtypeStruct((LENGTH, columns), BF), rows_spec(columns))],
        [rows_spec(width), whole_spec((width, columns)), whole_spec((1, columns))],
        LENGTH // ROWS,
        14,
    )(core, normed, weight, bias)[0]


def middle_kernel(
    core_ref, own_ref, other_ref, part_ref, first_ref, second_ref, ob_ref, gain_ref, shift_ref,
    h_ref, n_ref,
):
    attended = part_ref[...].astype(F32) + pick_half(first_ref, second_ref)
    hidden = pick_rows(core_ref, own_ref, other_ref) + attended + ob_ref[...]
    h_ref[...] = hidden
    xhat, _ = norm_parts(hidden)
    n_ref[...] = (xhat * gain_ref[...] + shift_ref[...]).astype(BF)


def middle(core, own, other, part, part_other, out_bias, gain, shift):
    width = own.shape[1]
    return block_call(
        middle_kernel,
        "middle",
        [
            (jax.ShapeDtypeStruct((LENGTH, width), F32), rows_spec(width)),
            (jax.ShapeDtypeStruct((LENGTH, width), BF), rows_spec(width)),
        ],
        [half_spec(width, True), half_spec(width, False), rows_spec(width)]
        + [whole_spec((ROWS, width))] * 2
        + [whole_spec((1, width))] * 3,
        LENGTH // ROWS,
        16,
    )(core, own, other, part, *part_other, out_bias, gain, shift)


def up_kernel(core_ref, n_ref, w_ref, b_ref, a_ref, d_ref):
    slope = 0.7978845608028654
    for row in range(2):
        up = nn_dot(n_ref[...], w_ref[row]) + b_ref[row]
        square = up * up
        gate = 1.0 / (1.0 + jnp.exp(up * (-2.0 * slope - 2.0 * slope * 0.044715 * square)))
        gated = up * gate
        a_ref[row] = gated.astype(BF)
        inner = 2.0 * slope + 6.0 * slope * 0.044715 * square
        d_ref[row] = (gate + (gated - gated * gate) * inner).astype(BF)


def up_project(core, normed, weight, bias):
    width, columns = weight.shape[1:]
    both = (jax.ShapeDtypeStruct((2, LENGTH, columns), BF), rows_spec(columns, 2))
    return block_call(
        up_kernel,
        "up_project",
        [both, both],
        [rows_spec(width), whole_spec((2, width, columns)), whole_spec((2, 1, columns))],
        LENGTH // ROWS,
        20,
    )(core, normed, weight, bias[:, None])


def up_back_kernel(core_ref, cot_ref, d_ref, down_ref, up_ref, u_ref, b_ref, n_ref):
    total = None
    for row in range(2):
        grad = nn_dot(cot_ref[...], down_ref[row]) * d_ref[row].astype(F32)
        low = grad.astype(BF)
        u_ref[row] = low
        sums = row_sums(low.astype(F32))

        @pl.when(pl.program_id(0) == 0)
        def _():
            b_ref[row] = sums

        @pl.when(pl.program_id(0) > 0)
        def _():
            b_ref[row] += sums

        part = nt_dot(low, up_ref[row])
        total = part if total is None else total + part
    n_ref[...] = total.astype(BF)


def up_back(core, cot, slope, down, up):
    width, columns = down.shape[1:]
    return block_call(
        up_back_kernel,
        "up_back",
        [
            (jax.ShapeDtypeStruct((2, LENGTH, columns), BF), rows_spec(columns, 2)),
            (jax.ShapeDtypeStruct((2, 8, columns), F32), whole_spec((2, 8, columns))),
            (jax.ShapeDtypeStruct((LENGTH, width), BF), rows_spec(width)),
        ],
        [
            rows_spec(width),
            rows_spec(columns, 2),
            whole_spec((2, width, columns)),
            whole_spec((2, width, columns)),
        ],
        LENGTH // ROWS,
        24,
    )(core, cot, slope, down, up)


def second_back_kernel(
    core_ref, h_ref, part_ref, first_ref, second_ref, cot_ref, gain_ref, w_ref,
    dh_ref, do_ref, dc_ref, sum_ref,
):
    xhat, scale = norm_parts(h_ref[...])
    grad = part_ref[...].astype(F32) + pick_half(first_ref, second_ref)
    hidden_grad = cot_ref[...].astype(F32) + norm_back(xhat, scale, gain_ref[...], grad)
    low = hidden_grad.astype(BF)

    @pl.when(pl.program_id(0) == core_ref[0])
    def _():
        dh_ref[...] = hidden_grad

    do_ref[...] = low
    dc_ref[...] = nn_dot(low, w_ref[...]).astype(BF)
    sums = (row_sums(low.astype(F32)), row_sums(grad * xhat), row_sums(grad))
    for position, value in enumerate(sums):

        @pl.when(pl.program_id(0) == 0)
        def _():
            sum_ref[position] = value

        @pl.when(pl.program_id(0) > 0)
        def _():
            sum_ref[position] += value


def second_back(core, hidden, part, other, cot, gain, weight):
    width, columns = weight.shape
    return block_call(
        second_back_kernel,
        "second_back",
        [
            (jax.ShapeDtypeStruct((ROWS, width), F32), whole_spec((ROWS, width))),
            (jax.ShapeDtypeStruct((LENGTH, width), BF), rows_spec(width)),
            (jax.ShapeDtypeStruct((LENGTH, columns), BF), rows_spec(columns)),
            (jax.ShapeDtypeStruct((3, 8, width), F32), whole_spec((3, 8, width))),
        ],
        [rows_spec(width)] * 2
        + [whole_spec((ROWS, width))] * 2
        + [rows_spec(width), whole_spec((1, width)), whole_spec((width, columns))],
        LENGTH // ROWS,
        20,
    )(core, hidden, part, *other, cot, gain, weight)


def share(core, left, weight):
    count, _, depth = left.shape
    width = weight.shape[1]
    half = LENGTH // 2

    def kernel(core_ref, left_ref, weight_ref, own_ref, other_ref):
        total = nt_dot(left_ref[0], weight_ref[0])
        for index in range(1, count):
            total = total + nt_dot(left_ref[index], weight_ref[index])

        @pl.when(pl.program_id(0) == 0)
        def _():
            other_ref[...] = total.astype(BF)

        @pl.when(pl.program_id(0) == 1)
        def _():
            own_ref[...] = total

    def rows(i, c):
        return (0, jnp.where(i == 0, 1 - c[0], c[0]), 0)

    return block_call(
        kernel,
        "share",
        [
            (jax.ShapeDtypeStruct((half, width), F32), whole_spec((half, width))),
            (jax.ShapeDtypeStruct((half, width), BF), whole_spec((half, width))),
        ],
        [pl.BlockSpec((count, half, depth), rows), whole_spec(weight.shape)],
        2,
        16,
    )(core, left, weight)


def first_back_kernel(core_ref, x_ref, part_ref, first, second, dh_ref, gain_ref, t_ref, sum_ref):
    xhat, scale = norm_parts(x_ref[...].astype(F32))
    other = jnp.concatenate([first[...], second[...]], 0)
    grad = part_ref[...] + other.astype(F32)
    t_ref[...] = (dh_ref[...] + norm_back(xhat, scale, gain_ref[...], grad)).astype(BF)
    for position, value in enumerate((row_sums(grad * xhat), row_sums(grad))):

        @pl.when(pl.program_id(0) == 0)
        def _():
            sum_ref[position] = value

        @pl.when(pl.program_id(0) > 0)
        def _():
            sum_ref[position] += value


def first_back(core, own, part, other, hidden_grad, gain):
    width = own.shape[1]
    return block_call(
        first_back_kernel,
        "first_back",
        [
            (jax.ShapeDtypeStruct((LENGTH // 2, width), BF), rows_spec(width)),
            (jax.ShapeDtypeStruct((2, 8, width), F32), whole_spec((2, 8, width))),
        ],
        [rows_spec(width)] * 2
        + [whole_spec((ROWS // 2, width))] * 2
        + [rows_spec(width), whole_spec((1, width))],
        1,
        16,
    )(core, own, part, *other, hidden_grad, gain)


def unpack_kernel(place_ref, v_ref, g1, s1, qkv, ob, g2, s2, up, down, full):
    y, core = place_ref[0], place_ref[1]
    piece = g1.shape[1] // 8
    for d in range(8):
        rows = v_ref[d : d + 1]
        here = slice(d * piece, (d + 1) * piece)
        for ref, position in ((g1, 0), (s1, 1), (ob, 5), (g2, 6), (s2, 7), (down, 12)):
            ref[:, here] = rows[:, position * piece : (position + 1) * piece]
        for kind in range(3):
            full[kind : kind + 1, here] = rows[:, (2 + kind) * piece : (3 + kind) * piece]
        cut = slice(d % 2 * 4 * piece, (d % 2 + 1) * 4 * piece)
        full[3 + d // 2 : 4 + d // 2, cut] = rows[:, 8 * piece : 12 * piece]
    block = 2 * piece
    for kind in range(3):
        for y_index in range(2):
            cuts = []
            for core_index in range(2):
                at = (2 * y_index + core_index) * block
                cuts.append(full[kind : kind + 1, at : at + block])
            value = jnp.where(core == 0, cuts[0], cuts[1])
            for own in range(2):

                @pl.when((y ^ y_index) == own)
                def _():
                    at = (2 * kind + own) * block
                    qkv[:, at : at + block] = value

    for y_index in range(2):
        rows = [full[3 + 2 * y_index + i : 4 + 2 * y_index + i] for i in range(2)]
        value = jnp.where(core == 0, rows[0], rows[1])
        for own in range(2):

            @pl.when((y ^ y_index) == own)
            def _():
                up[own : own + 1] = value


def unpack(place, vectors, width):
    row = jax.ShapeDtypeStruct((1, width), F32)
    wide = jax.ShapeDtypeStruct((1, 3 * width // 2), F32)
    return pl.pallas_call(
        unpack_kernel,
        out_shape=(row, row, wide, row, row, row, jax.ShapeDtypeStruct((2, width), F32), row),
        in_specs=[smem_spec()] + vmem_specs(1),
        out_specs=tuple(vmem_specs(8)),
        scratch_shapes=[pltpu.VMEM((8, width), F32)],
        compiler_params=params(2),
        cost_estimate=cost(),
        name="unpack",
    )(place, vectors)


def pack_kernel(place_ref, first_ref, qkv_ref, second_ref, up_ref, cot_ref, full):
    y, core = place_ref[0], place_ref[1]
    width = full.shape[1]
    block = width // 4

    def column_sum(values):
        return jnp.sum(values, 0, keepdims=True)

    full[0:1] = column_sum(first_ref[0])
    full[1:2] = column_sum(first_ref[1])
    for position, index in ((5, 0), (6, 1), (7, 2)):
        full[position : position + 1] = 0.5 * column_sum(second_ref[index])
    full[12:13] = 0.5 * column_sum(cot_ref[...])
    qkv = qkv_ref[0:1]
    ups = [column_sum(up_ref[index]) for index in range(2)]
    for t in range(4):
        keep = (core == t % 2).astype(F32)
        mine = (y == t // 2).astype(F32)
        for kind in range(3):
            at = kind * 2 * block
            value = qkv[:, at : at + block] * mine + qkv[:, at + block : at + 2 * block] * (1.0 - mine)
            full[2 + kind : 3 + kind, t * block : (t + 1) * block] = value * keep
        full[8 + t : 9 + t] = (ups[0] * mine + ups[1] * (1.0 - mine)) * keep
    full[13:16] = jnp.zeros((3, width), F32)


def pack(place, first, qkv, second, up, cot):
    width = cot.shape[1]
    return pl.pallas_call(
        pack_kernel,
        out_shape=jax.ShapeDtypeStruct((16, width), F32),
        in_specs=[smem_spec()] + vmem_specs(5),
        out_specs=pl.BlockSpec(memory_space=pltpu.VMEM),
        compiler_params=params(4),
        cost_estimate=cost(),
        name="pack",
    )(place, first, qkv, second, up, cot)


def body(
    tokens,
    cotangent,
    first_gain,
    first_shift,
    w_qkv,
    qkv_bias,
    w_out,
    out_bias,
    second_gain,
    second_shift,
    w_up,
    up_bias,
    w_down,
    down_bias,
):
    dp_count = lax.axis_size("dp")
    dp = lax.axis_index("dp")
    y = lax.axis_index("y")
    core = lax.axis_index("core")
    dp_ref = dp.reshape(1).astype(jnp.int32)
    own_rows, width = tokens.shape
    piece = first_gain.shape[0]
    heads_own = w_qkv.shape[2]
    ff_own = w_up.shape[1]
    ff_piece = up_bias.shape[0]

    core_ref = core.reshape(1).astype(jnp.int32)
    place_ref = jnp.stack([y, core]).astype(jnp.int32)
    shard_one = jnp.concatenate([w_qkv[0], w_qkv[1], w_qkv[2], w_out.T], 1)
    fast = direct(shard_one)
    tie = lax.optimization_barrier
    tokens_other = swap(tokens, "core", 1)
    vectors = jnp.concatenate(
        [
            first_gain,
            first_shift,
            qkv_bias.reshape(-1),
            out_bias,
            second_gain,
            second_shift,
            up_bias,
            down_bias,
        ]
    )
    vectors = lax.all_to_all(
        jnp.broadcast_to(vectors[None], (dp_count, vectors.shape[0])), "dp", 0, 0, tiled=True
    )

    def own_half(rows):
        return lax.dynamic_slice_in_dim(rows, core * own_rows, own_rows, 0)

    def exchange(rows):
        half = rows.shape[0] // 2
        return [swap(rows[:half], "core", 1), swap(rows[half:], "core", 1)]

    if fast:
        one = gather_z(shard_one)
        shard_one, one, vectors, tokens_other, cotangent, w_up, w_down = tie(
            (shard_one, one, vectors, tokens_other, cotangent, w_up, w_down)
        )
        one = pair_up(shard_one, *one)
        one_xy1 = gather_xy1(*one)
        one, one_xy1, vectors, cotangent, w_up, w_down = tie(
            (one, one_xy1, vectors, cotangent, w_up, w_down)
        )
        one = gather_xy2(*one, *one_xy1)
        up = gather_z(w_up)
        cot_other = swap(cotangent, "core", 1)
        cot_other, vectors, w_down = tie((cot_other, vectors, w_down))
        shard_down = w_down.T
        gain_one, shift_one, qkv_own, out_full, gain_two, shift_two, up_own, down_full = unpack(
            place_ref, vectors, width
        )
    else:
        one, up, down = map(gather_plain, (shard_one, w_up, w_down.T))
        cot_other = swap(cotangent, "core", 1)

        def full(position, count=1):
            return vectors[:, position * piece : (position + count) * piece]

        def own_blocks(values):
            cut = values.reshape(values.shape[0], 2, 2, -1)
            cut = jnp.where(core == 0, cut[:, :, 0], cut[:, :, 1])
            both = [cut[:, 0], cut[:, 1]]
            first = jnp.where(y == 0, both[0], both[1])
            second = jnp.where(y == 0, both[1], both[0])
            return jnp.stack([first, second], 1)

        gain_one, shift_one, out_full, gain_two, shift_two = (
            full(position).reshape(1, -1) for position in (0, 1, 5, 6, 7)
        )
        qkv_full = full(2, 3).reshape(dp_count, 3, piece).transpose(1, 0, 2).reshape(3, width)
        qkv_own = own_blocks(qkv_full).reshape(1, -1)
        up_own = own_blocks(vectors[:, 8 * piece : 8 * piece + ff_piece].reshape(1, -1))[0]
        down_full = vectors[:, 8 * piece + ff_piece :].reshape(1, -1)
    normed_one, cot, cot_sums = prepare(
        core_ref, tokens, tokens_other, cotangent, cot_other, gain_one, shift_one
    )

    if fast:
        one, up, normed_one, cot, qkv_own, shard_down = tie(
            (one, up, normed_one, cot, qkv_own, shard_down)
        )
        up = pair_up(w_up, *up)
        up_xy1 = gather_xy1(*up)
        down = gather_z(shard_down)
    w_proj, w_ctx = place_one(one, dp_ref)
    projected = project(core_ref, normed_one, w_proj, qkv_own)
    context_first = attend_first(projected)
    if fast:
        context_first, up, up_xy1, down = tie((context_first, up, up_xy1, down))
        up = gather_xy2(*up, *up_xy1)
    context, logs = attend_rest(projected, *context_first)
    if fast:
        down = pair_up(shard_down, *down)
        context, up, down = tie((context, up, down))
        down_xy1 = gather_xy1(*down)
    out_part = nt_dot(context, w_ctx).astype(BF)
    out_other = exchange(out_part)

    hidden, normed_two = middle(
        core_ref, tokens, tokens_other, out_part, out_other, out_full, gain_two, shift_two
    )

    if fast:
        normed_two, down, down_xy1 = tie((normed_two, down, down_xy1))
        down = gather_xy2(*down, *down_xy1)
    weight_up = place_blocks(up, dp_ref)
    active, slope = up_project(core_ref, normed_two, weight_up, up_own)
    down_wgrad = wgrad(cot, active, dp_ref)
    if fast:
        down_wgrad, down, slope = tie((down_wgrad, down, slope))
        down_wgrad = scatter_xy1(down_wgrad)
    weight_down = place_blocks(down, dp_ref)
    upward_grad, up_bias_sums, normed_two_part = up_back(
        core_ref, cot, slope, weight_down, weight_up
    )
    up_wgrad = wgrad(normed_two, upward_grad, dp_ref)
    if fast:
        up_wgrad, down_wgrad, normed_two_part = tie((up_wgrad, down_wgrad, normed_two_part))
        up_wgrad = scatter_xy1(up_wgrad)
        down_sent = scatter_xy2(down_wgrad)
    normed_two_other = exchange(normed_two_part)

    hidden_grad, branch_grad, ctx_grad, second_sums = second_back(
        core_ref, hidden, normed_two_part, normed_two_other, cot, gain_two, w_ctx
    )
    parts = [attend_back_part(projected, ctx_grad, context, logs, pair) for pair in range(2)]
    mlp_part, mlp_sent = share(core_ref, active, weight_down)
    if fast:
        parts, up_wgrad, down_sent, ctx_grad, mlp_sent = tie(
            (parts, up_wgrad, down_sent, ctx_grad, mlp_sent)
        )
        up_sent = scatter_xy2(up_wgrad)
        down_wgrad = scatter_z(down_sent, down_wgrad)
    proj_grad, qkv_bias_own = attend_back_last(projected, ctx_grad, context, logs, parts)
    normed_one_part, sent = share(core_ref, proj_grad[None], w_proj[None])
    if fast:
        proj_grad, sent = tie((proj_grad, sent))
    one_wgrad = wgrad_one(normed_one, proj_grad, branch_grad, context, dp_ref)
    if fast:
        one_wgrad, up_sent, down_wgrad, sent = tie((one_wgrad, up_sent, down_wgrad, sent))
        one_wgrad = scatter_xy1(one_wgrad)
        up_wgrad = scatter_z(up_sent, up_wgrad)
    normed_one_other = exchange(sent)
    tokens_grad, first_sums = first_back(
        core_ref, tokens, normed_one_part, normed_one_other, hidden_grad, gain_one
    )

    if fast:
        sums = pack(place_ref, first_sums, qkv_bias_own, second_sums, up_bias_sums, cot_sums)
        sums = sums + swap(sums, "core", 1)
        sums = sums + (swap(sums, "dp", 1) + swap(sums, "y", 1) + swap_both(sums))
    else:

        def spread_blocks(values):
            block = values.shape[-1] // 2
            own, other = values[..., :block], values[..., block:]
            cut = [jnp.where(y == 0, own, other), jnp.where(y == 0, other, own)]
            return jnp.concatenate(
                [jnp.where(core == index, half, 0.0) for half in cut for index in range(2)], -1
            )

        sums = [
            jnp.sum(first_sums, 1),
            spread_blocks(qkv_bias_own[0].reshape(3, 2 * heads_own)),
            0.5 * jnp.sum(second_sums, 1),
            spread_blocks(jnp.sum(up_bias_sums, 1).reshape(1, -1)),
            0.5 * jnp.sum(cot_sums, 0)[None],
        ]
        sums = [
            item.reshape(item.shape[0], dp_count, -1).transpose(1, 0, 2).reshape(dp_count, -1)
            for item in sums
        ]
        sums = jnp.concatenate(sums, 1)
        sums = jnp.broadcast_to(sums[:, None, :], (dp_count, 4, sums.shape[1]))
        sums = sums.reshape(dp_count * 4, -1)
    if fast:
        one_wgrad, sums, up_wgrad, mlp_sent = tie((one_wgrad, sums, up_wgrad, mlp_sent))
        one_sent = scatter_xy2(one_wgrad)
    mlp_other = swap(mlp_sent, "core", 1)
    if fast:
        one_sent, sums, mlp_other = tie((one_sent, sums, mlp_other))
        one_wgrad = scatter_last(one_sent, one_wgrad, sums, dp_ref)
    block_out = (own_half(hidden) + mlp_part + mlp_other.astype(F32) + down_full).astype(BF)
    if fast:
        one_wgrad, block_out = tie((one_wgrad, block_out))
        shapes = (w_qkv.shape, w_out.shape, one_wgrad[1].shape, w_up.shape, w_down.shape)
        qkv_wgrad, out_wgrad, sums, up_wgrad, down_wgrad = scatter_end(
            one_wgrad, up_wgrad, down_wgrad, shapes
        )
        small = (sums[0], sums[1], sums[2:5], sums[5], sums[6], sums[7], sums[8:12], sums[12])
    else:
        one_wgrad, up_wgrad, down_wgrad = map(scatter_plain, (one_wgrad, up_wgrad, down_wgrad))
        down_wgrad = down_wgrad.T
        qkv_wgrad = one_wgrad[:, : 3 * heads_own].reshape(piece, 3, heads_own).transpose(1, 0, 2)
        out_wgrad = one_wgrad[:, 3 * heads_own :].T
        sums = lax.all_to_all(sums, ("dp", "y", "core"), 0, 0, tiled=True)
        sums = jnp.sum(sums, 0).reshape(-1, piece)
        small = (sums[0], sums[1], sums[2:5], sums[5], sums[6], sums[7], sums[8:12], sums[12])
    vector_grads = small[:6] + (small[6].reshape(-1), small[7])

    return (
        block_out,
        tokens_grad,
        vector_grads[0],
        vector_grads[1],
        qkv_wgrad,
        vector_grads[2],
        out_wgrad,
        vector_grads[3],
        vector_grads[4],
        vector_grads[5],
        up_wgrad,
        vector_grads[6],
        down_wgrad,
        vector_grads[7],
    )


def solution(mesh):
    devices = mesh.devices
    split = Mesh(devices.reshape(devices.shape[0], 2, 2), ("dp", "y", "core"))
    tensor = ("y", "core")
    rows = P(("dp", "y", "core"), None)
    specs = (
        P("dp"),
        P("dp"),
        P(None, "dp", tensor),
        P(None, "dp"),
        P(tensor, "dp"),
        P("dp"),
        P("dp"),
        P("dp"),
        P("dp", tensor),
        P("dp"),
        P(tensor, "dp"),
        P("dp"),
    )
    return jax.shard_map(
        body,
        mesh=split,
        in_specs=(rows, rows) + specs,
        out_specs=(rows, rows) + specs,
        check_vma=False,
    )
```
